32 devices in a mesh: section: 2 (over x), batch: 16 (over z, y, core).
Axes of the slice: x: 2, y: 2, z: 4, core: 2. Of those that a mesh axis runs over, the one named last changes fastest.
Arguments:
- tokens: bfloat16 [2, 32768, 512], P('section', 'batch'), may hold values from -6 to 6
- cotangent: bfloat16 [2, 32768, 512], P('section', 'batch'), may hold values from -6 to 6
- lengths: int32 [32, 4], P('batch'), may hold values from 0 to 1024, as said below
- qkv_weight: float32 [2, 3, 512, 512], P('section', None, 'batch'), may hold values from -0.25 to 0.25
- qkv_momentum: float32 [2, 3, 512, 512], P('section', None, 'batch'), may hold values from -512 to 512
- qkv_average: float32 [2, 3, 512, 512], P('section', None, 'batch'), may hold values from -0.25 to 0.25
- out_weight: float32 [2, 512, 512], P('section', 'batch'), may hold values from -3 to 3
- out_momentum: float32 [2, 512, 512], P('section', 'batch'), may hold values from -56 to 56
- out_average: float32 [2, 512, 512], P('section', 'batch'), may hold values from -3 to 3
- up_weight: float32 [2, 512, 2048], P('section', 'batch'), may hold values from -0.25 to 0.25
- up_momentum: float32 [2, 512, 2048], P('section', 'batch'), may hold values from -320 to 320
- up_average: float32 [2, 512, 2048], P('section', 'batch'), may hold values from -0.25 to 0.25
- down_weight: float32 [2, 2048, 512], P('section', 'batch'), may hold values from -0.125 to 0.125
- down_momentum: float32 [2, 2048, 512], P('section', 'batch'), may hold values from -640 to 640
- down_average: float32 [2, 2048, 512], P('section', 'batch'), may hold values from -0.125 to 0.125
- norm_params: float32 [2, 4, 512], P('section', None, 'batch')
- norm_momentum: float32 [2, 4, 512], P('section', None, 'batch'), may hold values from -512 to 512
- norm_average: float32 [2, 4, 512], P('section', None, 'batch')
Outputs:
- activations: bfloat16 [2, 32768, 512], P('section', 'batch')
- input_grad: float32 [2, 32768, 512], P('section', 'batch')
- qkv_grad: float32 [2, 3, 512, 512], P('section', None, 'batch')
- qkv_new_momentum: float32 [2, 3, 512, 512], P('section', None, 'batch')
- qkv_new_weight: float32 [2, 3, 512, 512], P('section', None, 'batch')
- qkv_new_average: float32 [2, 3, 512, 512], P('section', None, 'batch')
- out_grad: float32 [2, 512, 512], P('section', 'batch')
- out_new_momentum: float32 [2, 512, 512], P('section', 'batch')
- out_new_weight: float32 [2, 512, 512], P('section', 'batch')
- out_new_average: float32 [2, 512, 512], P('section', 'batch')
- up_grad: float32 [2, 512, 2048], P('section', 'batch')
- up_new_momentum: float32 [2, 512, 2048], P('section', 'batch')
- up_new_weight: float32 [2, 512, 2048], P('section', 'batch')
- up_new_average: float32 [2, 512, 2048], P('section', 'batch')
- down_grad: float32 [2, 2048, 512], P('section', 'batch')
- down_new_momentum: float32 [2, 2048, 512], P('section', 'batch')
- down_new_weight: float32 [2, 2048, 512], P('section', 'batch')
- down_new_average: float32 [2, 2048, 512], P('section', 'batch')
- norm_grad: float32 [2, 4, 512], P('section', None, 'batch')
- norm_new_momentum: float32 [2, 4, 512], P('section', None, 'batch')
- norm_new_weight: float32 [2, 4, 512], P('section', None, 'batch')
- norm_new_average: float32 [2, 4, 512], P('section', None, 'batch')
- ffn_shift_grad: float32 [2, 512], P('section', 'batch')
The draws below stay inside these ranges and needn't reach their ends.
Inputs may be any that keep to these rules, and one draw needn't show every extreme that they name: Each row sums to 1024; a row is either one item of 1024 positions followed by zeros, or 4 items of positive lengths; both kinds occur in every draw.
All inputs are finite; a program needn't handle non-finite values.
Results may differ from the reference program's by a relative error of at most 0.012.
Values may be sent and summed in bfloat16 or wider, within the bound.
No kernel may reach another device: no remote copies, remote signals or barrier semaphores. Data moves between devices by JAX's collectives and lax.ppermute only.
A program may use at most 256 MiB of HBM per device.

```python
import jax
import jax.numpy as jnp
from jax import lax

D = 512
HEADS = 8
HEAD_DIM = 64
FF = 2048
SEQ = 1024
SLOTS = 4
STEP = 5
TOKENS = 32768
ROWS = 32


def draw_lengths(key, part):
    phase = jax.random.randint(jax.random.fold_in(key, 3), (), 0, 2)
    row_ids = jnp.arange(ROWS, dtype=jnp.int32)
    whole = (row_ids + phase) % 2 == 0
    offsets = jax.random.randint(jax.random.fold_in(key, 4), (ROWS, SLOTS - 1), -(SEQ // 16), SEQ // 16 + 1)
    leading = SEQ // SLOTS + offsets
    closing = SEQ - jnp.sum(leading, axis=1, keepdims=True)
    ragged = jnp.concatenate([leading, closing], axis=1)
    single = jnp.concatenate([jnp.full((ROWS, 1), SEQ, jnp.int32), jnp.zeros((ROWS, SLOTS - 1), jnp.int32)], axis=1)
    return jnp.where(whole[:, None], single, ragged).astype(jnp.int32)


def norm_table(key):
    row_kind = (jnp.arange(4) % 2 == 0)[None, :, None]
    gain_part = 1.0 + 0.4 * jax.random.uniform(jax.random.fold_in(key, 1), (2, 4, D), minval=-1.0, maxval=1.0)
    shift_part = 0.3 * jax.random.normal(jax.random.fold_in(key, 2), (2, 4, D))
    return jnp.where(row_kind, gain_part, shift_part).astype(jnp.float32)


def draw_norm_params(key, part):
    return norm_table(jax.random.fold_in(key, 21))


def draw_norm_average(key, part):
    return norm_table(jax.random.fold_in(key, 22))


def shard_levels(own_key, dims, cuts, low, high):
    level = 1.0
    for dim, blocks in cuts:
        heights = jax.random.uniform(jax.random.fold_in(jax.random.fold_in(own_key, 6), dim), (blocks,), jnp.float32, low / len(cuts), high / len(cuts))
        level = level * jnp.repeat(jnp.exp(heights), dims[dim] // blocks).reshape((-1,) + (1,) * (len(dims) - 1 - dim))
    return level


def normal_values(stream_key, dims, scale, limit, cuts=(), held_as=jnp.bfloat16):
    array = jax.random.normal(stream_key, dims, jnp.float32) * scale
    if len(cuts) > 0:
        array = shard_levels(stream_key, dims, cuts, -0.22, 0.18) * array
    return jnp.clip(array, min=-limit, max=limit).astype(held_as)


def setup_inputs(seed: int = 0) -> dict:
    streams_of = jax.random.split(jax.random.key(seed), 19)
    return {
        "tokens": normal_values(streams_of[0], (2, TOKENS, D), 1.0, 6.0, ((0, 2), (1, 16))),
        "cotangent": normal_values(streams_of[1], (2, TOKENS, D), 1.0, 6.0, ((0, 2), (1, 16))),
        "lengths": draw_lengths(jax.random.fold_in(streams_of[18], 71), 0),
        "qkv_weight": normal_values(streams_of[3], (2, 3, D, D), D ** -0.5, 0.25, ((0, 2), (2, 16)), jnp.float32),
        "qkv_momentum": normal_values(streams_of[4], (2, 3, D, D), (0.5 * TOKENS ** 0.5), 512.0, ((0, 2), (2, 16)), jnp.float32),
        "qkv_average": normal_values(streams_of[5], (2, 3, D, D), D ** -0.5, 0.25, ((0, 2), (2, 16)), jnp.float32),
        "out_weight": normal_values(streams_of[6], (2, D, D), 4 ** -0.5, 3.0, ((0, 2), (1, 16)), jnp.float32),
        "out_momentum": normal_values(streams_of[7], (2, D, D), (0.05 * TOKENS ** 0.5), 56.0, ((0, 2), (1, 16)), jnp.float32),
        "out_average": normal_values(streams_of[8], (2, D, D), 4 ** -0.5, 3.0, ((0, 2), (1, 16)), jnp.float32),
        "up_weight": normal_values(streams_of[9], (2, D, FF), D ** -0.5, 0.25, ((0, 2), (1, 16)), jnp.float32),
        "up_momentum": normal_values(streams_of[10], (2, D, FF), (0.3 * TOKENS ** 0.5), 320.0, ((0, 2), (1, 16)), jnp.float32),
        "up_average": normal_values(streams_of[11], (2, D, FF), D ** -0.5, 0.25, ((0, 2), (1, 16)), jnp.float32),
        "down_weight": normal_values(streams_of[12], (2, FF, D), FF ** -0.5, 0.125, ((0, 2), (1, 16)), jnp.float32),
        "down_momentum": normal_values(streams_of[13], (2, FF, D), (0.6 * TOKENS ** 0.5), 640.0, ((0, 2), (1, 16)), jnp.float32),
        "down_average": normal_values(streams_of[14], (2, FF, D), FF ** -0.5, 0.125, ((0, 2), (1, 16)), jnp.float32),
        "norm_params": draw_norm_params(jax.random.fold_in(streams_of[18], 71), 0),
        "norm_momentum": normal_values(streams_of[16], (2, 4, D), (0.5 * TOKENS ** 0.5), 512.0, ((0, 2), (2, 16)), jnp.float32),
        "norm_average": draw_norm_average(jax.random.fold_in(streams_of[18], 71), 0),
    }


@jax.custom_vjp
def low(v):
    return lax.optimization_barrier(v.astype(jnp.bfloat16)).astype(jnp.float32)

@jax.custom_vjp
def low_back(v):
    return v

def low_keep(v):
    return (low(v), None)

def low_pass(kept, grad):
    return (grad,)

def back_keep(v):
    return (v, None)

def back_low(kept, grad):
    return (low(grad),)
low.defvjp(low_keep, low_pass)
low_back.defvjp(back_keep, back_low)
eps = 1e-05
momentum_decay = 0.9
rate_qkv = 0.0001
rate_out = 0.01
rate_up = 0.0002
rate_down = 4e-05
rate_norm = 0.0004
neg_large = -1e+30
highest = lax.Precision.HIGHEST

def layer_norm(values, norm_gain, norm_shift):
    centre = values - lax.optimization_barrier(jnp.mean(values, axis=-1, keepdims=True))
    spread = lax.optimization_barrier(jnp.mean(centre * centre, axis=-1, keepdims=True))
    return centre * lax.rsqrt(spread + eps) * norm_gain + norm_shift

def segment_ids(lengths):
    bounds = jnp.cumsum(lengths, axis=1)[:, :-1].astype(jnp.int32)
    places = jnp.arange(SEQ, dtype=jnp.int32)
    return lax.optimization_barrier(jnp.sum((places[None, :, None] >= bounds[:, None, :]).astype(jnp.int32), axis=2))

def attend_one(packed):
    query_heads, key_heads, value_heads, segment = packed
    factor = HEAD_DIM ** (-0.5)
    scores = jnp.einsum('qhd,khd->hqk', query_heads, key_heads, precision=highest) * factor
    scores = low_back(scores)
    inside = (segment[:, None] == segment[None, :])[None]
    scores = jnp.where(inside, scores, neg_large)
    maxima = lax.optimization_barrier(jnp.max(scores, axis=-1, keepdims=True))
    raised = jnp.exp(scores - maxima)
    probability = low(raised / lax.optimization_barrier(jnp.sum(raised, axis=-1, keepdims=True)))
    return jnp.einsum('hqk,khd->qhd', probability, value_heads, precision=highest)

def layer(inputs, qkv_full, out_full, up_full, down_full, norm_full, segments):
    normed = low(layer_norm(inputs, norm_full[0], norm_full[1]))
    projected = jnp.einsum('td,jde->jte', normed, qkv_full, precision=highest)
    projected = low(low_back(projected))
    heads = projected.reshape(3, ROWS, SEQ, HEADS, HEAD_DIM)
    mixed = lax.map(jax.checkpoint(attend_one), (heads[0], heads[1], heads[2], segments))
    mixed = low(low_back(mixed.reshape(TOKENS, D)))
    attn_branch = low_back(jnp.dot(mixed, out_full, precision=highest))
    middle = inputs + attn_branch
    second = low(layer_norm(middle, norm_full[2], norm_full[3]))
    hidden_pre = low_back(jnp.dot(second, up_full, precision=highest))
    hidden = low(jax.nn.gelu(hidden_pre))
    return middle + low_back(jnp.dot(hidden, down_full, precision=highest))

def update(gradient, weight, momentum, average, step_rate):
    new_momentum = momentum_decay * momentum + gradient
    new_weight = weight - step_rate * (gradient + momentum_decay * new_momentum)
    new_average = average + (new_weight - average) / (STEP + 1.0)
    return (gradient, new_momentum, new_weight, new_average)

def reference(tokens, cotangent, lengths, qkv_weight, qkv_momentum, qkv_average, out_weight, out_momentum, out_average, up_weight, up_momentum, up_average, down_weight, down_momentum, down_average, norm_params, norm_momentum, norm_average):
    segments = segment_ids(lengths)

    def forward(inputs, qkv_all, out_all, up_all, down_all, norm_all):
        encoded = layer(inputs[0], low(qkv_all[0]), low(out_all[0]), low(up_all[0]), low(down_all[0]), low(norm_all[0]), segments)
        sent = low(low_back(encoded))
        decoded = layer(inputs[1] + sent, low(qkv_all[1]), low(out_all[1]), low(up_all[1]), low(down_all[1]), low(norm_all[1]), segments)
        return jnp.stack([encoded, decoded])
    outputs, pullback = jax.vjp(forward, tokens.astype(jnp.float32), qkv_weight, out_weight, up_weight, down_weight, norm_params)
    grads = pullback(cotangent.astype(jnp.float32))
    qkv_new = update(grads[1], qkv_weight, qkv_momentum, qkv_average, rate_qkv)
    out_new = update(grads[2], out_weight, out_momentum, out_average, rate_out)
    up_new = update(grads[3], up_weight, up_momentum, up_average, rate_up)
    down_new = update(grads[4], down_weight, down_momentum, down_average, rate_down)
    norm_new = update(grads[5], norm_params, norm_momentum, norm_average, rate_norm)
    return (outputs.astype(jnp.bfloat16), grads[0], qkv_new[0], qkv_new[1], qkv_new[2], qkv_new[3], out_new[0], out_new[1], out_new[2], out_new[3], up_new[0], up_new[1], up_new[2], up_new[3], down_new[0], down_new[1], down_new[2], down_new[3], norm_new[0], norm_new[1], norm_new[2], norm_new[3], grads[5][:, 3, :])
```

```python
import functools
import math

import jax
import jax.numpy as jnp
from jax import lax
from jax.experimental import pallas as pl
from jax.experimental.pallas import tpu as pltpu
from jax.sharding import PartitionSpec as P

HEADS = 8
HEAD_DIM = 64
STEP = 5

eps = 1e-05
momentum_decay = 0.9
rate_qkv = 0.0001
rate_out = 0.01
rate_up = 0.0002
rate_down = 4e-05
rate_norm = 0.0004
neg_large = -1e30

low = jnp.bfloat16
full = jnp.float32

NN = (((1,), (0,)), ((), ()))
NT = (((1,), (1,)), ((), ()))
TN = (((0,), (0,)), ((), ()))

POWER = math.log2(math.e) * HEAD_DIM ** (-0.5)
SCALE = HEAD_DIM ** (-0.5)
GELU_C = math.sqrt(2.0 / math.pi)
GELU_A = 0.044715
LANES = 128
TILE = 16
PARTS = 4
VMEM_LIMIT = 58 * 2**20


def dot(a, b, dims):
    return lax.dot_general(a, b, dims, preferred_element_type=full)


def norm_stats(values):
    centre = values - jnp.mean(values, axis=-1, keepdims=True)
    spread = jnp.mean(centre * centre, axis=-1, keepdims=True)
    scale = lax.rsqrt(spread + eps)
    return centre * scale, scale


def norm_back(hat, scale, gain, grad):
    inner = grad * gain
    back = scale * (
        inner
        - jnp.mean(inner, axis=-1, keepdims=True)
        - hat * jnp.mean(inner * hat, axis=-1, keepdims=True)
    )
    return (
        back,
        jnp.sum(grad * hat, axis=0, keepdims=True),
        jnp.sum(grad, axis=0, keepdims=True),
    )


def norm_rows(block):
    return jnp.sum(block.astype(full), axis=0)


def gelu_both(u):
    square = u * u
    t = jnp.tanh(GELU_C * u * (1.0 + GELU_A * square))
    half = 0.5 + 0.5 * t
    slope = half + (0.5 * GELU_C) * u * (1.0 - t * t) * (1.0 + (3.0 * GELU_A) * square)
    return u * half, slope


def masks(lengths_ref, rows):
    place = lax.broadcasted_iota(jnp.int32, (rows, LANES), 0)
    lane = lax.broadcasted_iota(jnp.int32, (rows, LANES), 1)
    first = lengths_ref[0]
    second = first + lengths_ref[1]
    third = second + lengths_ref[2]
    item = (
        (place >= first).astype(jnp.int32)
        + (place >= second).astype(jnp.int32)
        + (place >= third).astype(jnp.int32)
    )
    own = item == lane
    query = jnp.where(own, neg_large, 0.0).astype(low)
    key = jnp.where(own | (lane > 3), 0.0, 1.0).astype(low)
    return query, key


def added(refs, rows=slice(None)):
    total = refs[0][rows].astype(full)
    for ref in refs[1:]:
        total = total + ref[rows].astype(full)
    return total


def attend_kernel(count, per, block, *refs):
    lengths_ref, refs = refs[0], refs[1:]
    inputs, refs = refs[:count], refs[count:]
    weight_ref, q_ref, k_ref, v_ref, o_ref, log_ref, a_s, vt_s, qm_s, km_s = refs
    length, width = q_ref.shape
    norm_vals = norm_rows(weight_ref[:, 3 * per : 3 * per + TILE, :])

    def weight(j):
        return weight_ref[:, j * per : (j + 1) * per, :].reshape(width, width)

    hat, _ = norm_stats(added(inputs))
    a_s[...] = (hat * norm_vals[0:1] + norm_vals[1:2]).astype(low)
    qm_s[...], km_s[...] = masks(lengths_ref, length)
    q_ref[...] = dot(a_s[...], weight(0), NN).astype(low)
    k_ref[...] = dot(a_s[...], weight(1), NN).astype(low)
    v_ref[...] = dot(a_s[...], weight(2), NN).astype(low)
    vt_s[...] = v_ref[...].T
    lanes = lax.broadcasted_iota(jnp.int32, (1, LANES), 1)
    zero = jnp.zeros((), low)

    jobs = [
        (p, h, b)
        for p in range(width // LANES)
        for h in range(2)
        for b in range(length // block)
    ]

    def scores(job):
        p, h, b = job
        cols = slice(p * LANES, (p + 1) * LANES)
        rows = slice(b * block, (b + 1) * block)
        queries = jnp.where(lanes // HEAD_DIM == h, q_ref[rows, cols], zero)
        return dot(
            jnp.concatenate([k_ref[:, cols], km_s[...]], axis=1),
            jnp.concatenate([queries, qm_s[rows, :]], axis=1),
            NT,
        )

    ahead = scores(jobs[0])
    for i, (p, h, b) in enumerate(jobs):
        s = ahead
        if i + 1 < len(jobs):
            ahead = scores(jobs[i + 1])
        head = 2 * p + h
        rows = slice(head * HEAD_DIM, (head + 1) * HEAD_DIM)
        cols = slice(b * block, (b + 1) * block)
        top = jnp.max(s, axis=0, keepdims=True) * POWER
        raised = jnp.exp2(s * POWER - top)
        total = jnp.sum(raised, axis=0, keepdims=True)
        mixed = dot(vt_s[rows, :], raised.astype(low), NN)
        o_ref[rows, cols] = (mixed * (1.0 / total)).astype(low)
        log_ref[head : head + 1, cols] = top + jnp.log2(total)


def attend(lengths, inputs, weights, per):
    length, width = inputs[0].shape
    shape = jax.ShapeDtypeStruct
    flops = 2 * length * width * width * 3 + 8 * length * length * width
    return pl.pallas_call(
        functools.partial(attend_kernel, len(inputs), per, min(512, length)),
        out_shape=(
            shape((length, width), low),
            shape((length, width), low),
            shape((length, width), low),
            shape((width, length), low),
            shape((HEADS, length), full),
        ),
        in_specs=[pl.BlockSpec(memory_space=pltpu.SMEM)]
        + [pl.BlockSpec(memory_space=pltpu.VMEM)] * (len(inputs) + 1),
        out_specs=[pl.BlockSpec(memory_space=pltpu.VMEM)] * 5,
        scratch_shapes=[
            pltpu.VMEM((length, width), low),
            pltpu.VMEM((width, length), low),
            pltpu.VMEM((length, LANES), low),
            pltpu.VMEM((length, LANES), low),
        ],
        compiler_params=pltpu.CompilerParams(vmem_limit_bytes=VMEM_LIMIT),
        cost_estimate=pl.CostEstimate(
            flops=2 * flops, bytes_accessed=8 * 2**20, transcendentals=HEADS * length * length
        ),
        name="attend",
    )(lengths, *inputs, weights)


def attend_back_kernel(count, per, block, *refs):
    lengths_ref, refs = refs[0], refs[1:]
    inputs, refs = refs[:count], refs[count:]
    (
        weight_ref, q_ref, k_ref, v_ref, do_ref, dot_ref, log_ref, sum_ref, dx2_ref,
        dx_ref, dxl_ref, grad_ref,
        qt_s, kt_s, dqt_s, dkt_s, dvt_s, dk_s, dv_s, qm_s, km_s,
    ) = refs
    length, width = q_ref.shape
    devices = weight_ref.shape[0]
    blocks = length // block
    qm_s[...], km_s[...] = masks(lengths_ref, length)
    qt_s[...] = q_ref[...].T
    kt_s[...] = k_ref[...].T
    lanes = lax.broadcasted_iota(jnp.int32, (1, LANES), 1)
    zero = jnp.zeros((), low)

    def pair(p, carry):
        off = pl.multiple_of(p * LANES, LANES)
        wide = pl.ds(off, LANES)
        keys = jnp.concatenate([k_ref[:, wide], km_s[...]], axis=1)
        jobs = [(h, b) for h in range(2) for b in range(blocks)]

        def scores(job):
            h, b = job
            rows = slice(b * block, (b + 1) * block)
            keep = lanes // HEAD_DIM == h
            queries = jnp.where(keep, q_ref[rows, wide], zero)
            outer = jnp.where(keep, do_ref[rows, wide], zero)
            return (
                dot(keys, jnp.concatenate([queries, qm_s[rows, :]], axis=1), NT),
                dot(v_ref[:, wide], outer, NT),
            )

        ahead = scores(jobs[0])
        for i, (h, b) in enumerate(jobs):
            s, dp = ahead
            if i + 1 < len(jobs):
                ahead = scores(jobs[i + 1])
            rows = pl.ds(pl.multiple_of(off + h * HEAD_DIM, HEAD_DIM), HEAD_DIM)
            cols = slice(b * block, (b + 1) * block)
            head = pl.ds(2 * p + h, 1)
            prob = jnp.exp2(s * POWER - log_ref[head, cols])
            ds = (prob * (dp - sum_ref[head, cols])).astype(low)
            prob = prob.astype(low)
            dv = dot(dot_ref[rows, cols], prob, NT)
            dk = dot(qt_s[rows, cols], ds, NT)
            dqt_s[rows, cols] = (dot(kt_s[rows, :], ds, NN) * SCALE).astype(low)
            if b > 0:
                dv = dv_s[...] + dv
                dk = dk_s[...] + dk
            if b < blocks - 1:
                dv_s[...] = dv
                dk_s[...] = dk
            else:
                dvt_s[rows, :] = dv.astype(low)
                dkt_s[rows, :] = (dk * SCALE).astype(low)
        return carry

    lax.fori_loop(0, width // LANES, pair, 0)

    norm_vals = norm_rows(weight_ref[:, 3 * per : 3 * per + TILE, :])
    hat, scale = norm_stats(added(inputs))
    a = (hat * norm_vals[0:1] + norm_vals[1:2]).astype(low)
    da = jnp.zeros((length, width), full)
    for j, piece in enumerate((dqt_s, dkt_s, dvt_s)):
        weight = weight_ref[:, j * per : (j + 1) * per, :].reshape(width, width)
        grads = piece[...].T
        da = da + dot(grads, weight, NT)
        grad_ref[:, j * per : (j + 1) * per, :] = (
            dot(a, grads, TN).astype(low).reshape(devices, per, width)
        )
    back, gain, shift = norm_back(hat, scale, norm_vals[0:1], da)
    dx = dx2_ref[...] + back
    dx_ref[...] = dx
    dxl_ref[...] = dx.astype(low)
    tail = jnp.concatenate([gain, shift, jnp.zeros((TILE - 2, width), full)], axis=0)
    grad_ref[:, 3 * per : 3 * per + TILE, :] = jnp.broadcast_to(
        tail.astype(low)[None], (devices, TILE, width)
    )


def attend_back(lengths, inputs, weights, kept, outer, outer_t, sums, dx2, per):
    q, k, v, _, logs = kept
    length, width = q.shape
    shape = jax.ShapeDtypeStruct
    flops = 2 * length * width * width * 6 + 20 * length * length * width
    return pl.pallas_call(
        functools.partial(attend_back_kernel, len(inputs), per, min(256, length)),
        out_shape=(
            shape((length, width), full),
            shape((length, width), low),
            shape(weights.shape, low),
        ),
        in_specs=[pl.BlockSpec(memory_space=pltpu.SMEM)]
        + [pl.BlockSpec(memory_space=pltpu.VMEM)] * (len(inputs) + 9),
        out_specs=[pl.BlockSpec(memory_space=pltpu.VMEM)] * 3,
        scratch_shapes=[pltpu.VMEM((width, length), low)] * 5
        + [pltpu.VMEM((HEAD_DIM, length), full)] * 2
        + [pltpu.VMEM((length, LANES), low)] * 2,
        compiler_params=pltpu.CompilerParams(vmem_limit_bytes=VMEM_LIMIT),
        cost_estimate=pl.CostEstimate(
            flops=2 * flops, bytes_accessed=16 * 2**20, transcendentals=HEADS * length * length
        ),
        name="attend_back",
    )(lengths, *inputs, weights, q, k, v, outer, outer_t, logs, sums, dx2)


def middle_start(inputs, o_ref, out_ref, norm_ref, width):
    norm_vals = norm_rows(norm_ref[...])
    x2 = added(inputs) + dot(o_ref[...], out_ref[...].reshape(width, width), TN)
    hat, _ = norm_stats(x2)
    return x2, (hat * norm_vals[2:3] + norm_vals[3:4]).astype(low)


def ffn_forward_kernel(count, block, *refs):
    inputs, refs = refs[:count], refs[count:]
    o_ref, norm_ref, out_ref, up_ref, down_ref, x2_ref, h_ref, slope_ref, y_ref, c_s, acc_s = refs
    length, width = x2_ref.shape
    j = pl.program_id(0)

    @pl.when(j == 0)
    def _():
        x2, c = middle_start(inputs, o_ref, out_ref, norm_ref, width)
        x2_ref[...] = x2
        acc_s[...] = x2
        c_s[...] = c

    up = up_ref[...].reshape(width, width)
    down = down_ref[...].reshape(width, width)
    spans = [slice(i, i + block) for i in range(0, length, block)]
    ahead = dot(c_s[spans[0], :], up, NN)
    for i, rows in enumerate(spans):
        u = ahead
        if i + 1 < len(spans):
            ahead = dot(c_s[spans[i + 1], :], up, NN)
        h, slope = gelu_both(u)
        h = h.astype(low)
        h_ref[rows, :] = h
        slope_ref[rows, :] = slope.astype(low)
        acc_s[rows, :] += dot(h, down, NN)

    @pl.when(j == pl.num_programs(0) - 1)
    def _():
        y_ref[...] = acc_s[...].astype(low)


def piece_specs(devices, per, width):
    return [
        pl.BlockSpec((devices, per, width), lambda j: (0, 8, 0)),
        pl.BlockSpec((devices, per, width), lambda j: (0, j, 0)),
        pl.BlockSpec((devices // PARTS, 4 * per, width), lambda j: (j, 1, 0)),
    ]


def constant(*dims):
    return pl.BlockSpec(dims, lambda j: (0,) * len(dims))


def norm_spec(devices, per, width):
    return pl.BlockSpec((devices, TILE, width), lambda j: (0, 3 * per // TILE, 0))


def ffn_forward(inputs, mixed, first, second, per):
    length, width = inputs[0].shape
    devices = first.shape[0]
    shape = jax.ShapeDtypeStruct
    hidden = PARTS * width
    return pl.pallas_call(
        functools.partial(ffn_forward_kernel, len(inputs), min(256, length)),
        grid=(PARTS,),
        out_shape=(
            shape((length, width), full),
            shape((length, hidden), low),
            shape((length, hidden), low),
            shape((length, width), low),
        ),
        in_specs=[constant(length, width)] * len(inputs)
        + [constant(width, length), norm_spec(devices, per, width)]
        + piece_specs(devices, per, width),
        out_specs=[
            constant(length, width),
            pl.BlockSpec((length, width), lambda j: (0, j)),
            pl.BlockSpec((length, width), lambda j: (0, j)),
            constant(length, width),
        ],
        scratch_shapes=[pltpu.VMEM((length, width), low), pltpu.VMEM((length, width), full)],
        compiler_params=pltpu.CompilerParams(vmem_limit_bytes=VMEM_LIMIT),
        cost_estimate=pl.CostEstimate(
            flops=2 * length * width * width * 9,
            bytes_accessed=16 * 2**20,
            transcendentals=length * hidden,
        ),
        name="ffn_forward",
    )(*inputs, mixed, first, second, second, second)


def ffn_back_kernel(count, fused, block, *refs):
    if fused:
        inputs, refs = refs[:count], refs[count:]
        (
            o_ref, cot_ref, norm_ref, out_ref, up_ref, down_ref,
            y_ref, dx2_ref, do_ref, dot_ref, sum_ref, grad_ref,
            c_s, dc_s, h_s, du_s, x2_ref, acc_s,
        ) = refs
        dyb_ref = cot_ref
    else:
        (
            x2_ref, h_ref, slope_ref, later_ref,
            o_ref, cot_ref, norm_ref, out_ref, up_ref, down_ref,
            dx2_ref, do_ref, dot_ref, sum_ref, grad_ref,
            c_s, dc_s, h_s, du_s, dyb_ref,
        ) = refs
        h_s = h_ref
    length, width = dx2_ref.shape
    devices, per, _ = out_ref.shape
    j = pl.program_id(0)

    def cot(rows):
        dy = cot_ref[rows, :].astype(full)
        if not fused:
            dy = dy + later_ref[rows, :].astype(low).astype(full)
        return dy

    everything = slice(0, length)

    @pl.when(j == 0)
    def _():
        if fused:
            x2, c = middle_start(inputs, o_ref, out_ref, norm_ref, width)
            x2_ref[...] = x2
            acc_s[...] = x2
        else:
            norm_vals = norm_rows(norm_ref[...])
            hat, _ = norm_stats(x2_ref[...])
            c = (hat * norm_vals[2:3] + norm_vals[3:4]).astype(low)
            dyb_ref[...] = cot(everything).astype(low)
        c_s[...] = c
        dc_s[...] = jnp.zeros((length, width), full)

    up = up_ref[...].reshape(width, width)
    down = down_ref[...].reshape(width, width)
    spans = [slice(i, i + block) for i in range(0, length, block)]

    def products(rows):
        dh = dot(dyb_ref[rows, :], down, NT)
        return (dot(c_s[rows, :], up, NN) if fused else None), dh

    ahead = products(spans[0])
    for i, rows in enumerate(spans):
        u, dh = ahead
        if i + 1 < len(spans):
            ahead = products(spans[i + 1])
        if fused:
            h, slope = gelu_both(u)
            h = h.astype(low)
            h_s[rows, :] = h
            acc_s[rows, :] += dot(h, down, NN)
        else:
            slope = slope_ref[rows, :].astype(full)
        du = (slope * dh).astype(low)
        du_s[rows, :] = du
        dc_s[rows, :] += dot(du, up, NT)
    grad_ref[pl.ds(j * (devices // PARTS), devices // PARTS), 4 * per : 8 * per, :] = (
        dot(h_s[...], dyb_ref[...], TN).astype(low).reshape(devices // PARTS, 4 * per, width)
    )
    grad_ref[:, pl.ds(pl.multiple_of(j * per, TILE), per), :] = (
        dot(c_s[...], du_s[...], TN).astype(low).reshape(devices, per, width)
    )

    @pl.when(j == pl.num_programs(0) - 1)
    def _():
        if fused:
            y_ref[...] = acc_s[...].astype(low)
        norm_vals = norm_rows(norm_ref[...])
        hat, scale = norm_stats(x2_ref[...])
        back, gain, shift = norm_back(hat, scale, norm_vals[2:3], dc_s[...])
        dx2 = cot(everything) + back
        dx2_ref[...] = dx2
        dab = dx2.astype(low)
        out = out_ref[...].reshape(width, width)
        grad_ref[:, 8 * per : 9 * per, :] = (
            dot(o_ref[...], dab, NN).astype(low).reshape(devices, per, width)
        )
        do_ref[...] = dot(dab, out, NT).astype(low)
        outer = dot(out, dab, NT).astype(low)
        dot_ref[...] = outer
        product = outer.astype(full) * o_ref[...].astype(full)
        sum_ref[...] = jnp.sum(product.reshape(HEADS, HEAD_DIM, length), axis=1)
        zeros = jnp.zeros((2, width), full)
        tail = jnp.concatenate(
            [zeros, gain, shift, jnp.zeros((TILE - 4, width), full)], axis=0
        )
        grad_ref[:, 9 * per : 9 * per + TILE, :] = jnp.broadcast_to(
            tail.astype(low)[None], (devices, TILE, width)
        )


def ffn_back(inputs, kept, mixed, cot, first, second, per):
    fused = kept is None
    length, width = cot.shape
    devices = first.shape[0]
    shape = jax.ShapeDtypeStruct
    rows = second.shape[1] + TILE
    hidden = PARTS * width
    column = pl.BlockSpec((length, width), lambda j: (0, j))
    ahead = [constant(length, width)] * len(inputs) if fused else [
        constant(length, width), column, column, constant(length, width)]
    outs = [
        (shape((length, width), full), constant(length, width)),
        (shape((length, width), low), constant(length, width)),
        (shape((width, length), low), constant(width, length)),
        (shape((HEADS, length), full), constant(HEADS, length)),
        (shape((devices, rows, width), low), constant(devices, rows, width)),
    ]
    scratch = [
        pltpu.VMEM((length, width), low),
        pltpu.VMEM((length, width), full),
        pltpu.VMEM((length, width) if fused else (TILE, LANES), low),
        pltpu.VMEM((length, width), low),
    ]
    if fused:
        outs = [(shape((length, width), low), constant(length, width))] + outs
        scratch += [pltpu.VMEM((length, width), full)] * 2
    else:
        scratch += [pltpu.VMEM((length, width), low)]
    return pl.pallas_call(
        functools.partial(ffn_back_kernel, len(inputs), fused, min(256, length)),
        grid=(PARTS,),
        out_shape=tuple(o[0] for o in outs),
        in_specs=ahead
        + [constant(width, length), constant(length, width), norm_spec(devices, per, width)]
        + piece_specs(devices, per, width),
        out_specs=tuple(o[1] for o in outs),
        scratch_shapes=scratch,
        compiler_params=pltpu.CompilerParams(vmem_limit_bytes=VMEM_LIMIT),
        cost_estimate=pl.CostEstimate(
            flops=2 * length * width * width * (28 if fused else 19),
            bytes_accessed=24 * 2**20,
            transcendentals=length * hidden if fused else 0,
        ),
        name="ffn_both" if fused else "ffn_back",
    )(*(inputs if fused else kept), mixed, cot, first, second, second, second)


def across(block, bit):
    devices = lax.axis_size("batch")
    return lax.ppermute(block, "batch", [(i, i ^ bit) for i in range(devices)])


def pick(blocks, index, axis=0):
    return lax.dynamic_index_in_dim(blocks, index, axis, keepdims=False)


def gather_pieces(piece):
    me = lax.axis_index("batch")
    held = piece[None]
    bit = lax.axis_size("batch") // 2
    order = []
    while bit:
        order.append(bit)
        bit //= 2
    for bit in order:
        other = across(held, bit)
        held = jnp.where(
            (me & bit) == 0,
            jnp.concatenate([held, other]),
            jnp.concatenate([other, held]),
        )
    digits = len(order)
    held = held.reshape((2,) * digits + piece.shape)
    return held.transpose(tuple(range(digits))[::-1] + (digits, digits + 1)).reshape(
        (-1,) + piece.shape
    )


def scatter_pieces(blocks):
    devices = blocks.shape[0]
    me = lax.axis_index("batch")
    bit = 1
    while devices > 1:
        halves = blocks.reshape((devices // 2, 2) + blocks.shape[1:])
        mine = pick(halves, (me // bit) % 2, 1)
        other = pick(halves, 1 - (me // bit) % 2, 1)
        blocks = (mine.astype(full) + across(other, bit).astype(full)).astype(low)
        devices //= 2
        bit *= 2
    return blocks[0]


def widen(gathered, sizes, times):
    if times == 1:
        return gathered
    devices, _, width = gathered.shape
    grouped = gathered.reshape(devices // times, times, -1, width)
    parts, at = [], 0
    for size in sizes:
        parts.append(
            grouped[:, :, at : at + size].reshape(devices // times, times * size, width)
        )
        at += size
    return jnp.concatenate(parts, axis=1)


def narrow(grads, sizes, times):
    if times == 1:
        return grads
    groups, _, width = grads.shape
    parts, at = [], 0
    for size in sizes:
        parts.append(
            grads[:, at : at + times * size].reshape(groups * times, size, width)
        )
        at += times * size
    rest = grads[:, at:]
    parts.append(jnp.repeat(rest, times, axis=0))
    return jnp.concatenate(parts, axis=1)


def update(gradient, weight, momentum, average, step_rate):
    new_momentum = momentum_decay * momentum + gradient
    new_weight = weight - step_rate * (gradient + momentum_decay * new_momentum)
    new_average = average + (new_weight - average) / (STEP + 1.0)
    return (gradient, new_momentum, new_weight, new_average)


def shards(
    tokens,
    cotangent,
    lengths,
    qkv_weight,
    qkv_momentum,
    qkv_average,
    out_weight,
    out_momentum,
    out_average,
    up_weight,
    up_momentum,
    up_average,
    down_weight,
    down_momentum,
    down_average,
    norm_params,
    norm_momentum,
    norm_average,
):
    section = lax.axis_index("section")
    here = lax.axis_index("batch")
    width = tokens.shape[2]
    length = tokens.shape[1] // lengths.shape[0]
    assert lengths.shape[0] == lax.axis_size("section") == 2
    own_rows = out_weight.shape[1]
    times = max(1, TILE // own_rows)
    per = own_rows * times
    first_sizes = (own_rows,) * 3
    second_sizes = (own_rows,) * PARTS + (PARTS * own_rows, own_rows)

    def swap(block):
        return lax.ppermute(block, "section", [(0, 1), (1, 0)])

    def sorted_pair(mine, other):
        is_first = section == 0
        return jnp.where(is_first, mine, other), jnp.where(is_first, other, mine)

    lengths_mine = pick(lengths, section)
    norm_table = lax.dynamic_update_slice(
        jnp.zeros((TILE, width), low),
        norm_params[0].astype(low),
        (0, here * norm_params.shape[2]),
    )
    pack_first = jnp.concatenate(
        [qkv_weight[0].astype(low).reshape(-1, width), norm_table], axis=0
    )
    up_low = up_weight[0].astype(low).reshape(own_rows, PARTS, width)
    pack_second = jnp.concatenate(
        [
            up_low.transpose(1, 0, 2).reshape(-1, width),
            down_weight[0].astype(low),
            out_weight[0].astype(low),
        ],
        axis=0,
    )
    pair_first = sorted_pair(pack_first, swap(pack_first))
    pair_second = sorted_pair(pack_second, swap(pack_second))

    def full_first(piece):
        gathered = gather_pieces(piece)
        if times == 1:
            return gathered
        body = widen(gathered[:, : 3 * own_rows], first_sizes, times)
        table = gathered[:, 3 * own_rows :].reshape(-1, times, TILE, width)
        return jnp.concatenate([body, jnp.sum(table, axis=1)], axis=1)

    def full_second(piece):
        gathered = lax.all_gather(piece, "batch", axis=0, tiled=False)
        return widen(gathered, second_sizes, times)

    first = [full_first(piece) for piece in pair_first]
    second = [full_second(piece) for piece in pair_second]

    token_rows = tokens[0].reshape(2, length, width)
    cot_rows = cotangent[0].reshape(2, length, width)
    encoder_in, denoiser_in = sorted_pair(
        pick(token_rows, section), swap(pick(token_rows, 1 - section))
    )
    encoder_cot, denoiser_cot = sorted_pair(
        pick(cot_rows, section), swap(pick(cot_rows, 1 - section))
    )

    kept_e = attend(lengths_mine, [encoder_in], first[0], per)
    x2_e, hidden_e, slope_e, encoded = ffn_forward(
        [encoder_in], kept_e[3], first[0], second[0], per
    )
    inputs_d = [denoiser_in, encoded]
    kept_d = attend(lengths_mine, inputs_d, first[1], per)
    decoded, dx2_d, do_d, dot_d, sum_d, grads_second_d = ffn_back(
        inputs_d, None, kept_d[3], denoiser_cot, first[1], second[1], per
    )

    def reduce_second(grads):
        grads = narrow(grads, second_sizes, times)
        return lax.psum_scatter(
            grads.reshape(-1, width), "batch", scatter_dimension=0, tiled=True
        )

    second_d = reduce_second(grads_second_d)
    dx_d, dx_low_d, grads_first_d = attend_back(
        lengths_mine, inputs_d, first[1], kept_d, do_d, dot_d, sum_d, dx2_d, per
    )
    grads_first_d = narrow(grads_first_d, first_sizes, times)
    first_d = lax.psum_scatter(
        grads_first_d.reshape(-1, width), "batch", scatter_dimension=0, tiled=True
    )
    dx2_e, do_e, dot_e, sum_e, grads_second_e = ffn_back(
        [], (x2_e, hidden_e, slope_e, dx_d), kept_e[3], encoder_cot, first[0], second[0], per
    )
    second_e = reduce_second(grads_second_e)
    dx_e, dx_low_e, grads_first_e = attend_back(
        lengths_mine, [encoder_in], first[0], kept_e, do_e, dot_e, sum_e, dx2_e, per
    )
    first_e = scatter_pieces(narrow(grads_first_e, first_sizes, times))

    def summed(of_first, of_second):
        is_first = section == 0
        mine = jnp.where(is_first, of_first, of_second)
        other = swap(jnp.where(is_first, of_second, of_first))
        return mine.astype(full) + other.astype(full)

    total_second = summed(second_e, second_d)
    total_first = summed(first_e, first_d)

    def both(encoder_part, denoiser_part, encoder_sent, denoiser_sent):
        received = swap(jnp.where(section == 0, denoiser_sent, encoder_sent))
        mine = jnp.where(section == 0, encoder_part, denoiser_part)
        received = received.astype(mine.dtype)
        return jnp.where(
            section == 0, jnp.stack([mine, received]), jnp.stack([received, mine])
        ).reshape(1, 2 * length, width)

    activations = both(encoded, decoded, encoded, decoded)
    input_grad = both(dx_e, dx_d, dx_low_e, dx_low_d)

    qkv_grad = total_first[: 3 * own_rows].reshape(qkv_weight.shape)
    up_grad = total_second[: 4 * own_rows].reshape(PARTS, own_rows, width)
    up_grad = up_grad.transpose(1, 0, 2).reshape(up_weight.shape)
    down_grad = total_second[4 * own_rows : 8 * own_rows][None]
    out_grad = total_second[8 * own_rows : 9 * own_rows][None]
    norm_all = jnp.concatenate(
        [
            total_first[3 * own_rows : 3 * own_rows + 2],
            total_second[9 * own_rows + 2 : 9 * own_rows + 4],
        ],
        axis=0,
    )
    own_features = norm_params.shape[2]
    norm_grad = lax.dynamic_slice(
        norm_all, (0, here * own_features), (4, own_features)
    )[None]
    qkv_new = update(qkv_grad, qkv_weight, qkv_momentum, qkv_average, rate_qkv)
    out_new = update(out_grad, out_weight, out_momentum, out_average, rate_out)
    up_new = update(up_grad, up_weight, up_momentum, up_average, rate_up)
    down_new = update(down_grad, down_weight, down_momentum, down_average, rate_down)
    norm_new = update(norm_grad, norm_params, norm_momentum, norm_average, rate_norm)
    return (
        activations,
        input_grad,
        *qkv_new,
        *out_new,
        *up_new,
        *down_new,
        *norm_new,
        norm_grad[:, 3],
    )


def solution(mesh):
    rows = P("section", "batch", None)
    deep = P("section", None, "batch", None)
    features = P("section", None, "batch")
    return jax.shard_map(
        shards,
        mesh=mesh,
        in_specs=(rows, rows, P("batch", None))
        + (deep,) * 3
        + (rows,) * 9
        + (features,) * 3,
        out_specs=(rows, rows)
        + (deep,) * 4
        + (rows,) * 12
        + (features,) * 4
        + (P("section", "batch"),),
        check_vma=False,
    )
```

```python
import functools
import math

import jax
import jax.numpy as jnp
from jax import lax
from jax.experimental import pallas as pl
from jax.experimental.pallas import tpu as pltpu
from jax.sharding import PartitionSpec as P

HEADS = 8
HEAD_DIM = 64
STEP = 5

eps = 1e-05
momentum_decay = 0.9
rate_qkv = 0.0001
rate_out = 0.01
rate_up = 0.0002
rate_down = 4e-05
rate_norm = 0.0004
neg_large = -1e30

low = jnp.bfloat16
full = jnp.float32

NN = (((1,), (0,)), ((), ()))
NT = (((1,), (1,)), ((), ()))
TN = (((0,), (0,)), ((), ()))

POWER = math.log2(math.e) * HEAD_DIM ** (-0.5)
SCALE = HEAD_DIM ** (-0.5)
GELU_C = math.sqrt(2.0 / math.pi)
GELU_A = 0.044715
LANES = 128
TILE = 16
PARTS = 4
VMEM_LIMIT = 58 * 2**20


def dot(a, b, dims):
    return lax.dot_general(a, b, dims, preferred_element_type=full)


def norm_stats(values):
    centre = values - jnp.mean(values, axis=-1, keepdims=True)
    spread = jnp.mean(centre * centre, axis=-1, keepdims=True)
    scale = lax.rsqrt(spread + eps)
    return centre * scale, scale


def norm_back(hat, scale, gain, grad):
    inner = grad * gain
    back = scale * (
        inner
        - jnp.mean(inner, axis=-1, keepdims=True)
        - hat * jnp.mean(inner * hat, axis=-1, keepdims=True)
    )
    return (
        back,
        jnp.sum(grad * hat, axis=0, keepdims=True),
        jnp.sum(grad, axis=0, keepdims=True),
    )


def norm_rows(block):
    return jnp.sum(block.astype(full), axis=0)


def gelu_both(u):
    square = u * u
    t = jnp.tanh(GELU_C * u * (1.0 + GELU_A * square))
    half = 0.5 + 0.5 * t
    slope = half + (0.5 * GELU_C) * u * (1.0 - t * t) * (1.0 + (3.0 * GELU_A) * square)
    return u * half, slope


def masks(lengths_ref, rows):
    place = lax.broadcasted_iota(jnp.int32, (rows, LANES), 0)
    lane = lax.broadcasted_iota(jnp.int32, (rows, LANES), 1)
    first = lengths_ref[0]
    second = first + lengths_ref[1]
    third = second + lengths_ref[2]
    item = (
        (place >= first).astype(jnp.int32)
        + (place >= second).astype(jnp.int32)
        + (place >= third).astype(jnp.int32)
    )
    own = item == lane
    query = jnp.where(own, neg_large, 0.0).astype(low)
    key = jnp.where(own | (lane > 3), 0.0, 1.0).astype(low)
    return query, key


def added(refs, rows=slice(None)):
    total = refs[0][rows].astype(full)
    for ref in refs[1:]:
        total = total + ref[rows].astype(full)
    return total


def put_in_order(order_ref, weight_ref, ordered, per):
    for b in range(weight_ref.shape[0]):
        place = order_ref[b]
        for j in range(3):
            ordered[j, b * per : (b + 1) * per, :] = weight_ref[place, j * per : (j + 1) * per, :]


def put_blocks(order_ref, first, grad_ref, rows, values):
    count, size = values.shape[0], values.shape[1]
    for b in range(count):
        grad_ref[order_ref[first + b], rows, :] = values[b]


def attend_kernel(count, per, block, *refs):
    lengths_ref, order_ref, refs = refs[0], refs[1], refs[2:]
    inputs, refs = refs[:count], refs[count:]
    weight_ref, q_ref, k_ref, v_ref, o_ref, log_ref, a_s, vt_s, qm_s, km_s, w_s = refs
    length, width = q_ref.shape
    norm_vals = norm_rows(weight_ref[:, 3 * per : 3 * per + TILE, :])
    put_in_order(order_ref, weight_ref, w_s, per)

    def weight(j):
        return w_s[j]

    hat, _ = norm_stats(added(inputs))
    a_s[...] = (hat * norm_vals[0:1] + norm_vals[1:2]).astype(low)
    qm_s[...], km_s[...] = masks(lengths_ref, length)
    q_ref[...] = dot(a_s[...], weight(0), NN).astype(low)
    k_ref[...] = dot(a_s[...], weight(1), NN).astype(low)
    v_ref[...] = dot(a_s[...], weight(2), NN).astype(low)
    vt_s[...] = v_ref[...].T
    lanes = lax.broadcasted_iota(jnp.int32, (1, LANES), 1)
    zero = jnp.zeros((), low)

    jobs = [
        (p, h, b)
        for p in range(width // LANES)
        for h in range(2)
        for b in range(length // block)
    ]

    def scores(job):
        p, h, b = job
        cols = slice(p * LANES, (p + 1) * LANES)
        rows = slice(b * block, (b + 1) * block)
        queries = jnp.where(lanes // HEAD_DIM == h, q_ref[rows, cols], zero)
        return dot(
            jnp.concatenate([k_ref[:, cols], km_s[...]], axis=1),
            jnp.concatenate([queries, qm_s[rows, :]], axis=1),
            NT,
        )

    ahead = scores(jobs[0])
    for i, (p, h, b) in enumerate(jobs):
        s = ahead
        if i + 1 < len(jobs):
            ahead = scores(jobs[i + 1])
        head = 2 * p + h
        rows = slice(head * HEAD_DIM, (head + 1) * HEAD_DIM)
        cols = slice(b * block, (b + 1) * block)
        top = jnp.max(s, axis=0, keepdims=True) * POWER
        raised = jnp.exp2(s * POWER - top)
        total = jnp.sum(raised, axis=0, keepdims=True)
        mixed = dot(vt_s[rows, :], raised.astype(low), NN)
        o_ref[rows, cols] = (mixed * (1.0 / total)).astype(low)
        log_ref[head : head + 1, cols] = top + jnp.log2(total)


def attend(lengths, order, inputs, weights, per):
    length, width = inputs[0].shape
    shape = jax.ShapeDtypeStruct
    flops = 2 * length * width * width * 3 + 8 * length * length * width
    return pl.pallas_call(
        functools.partial(attend_kernel, len(inputs), per, min(512, length)),
        out_shape=(
            shape((length, width), low),
            shape((length, width), low),
            shape((length, width), low),
            shape((width, length), low),
            shape((HEADS, length), full),
        ),
        in_specs=[pl.BlockSpec(memory_space=pltpu.SMEM)] * 2
        + [pl.BlockSpec(memory_space=pltpu.VMEM)] * (len(inputs) + 1),
        out_specs=[pl.BlockSpec(memory_space=pltpu.VMEM)] * 5,
        scratch_shapes=[
            pltpu.VMEM((length, width), low),
            pltpu.VMEM((width, length), low),
            pltpu.VMEM((length, LANES), low),
            pltpu.VMEM((length, LANES), low),
            pltpu.VMEM((3, width, width), low),
        ],
        compiler_params=pltpu.CompilerParams(vmem_limit_bytes=VMEM_LIMIT),
        cost_estimate=pl.CostEstimate(
            flops=2 * flops, bytes_accessed=8 * 2**20, transcendentals=HEADS * length * length
        ),
        name="attend",
    )(lengths, order, *inputs, weights)


def attend_back_kernel(count, per, block, *refs):
    lengths_ref, order_ref, refs = refs[0], refs[1], refs[2:]
    inputs, refs = refs[:count], refs[count:]
    (
        weight_ref, q_ref, k_ref, v_ref, do_ref, dot_ref, log_ref, sum_ref, dx2_ref,
        dx_ref, dxl_ref, grad_ref,
        qt_s, kt_s, dqt_s, dkt_s, dvt_s, dk_s, dv_s, qm_s, km_s, w_s,
    ) = refs
    length, width = q_ref.shape
    devices = weight_ref.shape[0]
    blocks = length // block
    qm_s[...], km_s[...] = masks(lengths_ref, length)
    put_in_order(order_ref, weight_ref, w_s, per)
    qt_s[...] = q_ref[...].T
    kt_s[...] = k_ref[...].T
    lanes = lax.broadcasted_iota(jnp.int32, (1, LANES), 1)
    zero = jnp.zeros((), low)

    def pair(p, carry):
        off = pl.multiple_of(p * LANES, LANES)
        wide = pl.ds(off, LANES)
        keys = jnp.concatenate([k_ref[:, wide], km_s[...]], axis=1)
        jobs = [(h, b) for h in range(2) for b in range(blocks)]

        def scores(job):
            h, b = job
            rows = slice(b * block, (b + 1) * block)
            keep = lanes // HEAD_DIM == h
            queries = jnp.where(keep, q_ref[rows, wide], zero)
            outer = jnp.where(keep, do_ref[rows, wide], zero)
            return (
                dot(keys, jnp.concatenate([queries, qm_s[rows, :]], axis=1), NT),
                dot(v_ref[:, wide], outer, NT),
            )

        ahead = scores(jobs[0])
        for i, (h, b) in enumerate(jobs):
            s, dp = ahead
            if i + 1 < len(jobs):
                ahead = scores(jobs[i + 1])
            rows = pl.ds(pl.multiple_of(off + h * HEAD_DIM, HEAD_DIM), HEAD_DIM)
            cols = slice(b * block, (b + 1) * block)
            head = pl.ds(2 * p + h, 1)
            prob = jnp.exp2(s * POWER - log_ref[head, cols])
            ds = (prob * (dp - sum_ref[head, cols])).astype(low)
            prob = prob.astype(low)
            dv = dot(dot_ref[rows, cols], prob, NT)
            dk = dot(qt_s[rows, cols], ds, NT)
            dqt_s[rows, cols] = (dot(kt_s[rows, :], ds, NN) * SCALE).astype(low)
            if b > 0:
                dv = dv_s[...] + dv
                dk = dk_s[...] + dk
            if b < blocks - 1:
                dv_s[...] = dv
                dk_s[...] = dk
            else:
                dvt_s[rows, :] = dv.astype(low)
                dkt_s[rows, :] = (dk * SCALE).astype(low)
        return carry

    lax.fori_loop(0, width // LANES, pair, 0)

    norm_vals = norm_rows(weight_ref[:, 3 * per : 3 * per + TILE, :])
    hat, scale = norm_stats(added(inputs))
    a = (hat * norm_vals[0:1] + norm_vals[1:2]).astype(low)
    da = jnp.zeros((length, width), full)
    for j, piece in enumerate((dqt_s, dkt_s, dvt_s)):
        grads = piece[...].T
        da = da + dot(grads, w_s[j], NT)
        put_blocks(
            order_ref,
            0,
            grad_ref,
            slice(j * per, (j + 1) * per),
            dot(a, grads, TN).astype(low).reshape(devices, per, width),
        )
    back, gain, shift = norm_back(hat, scale, norm_vals[0:1], da)
    dx = dx2_ref[...] + back
    dx_ref[...] = dx
    dxl_ref[...] = dx.astype(low)
    tail = jnp.concatenate([gain, shift, jnp.zeros((TILE - 2, width), full)], axis=0)
    grad_ref[:, 3 * per : 3 * per + TILE, :] = jnp.broadcast_to(
        tail.astype(low)[None], (devices, TILE, width)
    )


def attend_back(lengths, order, inputs, weights, kept, outer, outer_t, sums, dx2, per):
    q, k, v, _, logs = kept
    length, width = q.shape
    shape = jax.ShapeDtypeStruct
    flops = 2 * length * width * width * 6 + 20 * length * length * width
    return pl.pallas_call(
        functools.partial(attend_back_kernel, len(inputs), per, min(256, length)),
        out_shape=(
            shape((length, width), full),
            shape((length, width), low),
            shape(weights.shape, low),
        ),
        in_specs=[pl.BlockSpec(memory_space=pltpu.SMEM)] * 2
        + [pl.BlockSpec(memory_space=pltpu.VMEM)] * (len(inputs) + 9),
        out_specs=[pl.BlockSpec(memory_space=pltpu.VMEM)] * 3,
        scratch_shapes=[pltpu.VMEM((width, length), low)] * 5
        + [pltpu.VMEM((HEAD_DIM, length), full)] * 2
        + [pltpu.VMEM((length, LANES), low)] * 2
        + [pltpu.VMEM((3, width, width), low)],
        compiler_params=pltpu.CompilerParams(vmem_limit_bytes=VMEM_LIMIT),
        cost_estimate=pl.CostEstimate(
            flops=2 * flops, bytes_accessed=16 * 2**20, transcendentals=HEADS * length * length
        ),
        name="attend_back",
    )(lengths, order, *inputs, weights, q, k, v, outer, outer_t, logs, sums, dx2)


def middle_start(inputs, o_ref, out_ref, norm_ref, width):
    norm_vals = norm_rows(norm_ref[...])
    x2 = added(inputs) + dot(o_ref[...], out_ref[...].reshape(width, width), TN)
    hat, _ = norm_stats(x2)
    return x2, (hat * norm_vals[2:3] + norm_vals[3:4]).astype(low)


def ffn_forward_kernel(count, block, *refs):
    inputs, refs = refs[:count], refs[count:]
    o_ref, norm_ref, out_ref, up_ref, down_ref, x2_ref, h_ref, slope_ref, y_ref, c_s, acc_s = refs
    length, width = x2_ref.shape
    j = pl.program_id(0)

    @pl.when(j == 0)
    def _():
        x2, c = middle_start(inputs, o_ref, out_ref, norm_ref, width)
        x2_ref[...] = x2
        acc_s[...] = x2
        c_s[...] = c

    up = up_ref[...].reshape(width, width)
    down = down_ref[...].reshape(width, width)
    spans = [slice(i, i + block) for i in range(0, length, block)]
    ahead = dot(c_s[spans[0], :], up, NN)
    for i, rows in enumerate(spans):
        u = ahead
        if i + 1 < len(spans):
            ahead = dot(c_s[spans[i + 1], :], up, NN)
        h, slope = gelu_both(u)
        h = h.astype(low)
        h_ref[rows, :] = h
        slope_ref[rows, :] = slope.astype(low)
        acc_s[rows, :] += dot(h, down, NN)

    @pl.when(j == pl.num_programs(0) - 1)
    def _():
        y_ref[...] = acc_s[...].astype(low)


def piece_specs(devices, per, width):
    return [
        pl.BlockSpec((devices, per, width), lambda j: (0, 8, 0)),
        pl.BlockSpec((devices, per, width), lambda j: (0, j, 0)),
        pl.BlockSpec((devices // PARTS, 4 * per, width), lambda j: (j, 1, 0)),
    ]


def constant(*dims):
    return pl.BlockSpec(dims, lambda j: (0,) * len(dims))


def norm_spec(devices, per, width):
    return pl.BlockSpec((devices, TILE, width), lambda j: (0, 3 * per // TILE, 0))


def ffn_forward(inputs, mixed, first, second, per):
    length, width = inputs[0].shape
    devices = first.shape[0]
    shape = jax.ShapeDtypeStruct
    hidden = PARTS * width
    return pl.pallas_call(
        functools.partial(ffn_forward_kernel, len(inputs), min(256, length)),
        grid=(PARTS,),
        out_shape=(
            shape((length, width), full),
            shape((length, hidden), low),
            shape((length, hidden), low),
            shape((length, width), low),
        ),
        in_specs=[constant(length, width)] * len(inputs)
        + [constant(width, length), norm_spec(devices, per, width)]
        + piece_specs(devices, per, width),
        out_specs=[
            constant(length, width),
            pl.BlockSpec((length, width), lambda j: (0, j)),
            pl.BlockSpec((length, width), lambda j: (0, j)),
            constant(length, width),
        ],
        scratch_shapes=[pltpu.VMEM((length, width), low), pltpu.VMEM((length, width), full)],
        compiler_params=pltpu.CompilerParams(vmem_limit_bytes=VMEM_LIMIT),
        cost_estimate=pl.CostEstimate(
            flops=2 * length * width * width * 9,
            bytes_accessed=16 * 2**20,
            transcendentals=length * hidden,
        ),
        name="ffn_forward",
    )(*inputs, mixed, first, second, second, second)


def ffn_back_kernel(count, fused, block, *refs):
    order_ref, refs = refs[0], refs[1:]
    if fused:
        inputs, refs = refs[:count], refs[count:]
        (
            o_ref, cot_ref, norm_ref, out_ref, up_ref, down_ref,
            y_ref, dx2_ref, do_ref, dot_ref, sum_ref, grad_ref,
            c_s, dc_s, h_s, du_s, x2_ref, acc_s,
        ) = refs
        dyb_ref = cot_ref
    else:
        (
            x2_ref, h_ref, slope_ref, later_ref,
            o_ref, cot_ref, norm_ref, out_ref, up_ref, down_ref,
            dx2_ref, do_ref, dot_ref, sum_ref, grad_ref,
            c_s, dc_s, h_s, du_s, dyb_ref,
        ) = refs
        h_s = h_ref
    length, width = dx2_ref.shape
    devices, per, _ = out_ref.shape
    j = pl.program_id(0)

    def cot(rows):
        dy = cot_ref[rows, :].astype(full)
        if not fused:
            dy = dy + later_ref[rows, :].astype(low).astype(full)
        return dy

    everything = slice(0, length)

    @pl.when(j == 0)
    def _():
        if fused:
            x2, c = middle_start(inputs, o_ref, out_ref, norm_ref, width)
            x2_ref[...] = x2
            acc_s[...] = x2
        else:
            norm_vals = norm_rows(norm_ref[...])
            hat, _ = norm_stats(x2_ref[...])
            c = (hat * norm_vals[2:3] + norm_vals[3:4]).astype(low)
            dyb_ref[...] = cot(everything).astype(low)
        c_s[...] = c
        dc_s[...] = jnp.zeros((length, width), full)

    up = up_ref[...].reshape(width, width)
    down = down_ref[...].reshape(width, width)
    spans = [slice(i, i + block) for i in range(0, length, block)]

    def products(rows):
        dh = dot(dyb_ref[rows, :], down, NT)
        return (dot(c_s[rows, :], up, NN) if fused else None), dh

    ahead = products(spans[0])
    for i, rows in enumerate(spans):
        u, dh = ahead
        if i + 1 < len(spans):
            ahead = products(spans[i + 1])
        if fused:
            h, slope = gelu_both(u)
            h = h.astype(low)
            h_s[rows, :] = h
            acc_s[rows, :] += dot(h, down, NN)
        else:
            slope = slope_ref[rows, :].astype(full)
        du = (slope * dh).astype(low)
        du_s[rows, :] = du
        dc_s[rows, :] += dot(du, up, NT)
    put_blocks(
        order_ref,
        j * (devices // PARTS),
        grad_ref,
        slice(4 * per, 8 * per),
        dot(h_s[...], dyb_ref[...], TN).astype(low).reshape(devices // PARTS, 4 * per, width),
    )
    put_blocks(
        order_ref,
        0,
        grad_ref,
        pl.ds(pl.multiple_of(j * per, TILE), per),
        dot(c_s[...], du_s[...], TN).astype(low).reshape(devices, per, width),
    )

    @pl.when(j == pl.num_programs(0) - 1)
    def _():
        if fused:
            y_ref[...] = acc_s[...].astype(low)
        norm_vals = norm_rows(norm_ref[...])
        hat, scale = norm_stats(x2_ref[...])
        back, gain, shift = norm_back(hat, scale, norm_vals[2:3], dc_s[...])
        dx2 = cot(everything) + back
        dx2_ref[...] = dx2
        dab = dx2.astype(low)
        out = out_ref[...].reshape(width, width)
        put_blocks(
            order_ref,
            0,
            grad_ref,
            slice(8 * per, 9 * per),
            dot(o_ref[...], dab, NN).astype(low).reshape(devices, per, width),
        )
        do_ref[...] = dot(dab, out, NT).astype(low)
        outer = dot(out, dab, NT).astype(low)
        dot_ref[...] = outer
        product = outer.astype(full) * o_ref[...].astype(full)
        sum_ref[...] = jnp.sum(product.reshape(HEADS, HEAD_DIM, length), axis=1)
        zeros = jnp.zeros((2, width), full)
        tail = jnp.concatenate(
            [zeros, gain, shift, jnp.zeros((TILE - 4, width), full)], axis=0
        )
        grad_ref[:, 9 * per : 9 * per + TILE, :] = jnp.broadcast_to(
            tail.astype(low)[None], (devices, TILE, width)
        )


def ffn_back(order, inputs, kept, mixed, cot, first, second, per):
    fused = kept is None
    length, width = cot.shape
    devices = first.shape[0]
    shape = jax.ShapeDtypeStruct
    rows = second.shape[1] + TILE
    hidden = PARTS * width
    column = pl.BlockSpec((length, width), lambda j: (0, j))
    ahead = [constant(length, width)] * len(inputs) if fused else [
        constant(length, width), column, column, constant(length, width)]
    outs = [
        (shape((length, width), full), constant(length, width)),
        (shape((length, width), low), constant(length, width)),
        (shape((width, length), low), constant(width, length)),
        (shape((HEADS, length), full), constant(HEADS, length)),
        (shape((devices, rows, width), low), constant(devices, rows, width)),
    ]
    scratch = [
        pltpu.VMEM((length, width), low),
        pltpu.VMEM((length, width), full),
        pltpu.VMEM((length, width) if fused else (TILE, LANES), low),
        pltpu.VMEM((length, width), low),
    ]
    if fused:
        outs = [(shape((length, width), low), constant(length, width))] + outs
        scratch += [pltpu.VMEM((length, width), full)] * 2
    else:
        scratch += [pltpu.VMEM((length, width), low)]
    return pl.pallas_call(
        functools.partial(ffn_back_kernel, len(inputs), fused, min(256, length)),
        grid=(PARTS,),
        out_shape=tuple(o[0] for o in outs),
        in_specs=[pl.BlockSpec(memory_space=pltpu.SMEM)]
        + ahead
        + [constant(width, length), constant(length, width), norm_spec(devices, per, width)]
        + piece_specs(devices, per, width),
        out_specs=tuple(o[1] for o in outs),
        scratch_shapes=scratch,
        compiler_params=pltpu.CompilerParams(vmem_limit_bytes=VMEM_LIMIT),
        cost_estimate=pl.CostEstimate(
            flops=2 * length * width * width * (28 if fused else 19),
            bytes_accessed=24 * 2**20,
            transcendentals=length * hidden if fused else 0,
        ),
        name="ffn_both" if fused else "ffn_back",
    )(order, *(inputs if fused else kept), mixed, cot, first, second, second, second)


def across(block, bit):
    devices = lax.axis_size("batch")
    return lax.ppermute(block, "batch", [(i, i ^ bit) for i in range(devices)])


def pick(blocks, index, axis=0):
    return lax.dynamic_index_in_dim(blocks, index, axis, keepdims=False)


def stages():
    bits = lax.axis_size("batch").bit_length() - 1
    high = list(range(bits - 1, 1, -1))
    groups = [high[i : i + 2][::-1] for i in range(0, len(high), 2)]
    return groups + [[b] for b in range(min(bits, 2) - 1, -1, -1)]


def partners(group):
    return [
        sum(((digit >> i) & 1) << b for i, b in enumerate(group))
        for digit in range(1, 1 << len(group))
    ]


def places(device):
    flips = device ^ lax.axis_index("batch")
    place, weight = jnp.zeros_like(device), 1
    for group in stages():
        for b in group:
            place = place + ((flips >> b) & 1) * weight
            weight *= 2
    return place


def flipped(blocks, axis, bit):
    halves = [lax.index_in_dim(blocks, i, axis) for i in range(2)]
    is_set = (lax.axis_index("batch") >> bit) & 1 == 1
    return jnp.where(is_set, jnp.concatenate(halves[::-1], axis), blocks)


def by_device(blocks):
    filled = [b for group in stages() for b in group]
    bits = len(filled)
    rest = tuple(range(bits, bits + blocks.ndim - 1))
    shape = blocks.shape
    blocks = blocks.reshape((2,) * bits + shape[1:])
    blocks = blocks.transpose(
        tuple(bits - 1 - filled.index(b) for b in range(bits - 1, -1, -1)) + rest
    )
    for b in range(bits):
        blocks = flipped(blocks, bits - 1 - b, b)
    return blocks.reshape(shape)


def by_place(blocks):
    filled = [b for group in stages() for b in group]
    bits = len(filled)
    rest = tuple(range(bits, bits + blocks.ndim - 1))
    shape = blocks.shape
    blocks = blocks.reshape((2,) * bits + shape[1:])
    for b in range(bits):
        blocks = flipped(blocks, bits - 1 - b, b)
    blocks = blocks.transpose(tuple(bits - 1 - b for b in filled[::-1]) + rest)
    return blocks.reshape(shape)


def tie(value, *after):
    return lax.optimization_barrier((value,) + after)[0]


def scatter_stage(blocks, group):
    ways = 1 << len(group)
    parts = blocks.reshape((ways, -1) + blocks.shape[1:])
    return parts[0], [
        across(parts[i + 1], flip) for i, flip in enumerate(partners(group))
    ]


def total_of(mine, received):
    total = mine.astype(full)
    for block in received:
        total = total + block.astype(full)
    return total


def widen(gathered, sizes, times):
    if times == 1:
        return gathered
    devices, _, width = gathered.shape
    grouped = gathered.reshape(devices // times, times, -1, width)
    parts, at = [], 0
    for size in sizes:
        parts.append(
            grouped[:, :, at : at + size].reshape(devices // times, times * size, width)
        )
        at += size
    return jnp.concatenate(parts, axis=1)


def narrow(grads, sizes, times):
    if times == 1:
        return grads
    groups, _, width = grads.shape
    parts, at = [], 0
    for size in sizes:
        parts.append(
            grads[:, at : at + times * size].reshape(groups * times, size, width)
        )
        at += times * size
    rest = grads[:, at:]
    parts.append(jnp.repeat(rest, times, axis=0))
    return jnp.concatenate(parts, axis=1)


def update(gradient, weight, momentum, average, step_rate):
    new_momentum = momentum_decay * momentum + gradient
    new_weight = weight - step_rate * (gradient + momentum_decay * new_momentum)
    new_average = average + (new_weight - average) / (STEP + 1.0)
    return (gradient, new_momentum, new_weight, new_average)


def shards(
    tokens,
    cotangent,
    lengths,
    qkv_weight,
    qkv_momentum,
    qkv_average,
    out_weight,
    out_momentum,
    out_average,
    up_weight,
    up_momentum,
    up_average,
    down_weight,
    down_momentum,
    down_average,
    norm_params,
    norm_momentum,
    norm_average,
):
    section = lax.axis_index("section")
    here = lax.axis_index("batch")
    width = tokens.shape[2]
    length = tokens.shape[1] // lengths.shape[0]
    assert lengths.shape[0] == lax.axis_size("section") == 2
    own_rows = out_weight.shape[1]
    times = max(1, TILE // own_rows)
    per = own_rows * times
    first_sizes = (own_rows,) * 3
    second_sizes = (own_rows,) * PARTS + (PARTS * own_rows, own_rows)

    def swap(block):
        return lax.ppermute(block, "section", [(0, 1), (1, 0)])

    def sorted_pair(mine, other):
        is_first = section == 0
        return jnp.where(is_first, mine, other), jnp.where(is_first, other, mine)

    lengths_mine = pick(lengths, section)
    norm_table = lax.dynamic_update_slice(
        jnp.zeros((TILE, width), low),
        norm_params[0].astype(low),
        (0, here * norm_params.shape[2]),
    )
    pack_first = jnp.concatenate(
        [qkv_weight[0].astype(low).reshape(-1, width), norm_table], axis=0
    )
    up_low = up_weight[0].astype(low).reshape(own_rows, PARTS, width)
    pack_second = jnp.concatenate(
        [
            up_low.transpose(1, 0, 2).reshape(-1, width),
            down_weight[0].astype(low),
            out_weight[0].astype(low),
        ],
        axis=0,
    )
    order = places(jnp.arange(lax.axis_size("batch"), dtype=jnp.int32))
    steps = stages()

    received_first = swap(pack_first)
    piece_e, piece_d = sorted_pair(pack_first, received_first)
    pair_second = sorted_pair(pack_second, swap(tie(pack_second, received_first)))
    token_rows = tokens[0].reshape(2, length, width)
    cot_rows = cotangent[0].reshape(2, length, width)
    token_other = swap(tie(pick(token_rows, 1 - section), received_first))

    held_e, held_d, coming = piece_e[None], piece_d[None], []
    for group in steps[:-1]:
        held_e = jnp.concatenate([held_e] + [across(held_e, f) for f in partners(group)])
        held_d = tie(jnp.concatenate([held_d] + coming), held_e)
        coming = [across(held_d, f) for f in partners(group)]
    held_e = jnp.concatenate([held_e] + [across(held_e, f) for f in partners(steps[-1])])

    def whole_first(held):
        if times == 1:
            return held
        held = by_device(held)
        body = widen(held[:, : 3 * own_rows], first_sizes, times)
        table = held[:, 3 * own_rows :].reshape(-1, times, TILE, width)
        return jnp.concatenate([body, jnp.sum(table, axis=1)], axis=1)

    def whole_second(piece):
        gathered = lax.all_gather(piece, "batch", axis=0, tiled=False)
        return widen(gathered, second_sizes, times)

    second = [whole_second(piece) for piece in pair_second]
    natural = jnp.arange(second[0].shape[0], dtype=jnp.int32)
    placed = order if times == 1 else natural

    encoder_in = jnp.where(section == 0, pick(token_rows, section), token_other)
    first_e = whole_first(held_e)
    kept_e = attend(lengths_mine, placed, [encoder_in], first_e, per)
    held_d = jnp.concatenate([held_d] + [tie(b, kept_e[4]) for b in coming])
    coming = [across(held_d, f) for f in partners(steps[-1])]
    cot_other = swap(tie(pick(cot_rows, 1 - section), kept_e[4]))
    x2_e, hidden_e, slope_e, encoded = ffn_forward(
        [encoder_in], kept_e[3], first_e, second[0], per
    )
    denoiser_in = jnp.where(
        section == 0, tie(token_other, kept_e[4]), pick(token_rows, section)
    )
    first_d = whole_first(jnp.concatenate([held_d] + [tie(b, encoded) for b in coming]))
    inputs_d = [denoiser_in, encoded]
    kept_d = attend(lengths_mine, placed, inputs_d, first_d, per)
    encoder_cot, denoiser_cot = sorted_pair(
        pick(cot_rows, section), tie(cot_other, kept_d[4])
    )
    decoded, dx2_d, do_d, dot_d, sum_d, grads_second_d = ffn_back(
        placed, inputs_d, None, kept_d[3], denoiser_cot, first_d, second[1], per
    )

    def ordered(grads, sizes):
        if times == 1:
            return grads
        return by_place(narrow(grads, sizes, times))

    back = steps[::-1]
    kept_second_d, sent = scatter_stage(ordered(grads_second_d, second_sizes), back[0])
    dx_d, dx_low_d, grads_first_d = attend_back(
        lengths_mine, placed, inputs_d, first_d, kept_d, do_d, dot_d, sum_d, dx2_d, per
    )
    half = total_of(kept_second_d, [tie(b, dx_low_d) for b in sent]).astype(low)
    kept_second_d, sent_second_d = scatter_stage(half, back[1])
    kept_first_d, sent_first_d = scatter_stage(ordered(grads_first_d, first_sizes), back[0])
    dx2_e, do_e, dot_e, sum_e, grads_second_e = ffn_back(
        natural, [], (x2_e, hidden_e, slope_e, tie(dx_d, half)), kept_e[3], encoder_cot, first_e, second[0], per
    )
    second_e = lax.psum_scatter(
        narrow(grads_second_e, second_sizes, times).reshape(-1, width),
        "batch",
        scatter_dimension=0,
        tiled=True,
    )
    half = total_of(kept_first_d, sent_first_d).astype(low)
    kept_first_d, sent_first_d = scatter_stage(half, back[1])
    dx_e, dx_low_e, grads_first_e = attend_back(
        lengths_mine, placed, [encoder_in], first_e, kept_e, do_e, dot_e, sum_e, tie(dx2_e, half), per
    )
    kept_first_e, sent_first_e = scatter_stage(ordered(grads_first_e, first_sizes), back[0])

    def finish(mine, received, later):
        for group in later:
            mine, received = scatter_stage(total_of(mine, received).astype(low), group)
        return total_of(mine, received)[0]

    second_d = finish(kept_second_d, [tie(b, dx_low_e) for b in sent_second_d], back[2:])
    first_d = finish(kept_first_d, [tie(b, dx_low_e) for b in sent_first_d], back[2:])
    first_e = finish(kept_first_e, sent_first_e, back[1:])

    def summed(of_first, of_second):
        is_first = section == 0
        mine = jnp.where(is_first, of_first.astype(full), of_second.astype(full))
        other = swap(jnp.where(is_first, of_second.astype(low), of_first.astype(low)))
        return mine + other.astype(full)

    total_second = summed(second_e, second_d)
    total_first = summed(first_e, first_d)

    def both(encoder_part, denoiser_part, received):
        mine = jnp.where(section == 0, encoder_part, denoiser_part)
        received = received.astype(mine.dtype)
        return jnp.where(
            section == 0, jnp.stack([mine, received]), jnp.stack([received, mine])
        ).reshape(1, 2 * length, width)

    activations = both(
        encoded, decoded, swap(tie(jnp.where(section == 0, decoded, encoded), dx2_d))
    )
    input_grad = both(dx_e, dx_d, swap(jnp.where(section == 0, dx_low_d, dx_low_e)))

    qkv_grad = total_first[: 3 * own_rows].reshape(qkv_weight.shape)
    up_grad = total_second[: 4 * own_rows].reshape(PARTS, own_rows, width)
    up_grad = up_grad.transpose(1, 0, 2).reshape(up_weight.shape)
    down_grad = total_second[4 * own_rows : 8 * own_rows][None]
    out_grad = total_second[8 * own_rows : 9 * own_rows][None]
    norm_all = jnp.concatenate(
        [
            total_first[3 * own_rows : 3 * own_rows + 2],
            total_second[9 * own_rows + 2 : 9 * own_rows + 4],
        ],
        axis=0,
    )
    own_features = norm_params.shape[2]
    norm_grad = lax.dynamic_slice(
        norm_all, (0, here * own_features), (4, own_features)
    )[None]
    qkv_new = update(qkv_grad, qkv_weight, qkv_momentum, qkv_average, rate_qkv)
    out_new = update(out_grad, out_weight, out_momentum, out_average, rate_out)
    up_new = update(up_grad, up_weight, up_momentum, up_average, rate_up)
    down_new = update(down_grad, down_weight, down_momentum, down_average, rate_down)
    norm_new = update(norm_grad, norm_params, norm_momentum, norm_average, rate_norm)
    return (
        activations,
        input_grad,
        *qkv_new,
        *out_new,
        *up_new,
        *down_new,
        *norm_new,
        norm_grad[:, 3],
    )


def solution(mesh):
    rows = P("section", "batch", None)
    deep = P("section", None, "batch", None)
    features = P("section", None, "batch")
    return jax.shard_map(
        shards,
        mesh=mesh,
        in_specs=(rows, rows, P("batch", None))
        + (deep,) * 3
        + (rows,) * 9
        + (features,) * 3,
        out_specs=(rows, rows)
        + (deep,) * 4
        + (rows,) * 12
        + (features,) * 4
        + (P("section", "batch"),),
        check_vma=False,
    )
```

```python
import functools
import math

import jax
import jax.numpy as jnp
from jax import lax
from jax.experimental import pallas as pl
from jax.experimental.pallas import tpu as pltpu
from jax.sharding import PartitionSpec as P

HEADS = 8
HEAD_DIM = 64
STEP = 5

eps = 1e-05
momentum_decay = 0.9
rate_qkv = 0.0001
rate_out = 0.01
rate_up = 0.0002
rate_down = 4e-05
rate_norm = 0.0004
neg_large = -1e30

low = jnp.bfloat16
full = jnp.float32

NN = (((1,), (0,)), ((), ()))
NT = (((1,), (1,)), ((), ()))
TN = (((0,), (0,)), ((), ()))

POWER = math.log2(math.e) * HEAD_DIM ** (-0.5)
SCALE = HEAD_DIM ** (-0.5)
GELU_C = math.sqrt(2.0 / math.pi)
GELU_A = 0.044715
LANES = 128
TILE = 16
PARTS = 4
VMEM_LIMIT = 58 * 2**20


def dot(a, b, dims):
    return lax.dot_general(a, b, dims, preferred_element_type=full)


def norm_stats(values):
    centre = values - jnp.mean(values, axis=-1, keepdims=True)
    spread = jnp.mean(centre * centre, axis=-1, keepdims=True)
    scale = lax.rsqrt(spread + eps)
    return centre * scale, scale


def norm_back(hat, scale, gain, grad):
    inner = grad * gain
    back = scale * (
        inner
        - jnp.mean(inner, axis=-1, keepdims=True)
        - hat * jnp.mean(inner * hat, axis=-1, keepdims=True)
    )
    return (
        back,
        jnp.sum(grad * hat, axis=0, keepdims=True),
        jnp.sum(grad, axis=0, keepdims=True),
    )


def norm_rows(block):
    return jnp.sum(block.astype(full), axis=0)


def gelu_both(u):
    square = u * u
    t = jnp.tanh(GELU_C * u * (1.0 + GELU_A * square))
    half = 0.5 + 0.5 * t
    slope = half + (0.5 * GELU_C) * u * (1.0 - t * t) * (1.0 + (3.0 * GELU_A) * square)
    return u * half, slope


def masks(lengths_ref, rows):
    place = lax.broadcasted_iota(jnp.int32, (rows, LANES), 0)
    lane = lax.broadcasted_iota(jnp.int32, (rows, LANES), 1)
    first = lengths_ref[0]
    second = first + lengths_ref[1]
    third = second + lengths_ref[2]
    item = (
        (place >= first).astype(jnp.int32)
        + (place >= second).astype(jnp.int32)
        + (place >= third).astype(jnp.int32)
    )
    own = item == lane
    query = jnp.where(own, neg_large, 0.0).astype(low)
    key = jnp.where(own | (lane > 3), 0.0, 1.0).astype(low)
    return query, key


def added(refs, rows=slice(None)):
    total = refs[0][rows].astype(full)
    for ref in refs[1:]:
        total = total + ref[rows].astype(full)
    return total


def put_in_order(order_ref, weight_ref, ordered, per, pieces):
    for b in range(weight_ref.shape[0]):
        place = order_ref[b]
        for j in range(pieces):
            ordered[j, b * per : (b + 1) * per, :] = weight_ref[place, j * per : (j + 1) * per, :]


def put_blocks(order_ref, first, grad_refs, rows, values):
    if len(grad_refs) == 1:
        for b in range(values.shape[0]):
            grad_refs[0][order_ref[first + b], rows, :] = values[b]
        return
    half = grad_refs[0].shape[0]
    for b in range(0, values.shape[0], 2):
        places = order_ref[first + b], order_ref[first + b + 1]
        even = places[0] < half
        place = jnp.where(even, places[0], places[1])
        grad_refs[0][place, rows, :] = jnp.where(even, values[b], values[b + 1])
        grad_refs[1][place, rows, :] = jnp.where(even, values[b + 1], values[b])


def put_everywhere(grad_refs, rows, values):
    for ref in grad_refs:
        ref[:, rows, :] = jnp.broadcast_to(values[None], (ref.shape[0],) + values.shape)


def grad_shapes(devices, rows, width, split):
    if split:
        return [jax.ShapeDtypeStruct((devices // 2, rows, width), low)] * 2
    return [jax.ShapeDtypeStruct((devices, rows, width), low)]


def attend_kernel(count, per, block, *refs):
    lengths_ref, order_ref, refs = refs[0], refs[1], refs[2:]
    inputs, refs = refs[:count], refs[count:]
    weight_ref, q_ref, k_ref, v_ref, o_ref, log_ref, a_s, vt_s, qm_s, km_s, w_s = refs
    length, width = q_ref.shape
    norm_vals = norm_rows(weight_ref[:, 4 * per : 4 * per + TILE, :])
    put_in_order(order_ref, weight_ref, w_s, per, 3)

    def weight(j):
        return w_s[j]

    hat, _ = norm_stats(added(inputs))
    a_s[...] = (hat * norm_vals[0:1] + norm_vals[1:2]).astype(low)
    qm_s[...], km_s[...] = masks(lengths_ref, length)
    q_ref[...] = dot(a_s[...], weight(0), NN).astype(low)
    k_ref[...] = dot(a_s[...], weight(1), NN).astype(low)
    v_ref[...] = dot(a_s[...], weight(2), NN).astype(low)
    vt_s[...] = v_ref[...].T
    lanes = lax.broadcasted_iota(jnp.int32, (1, LANES), 1)
    zero = jnp.zeros((), low)

    jobs = [
        (p, h, b)
        for p in range(width // LANES)
        for h in range(2)
        for b in range(length // block)
    ]

    def scores(job):
        p, h, b = job
        cols = slice(p * LANES, (p + 1) * LANES)
        rows = slice(b * block, (b + 1) * block)
        queries = jnp.where(lanes // HEAD_DIM == h, q_ref[rows, cols], zero)
        return dot(
            jnp.concatenate([k_ref[:, cols], km_s[...]], axis=1),
            jnp.concatenate([queries, qm_s[rows, :]], axis=1),
            NT,
        )

    ahead = scores(jobs[0])
    for i, (p, h, b) in enumerate(jobs):
        s = ahead
        if i + 1 < len(jobs):
            ahead = scores(jobs[i + 1])
        head = 2 * p + h
        rows = slice(head * HEAD_DIM, (head + 1) * HEAD_DIM)
        cols = slice(b * block, (b + 1) * block)
        top = jnp.max(s, axis=0, keepdims=True) * POWER
        raised = jnp.exp2(s * POWER - top)
        total = jnp.sum(raised, axis=0, keepdims=True)
        mixed = dot(vt_s[rows, :], raised.astype(low), NN)
        o_ref[rows, cols] = (mixed * (1.0 / total)).astype(low)
        log_ref[head : head + 1, cols] = top + jnp.log2(total)


def attend(lengths, order, inputs, weights, per):
    length, width = inputs[0].shape
    shape = jax.ShapeDtypeStruct
    flops = 2 * length * width * width * 3 + 8 * length * length * width
    return pl.pallas_call(
        functools.partial(attend_kernel, len(inputs), per, min(512, length)),
        out_shape=(
            shape((length, width), low),
            shape((length, width), low),
            shape((length, width), low),
            shape((width, length), low),
            shape((HEADS, length), full),
        ),
        in_specs=[pl.BlockSpec(memory_space=pltpu.SMEM)] * 2
        + [pl.BlockSpec(memory_space=pltpu.VMEM)] * (len(inputs) + 1),
        out_specs=[pl.BlockSpec(memory_space=pltpu.VMEM)] * 5,
        scratch_shapes=[
            pltpu.VMEM((length, width), low),
            pltpu.VMEM((width, length), low),
            pltpu.VMEM((length, LANES), low),
            pltpu.VMEM((length, LANES), low),
            pltpu.VMEM((3, width, width), low),
        ],
        compiler_params=pltpu.CompilerParams(vmem_limit_bytes=VMEM_LIMIT),
        cost_estimate=pl.CostEstimate(
            flops=2 * flops, bytes_accessed=8 * 2**20, transcendentals=HEADS * length * length
        ),
        name="attend",
    )(lengths, order, *inputs, weights)


def heads_back(refs, scratch, pairs, block):
    q_ref, k_ref, v_ref, do_ref, dot_ref, log_ref, sum_ref, dqt_ref, dkt_ref, dvt_ref = refs
    qt_s, kt_s, dk_s, dv_s, qm_s, km_s = scratch
    length = q_ref.shape[0]
    blocks = length // block
    qt_s[...] = q_ref[...].T
    kt_s[...] = k_ref[...].T
    lanes = lax.broadcasted_iota(jnp.int32, (1, LANES), 1)
    zero = jnp.zeros((), low)

    def pair(p, carry):
        off = pl.multiple_of(p * LANES, LANES)
        wide = pl.ds(off, LANES)
        keys = jnp.concatenate([k_ref[:, wide], km_s[...]], axis=1)
        jobs = [(h, b) for h in range(2) for b in range(blocks)]

        def scores(job):
            h, b = job
            rows = slice(b * block, (b + 1) * block)
            keep = lanes // HEAD_DIM == h
            queries = jnp.where(keep, q_ref[rows, wide], zero)
            outer = jnp.where(keep, do_ref[rows, wide], zero)
            return (
                dot(keys, jnp.concatenate([queries, qm_s[rows, :]], axis=1), NT),
                dot(v_ref[:, wide], outer, NT),
            )

        ahead = scores(jobs[0])
        for i, (h, b) in enumerate(jobs):
            s, dp = ahead
            if i + 1 < len(jobs):
                ahead = scores(jobs[i + 1])
            rows = pl.ds(pl.multiple_of(off + h * HEAD_DIM, HEAD_DIM), HEAD_DIM)
            cols = slice(b * block, (b + 1) * block)
            head = pl.ds(2 * (pairs[0] + p) + h, 1)
            prob = jnp.exp2(s * POWER - log_ref[head, cols])
            ds = (prob * (dp - sum_ref[head, cols])).astype(low)
            prob = prob.astype(low)
            dv = dot(dot_ref[rows, cols], prob, NT)
            dk = dot(qt_s[rows, cols], ds, NT)
            dqt_ref[rows, cols] = (dot(kt_s[rows, :], ds, NN) * SCALE).astype(low)
            if b > 0:
                dv = dv_s[...] + dv
                dk = dk_s[...] + dk
            if b < blocks - 1:
                dv_s[...] = dv
                dk_s[...] = dk
            else:
                dvt_ref[rows, :] = dv.astype(low)
                dkt_ref[rows, :] = (dk * SCALE).astype(low)
        return carry

    lax.fori_loop(0, pairs[1] - pairs[0], pair, 0)


def attend_back_kernel(count, per, block, pairs, last, *refs):
    lengths_ref, refs = refs[0], refs[1:]
    heads, refs = refs[:7], refs[7:]
    if last:
        before = 3 if pairs[0] > 0 else 0
        order_ref, refs = refs[0], refs[1:]
        earlier, refs = refs[:before], refs[before:]
        inputs, refs = refs[:count], refs[count:]
        weight_ref, dx2_ref, outg_ref, norms_ref, dx_ref, dxl_ref, *refs = refs
        grads_at = len(refs) - 10
        grad_refs, grads_s, scratch = refs[:grads_at], refs[grads_at : grads_at + 3], refs[grads_at + 3 :]
        *scratch, w_s = scratch
    else:
        grads_s, scratch = refs[:3], refs[3:]
    length = heads[0].shape[0]
    scratch[4][...], scratch[5][...] = masks(lengths_ref, length)
    heads_back(heads + tuple(grads_s), scratch, pairs, block)
    if not last:
        return
    width = w_s.shape[1]
    put_in_order(order_ref, weight_ref, w_s, per, 3)
    norm_vals = norm_rows(weight_ref[:, 4 * per : 4 * per + TILE, :])
    hat, scale = norm_stats(added(inputs))
    a = (hat * norm_vals[0:1] + norm_vals[1:2]).astype(low)
    da = jnp.zeros((length, width), full)
    for j in range(3):
        if before:
            grads = jnp.concatenate([earlier[j][...].T, grads_s[j][...].T], axis=1)
        else:
            grads = grads_s[j][...].T
        da = da + dot(grads, w_s[j], NT)
        put_blocks(
            order_ref,
            0,
            grad_refs,
            slice(j * per, (j + 1) * per),
            dot(a, grads, TN).astype(low).reshape(width // per, per, width),
        )
    back, gain, shift = norm_back(hat, scale, norm_vals[0:1], da)
    dx = dx2_ref[...] + back
    dx_ref[...] = dx
    dxl_ref[...] = dx.astype(low)
    put_blocks(
        order_ref,
        0,
        grad_refs,
        slice(3 * per, 4 * per),
        outg_ref[...].reshape(width // per, per, width),
    )
    tail = jnp.concatenate(
        [gain, shift, norms_ref[...], jnp.zeros((TILE - 4, width), full)], axis=0
    )
    put_everywhere(grad_refs, slice(4 * per, 4 * per + TILE), tail.astype(low))


def head_specs(length, pairs):
    wide = (pairs[1] - pairs[0]) * LANES
    at = pairs[0] * LANES // wide
    assert at * wide == pairs[0] * LANES
    columns = pl.BlockSpec((length, wide), lambda i: (0, at))
    return [columns] * 4 + [pl.BlockSpec((wide, length), lambda i: (at, 0))] + [
        pl.BlockSpec(memory_space=pltpu.VMEM)] * 2


def head_scratch(length, pairs):
    wide = (pairs[1] - pairs[0]) * LANES
    return (
        [pltpu.VMEM((wide, length), low)] * 2
        + [pltpu.VMEM((HEAD_DIM, length), full)] * 2
        + [pltpu.VMEM((length, LANES), low)] * 2
    )


def attend_back(
    lengths, order, inputs, weights, kept, outer, dx2, others, per, pairs, earlier, split
):
    q, k, v, _, logs = kept
    outer, outer_t, sums = outer
    length, width = q.shape
    shape = jax.ShapeDtypeStruct
    count = pairs[1] - pairs[0]
    wide = count * LANES
    devices = weights.shape[0]
    last = earlier is not None
    flops = 20 * length * length * wide + (12 * length * width * width if last else 0)
    whole = pl.BlockSpec(memory_space=pltpu.VMEM)
    smem = pl.BlockSpec(memory_space=pltpu.SMEM)
    arrays = [lengths, q, k, v, outer, outer_t, logs, sums]
    specs = [smem] + head_specs(length, pairs)
    transposed = [shape((wide, length), low)] * 3
    scratch = head_scratch(length, pairs)
    if last:
        arrays += [order, *earlier, *inputs, weights, dx2, *others]
        specs += [smem] + [whole] * (len(earlier) + len(inputs) + 4)
        outs = [shape((length, width), full), shape((length, width), low)]
        outs += grad_shapes(devices, 4 * per + TILE, width, split)
        scratch = [pltpu.VMEM((wide, length), low)] * 3 + scratch
        scratch += [pltpu.VMEM((3, width, width), low)]
    else:
        outs = transposed
    return pl.pallas_call(
        functools.partial(
            attend_back_kernel, len(inputs), per, min(256, length), pairs, last
        ),
        grid=(1,),
        out_shape=tuple(outs),
        in_specs=specs,
        out_specs=[whole] * len(outs),
        scratch_shapes=scratch,
        compiler_params=pltpu.CompilerParams(vmem_limit_bytes=VMEM_LIMIT),
        cost_estimate=pl.CostEstimate(
            flops=2 * flops,
            bytes_accessed=16 * 2**20,
            transcendentals=2 * count * length * length,
        ),
        name="attend_back" if last else "attend_back_part",
    )(*arrays)


def middle_start(inputs, o_ref, out, norm_ref):
    norm_vals = norm_rows(norm_ref[...])
    x2 = added(inputs) + dot(o_ref[...], out, TN)
    hat, _ = norm_stats(x2)
    return x2, (hat * norm_vals[2:3] + norm_vals[3:4]).astype(low)


def ffn_forward_kernel(count, block, *refs):
    order_ref, refs = refs[0], refs[1:]
    inputs, refs = refs[:count], refs[count:]
    (
        o_ref, norm_ref, out_ref, up_ref, down_ref,
        x2_ref, h_ref, slope_ref, y_ref,
        c_s, acc_s, out_s,
    ) = refs
    length, width = x2_ref.shape
    j = pl.program_id(0)

    @pl.when(j == 0)
    def _():
        put_in_order(order_ref, out_ref, out_s, out_ref.shape[1], 1)
        x2, c = middle_start(inputs, o_ref, out_s[0], norm_ref)
        x2_ref[...] = x2
        acc_s[...] = x2
        c_s[...] = c

    up = up_ref[...].reshape(width, width)
    down = down_ref[...].reshape(width, width)
    spans = [slice(i, i + block) for i in range(0, length, block)]
    ahead = dot(c_s[spans[0], :], up, NN)
    for i, rows in enumerate(spans):
        u = ahead
        if i + 1 < len(spans):
            ahead = dot(c_s[spans[i + 1], :], up, NN)
        h, slope = gelu_both(u)
        h = h.astype(low)
        h_ref[rows, :] = h
        slope_ref[rows, :] = slope.astype(low)
        acc_s[rows, :] += dot(h, down, NN)

    @pl.when(j == pl.num_programs(0) - 1)
    def _():
        y_ref[...] = acc_s[...].astype(low)


def piece_specs(devices, per, width):
    return [
        pl.BlockSpec((devices, per, width), lambda j: (0, 3, 0)),
        pl.BlockSpec((devices, per, width), lambda j: (0, j, 0)),
        pl.BlockSpec((devices // PARTS, 4 * per, width), lambda j: (j, 1, 0)),
    ]


def constant(*dims):
    return pl.BlockSpec(dims, lambda j: (0,) * len(dims))


def norm_spec(devices, per, width):
    return pl.BlockSpec((devices, TILE, width), lambda j: (0, 4 * per // TILE, 0))


def ffn_forward(order, inputs, mixed, first, second, per):
    length, width = inputs[0].shape
    devices = first.shape[0]
    shape = jax.ShapeDtypeStruct
    hidden = PARTS * width
    return pl.pallas_call(
        functools.partial(ffn_forward_kernel, len(inputs), min(256, length)),
        grid=(PARTS,),
        out_shape=(
            shape((length, width), full),
            shape((length, hidden), low),
            shape((length, hidden), low),
            shape((length, width), low),
        ),
        in_specs=[pl.BlockSpec(memory_space=pltpu.SMEM)]
        + [constant(length, width)] * len(inputs)
        + [constant(width, length), norm_spec(devices, per, width)]
        + piece_specs(devices, per, width),
        out_specs=[
            constant(length, width),
            pl.BlockSpec((length, width), lambda j: (0, j)),
            pl.BlockSpec((length, width), lambda j: (0, j)),
            constant(length, width),
        ],
        scratch_shapes=[
            pltpu.VMEM((length, width), low),
            pltpu.VMEM((length, width), full),
            pltpu.VMEM((1, width, width), low),
        ],
        compiler_params=pltpu.CompilerParams(vmem_limit_bytes=VMEM_LIMIT),
        cost_estimate=pl.CostEstimate(
            flops=2 * length * width * width * 9,
            bytes_accessed=16 * 2**20,
            transcendentals=length * hidden,
        ),
        name="ffn_forward",
    )(order, *inputs, mixed, first, first, second, second)


def ffn_back_kernel(count, fused, block, *refs):
    order_ref, refs = refs[0], refs[1:]
    if fused:
        inputs, refs = refs[:count], refs[count:]
        (
            o_ref, cot_ref, norm_ref, out_ref, up_ref, down_ref,
            y_ref, dx2_ref, do_ref, dot_ref, sum_ref, outg_ref, norms_ref, grad_ref,
            out_s, c_s, dc_s, h_s, du_s, x2_ref, acc_s,
        ) = refs
        dyb_ref = cot_ref
    else:
        (
            x2_ref, h_ref, slope_ref, later_ref,
            o_ref, cot_ref, norm_ref, out_ref, up_ref, down_ref,
            dx2_ref, do_ref, dot_ref, sum_ref, outg_ref, norms_ref, grad_ref,
            out_s, c_s, dc_s, h_s, du_s, dyb_ref,
        ) = refs
        h_s = h_ref
    length, width = dx2_ref.shape
    devices, per, _ = out_ref.shape
    j = pl.program_id(0)

    def cot(rows):
        dy = cot_ref[rows, :].astype(full)
        if not fused:
            dy = dy + later_ref[rows, :].astype(low).astype(full)
        return dy

    everything = slice(0, length)

    @pl.when(j == 0)
    def _():
        put_in_order(order_ref, out_ref, out_s, per, 1)
        if fused:
            x2, c = middle_start(inputs, o_ref, out_s[0], norm_ref)
            x2_ref[...] = x2
            acc_s[...] = x2
        else:
            norm_vals = norm_rows(norm_ref[...])
            hat, _ = norm_stats(x2_ref[...])
            c = (hat * norm_vals[2:3] + norm_vals[3:4]).astype(low)
            dyb_ref[...] = cot(everything).astype(low)
        c_s[...] = c
        dc_s[...] = jnp.zeros((length, width), full)

    up = up_ref[...].reshape(width, width)
    down = down_ref[...].reshape(width, width)
    spans = [slice(i, i + block) for i in range(0, length, block)]

    def products(rows):
        dh = dot(dyb_ref[rows, :], down, NT)
        return (dot(c_s[rows, :], up, NN) if fused else None), dh

    ahead = products(spans[0])
    for i, rows in enumerate(spans):
        u, dh = ahead
        if i + 1 < len(spans):
            ahead = products(spans[i + 1])
        if fused:
            h, slope = gelu_both(u)
            h = h.astype(low)
            h_s[rows, :] = h
            acc_s[rows, :] += dot(h, down, NN)
        else:
            slope = slope_ref[rows, :].astype(full)
        du = (slope * dh).astype(low)
        du_s[rows, :] = du
        dc_s[rows, :] += dot(du, up, NT)
    grad_ref[pl.ds(j * (devices // PARTS), devices // PARTS), 4 * per : 8 * per, :] = (
        dot(h_s[...], dyb_ref[...], TN).astype(low).reshape(devices // PARTS, 4 * per, width)
    )
    grad_ref[:, pl.ds(pl.multiple_of(j * per, TILE), per), :] = (
        dot(c_s[...], du_s[...], TN).astype(low).reshape(devices, per, width)
    )

    @pl.when(j == pl.num_programs(0) - 1)
    def _():
        if fused:
            y_ref[...] = acc_s[...].astype(low)
        norm_vals = norm_rows(norm_ref[...])
        hat, scale = norm_stats(x2_ref[...])
        back, gain, shift = norm_back(hat, scale, norm_vals[2:3], dc_s[...])
        dx2 = cot(everything) + back
        dx2_ref[...] = dx2
        dab = dx2.astype(low)
        out = out_s[0]
        outg_ref[...] = dot(o_ref[...], dab, NN).astype(low)
        do_ref[...] = dot(dab, out, NT).astype(low)
        outer = dot(out, dab, NT).astype(low)
        dot_ref[...] = outer
        product = outer.astype(full) * o_ref[...].astype(full)
        sum_ref[...] = jnp.sum(product.reshape(HEADS, HEAD_DIM, length), axis=1)
        norms_ref[0:1, :] = gain
        norms_ref[1:2, :] = shift


def ffn_back(order, inputs, kept, mixed, cot, first, second, per):
    fused = kept is None
    length, width = cot.shape
    devices = first.shape[0]
    shape = jax.ShapeDtypeStruct
    hidden = PARTS * width
    column = pl.BlockSpec((length, width), lambda j: (0, j))
    ahead = [constant(length, width)] * len(inputs) if fused else [
        constant(length, width), column, column, constant(length, width)]
    outs = [
        (shape((length, width), full), constant(length, width)),
        (shape((length, width), low), constant(length, width)),
        (shape((width, length), low), constant(width, length)),
        (shape((HEADS, length), full), constant(HEADS, length)),
        (shape((width, width), low), constant(width, width)),
        (shape((2, width), full), constant(2, width)),
        (shape(second.shape, low), constant(*second.shape)),
    ]
    scratch = [
        pltpu.VMEM((1, width, width), low),
        pltpu.VMEM((length, width), low),
        pltpu.VMEM((length, width), full),
        pltpu.VMEM((length, width) if fused else (TILE, LANES), low),
        pltpu.VMEM((length, width), low),
    ]
    if fused:
        outs = [(shape((length, width), low), constant(length, width))] + outs
        scratch += [pltpu.VMEM((length, width), full)] * 2
    else:
        scratch += [pltpu.VMEM((length, width), low)]
    return pl.pallas_call(
        functools.partial(ffn_back_kernel, len(inputs), fused, min(256, length)),
        grid=(PARTS,),
        out_shape=tuple(o[0] for o in outs),
        in_specs=[pl.BlockSpec(memory_space=pltpu.SMEM)]
        + ahead
        + [constant(width, length), constant(length, width), norm_spec(devices, per, width)]
        + piece_specs(devices, per, width),
        out_specs=tuple(o[1] for o in outs),
        scratch_shapes=scratch,
        compiler_params=pltpu.CompilerParams(vmem_limit_bytes=VMEM_LIMIT),
        cost_estimate=pl.CostEstimate(
            flops=2 * length * width * width * (28 if fused else 19),
            bytes_accessed=24 * 2**20,
            transcendentals=length * hidden if fused else 0,
        ),
        name="ffn_both" if fused else "ffn_back",
    )(order, *(inputs if fused else kept), mixed, cot, first, first, second, second)


def across(block, bit):
    devices = lax.axis_size("batch")
    return lax.ppermute(block, "batch", [(i, i ^ bit) for i in range(devices)])


def pick(blocks, index, axis=0):
    return lax.dynamic_index_in_dim(blocks, index, axis, keepdims=False)


def stages():
    return list(range(lax.axis_size("batch").bit_length() - 1))[::-1]


def places(device):
    flips = device ^ lax.axis_index("batch")
    place, weight = jnp.zeros_like(device), 1
    for bit in stages():
        place = place + ((flips >> bit) & 1) * weight
        weight *= 2
    return place


def flipped(blocks, axis, bit):
    halves = [lax.index_in_dim(blocks, i, axis) for i in range(2)]
    is_set = (lax.axis_index("batch") >> bit) & 1 == 1
    return jnp.where(is_set, jnp.concatenate(halves[::-1], axis), blocks)


def by_device(blocks):
    filled = stages()
    bits = len(filled)
    rest = tuple(range(bits, bits + blocks.ndim - 1))
    shape = blocks.shape
    blocks = blocks.reshape((2,) * bits + shape[1:])
    blocks = blocks.transpose(
        tuple(bits - 1 - filled.index(b) for b in range(bits - 1, -1, -1)) + rest
    )
    for b in range(bits):
        blocks = flipped(blocks, bits - 1 - b, b)
    return blocks.reshape(shape)


def by_place(blocks):
    filled = stages()
    bits = len(filled)
    rest = tuple(range(bits, bits + blocks.ndim - 1))
    shape = blocks.shape
    blocks = blocks.reshape((2,) * bits + shape[1:])
    for b in range(bits):
        blocks = flipped(blocks, bits - 1 - b, b)
    blocks = blocks.transpose(tuple(bits - 1 - b for b in filled[::-1]) + rest)
    return blocks.reshape(shape)


def tie(value, *after):
    return lax.optimization_barrier((value,) + after)[0]


def joined(held, received):
    return jnp.concatenate([held, received], axis=0)


def halves(blocks):
    count = blocks.shape[0] // 2
    return blocks[:count], blocks[count:]


def plus(mine, received):
    return (mine.astype(full) + received.astype(full)).astype(low)


def widen(gathered, sizes, times):
    if times == 1:
        return gathered
    devices, _, width = gathered.shape
    grouped = gathered.reshape(devices // times, times, -1, width)
    parts, at = [], 0
    for size in sizes:
        parts.append(
            grouped[:, :, at : at + size].reshape(devices // times, times * size, width)
        )
        at += size
    return jnp.concatenate(parts, axis=1)


def narrow(grads, sizes, times):
    if times == 1:
        return grads
    groups, _, width = grads.shape
    parts, at = [], 0
    for size in sizes:
        parts.append(
            grads[:, at : at + times * size].reshape(groups * times, size, width)
        )
        at += times * size
    rest = grads[:, at:]
    parts.append(jnp.repeat(rest, times, axis=0))
    return jnp.concatenate(parts, axis=1)


def update(gradient, weight, momentum, average, step_rate):
    new_momentum = momentum_decay * momentum + gradient
    new_weight = weight - step_rate * (gradient + momentum_decay * new_momentum)
    new_average = average + (new_weight - average) / (STEP + 1.0)
    return (gradient, new_momentum, new_weight, new_average)


def shards(
    tokens,
    cotangent,
    lengths,
    qkv_weight,
    qkv_momentum,
    qkv_average,
    out_weight,
    out_momentum,
    out_average,
    up_weight,
    up_momentum,
    up_average,
    down_weight,
    down_momentum,
    down_average,
    norm_params,
    norm_momentum,
    norm_average,
):
    section = lax.axis_index("section")
    here = lax.axis_index("batch")
    width = tokens.shape[2]
    length = tokens.shape[1] // lengths.shape[0]
    assert lengths.shape[0] == lax.axis_size("section") == 2
    own_rows = out_weight.shape[1]
    times = max(1, TILE // own_rows)
    per = own_rows * times
    first_sizes = (own_rows,) * 4
    second_sizes = (own_rows,) * PARTS + (PARTS * own_rows,)

    def swap(block):
        return lax.ppermute(block, "section", [(0, 1), (1, 0)])

    def sorted_pair(mine, other):
        is_first = section == 0
        return jnp.where(is_first, mine, other), jnp.where(is_first, other, mine)

    lengths_mine = pick(lengths, section)
    norm_table = lax.dynamic_update_slice(
        jnp.zeros((TILE, width), low),
        norm_params[0].astype(low),
        (0, here * norm_params.shape[2]),
    )
    pack_first = jnp.concatenate(
        [
            qkv_weight[0].astype(low).reshape(-1, width),
            out_weight[0].astype(low),
            norm_table,
        ],
        axis=0,
    )
    up_low = up_weight[0].astype(low).reshape(own_rows, PARTS, width)
    pack_second = jnp.concatenate(
        [
            up_low.transpose(1, 0, 2).reshape(-1, width),
            down_weight[0].astype(low),
        ],
        axis=0,
    )
    order = places(jnp.arange(lax.axis_size("batch"), dtype=jnp.int32))
    steps = stages()
    split = times == 1

    both_packs = jnp.concatenate([pack_first, pack_second], axis=0)
    received = swap(both_packs)
    first_rows = pack_first.shape[0]
    pair_second = sorted_pair(pack_second, received[first_rows:])
    piece_e, piece_d = sorted_pair(pack_first, received[:first_rows])
    token_rows = tokens[0].reshape(2, length, width)
    cot_rows = cotangent[0].reshape(2, length, width)
    token_other = swap(tie(pick(token_rows, 1 - section), received))
    cot_other = swap(tie(pick(cot_rows, 1 - section), token_other))

    def gathered(held, bits):
        flips = [sum(((d >> i) & 1) << b for i, b in enumerate(bits)) for d in range(1, 1 << len(bits))]
        return [across(held, flip) for flip in flips]

    high = steps[:-2]
    wide = [high[i : i + 2] for i in range(0, len(high), 2)]
    held_e = piece_e[None]
    for bits in wide:
        held_e = jnp.concatenate([held_e] + gathered(held_e, bits))
    held_d, coming = tie(piece_d[None], held_e), []
    for bits in wide:
        held_d = jnp.concatenate([held_d] + coming)
        coming = gathered(held_d, bits)
    for bit in steps[-2:]:
        held_e = joined(held_e, across(held_e, 1 << bit))

    def whole_first(held):
        if times == 1:
            return held
        held = by_device(held)
        body = widen(held[:, : 4 * own_rows], first_sizes, times)
        table = held[:, 4 * own_rows :].reshape(-1, times, TILE, width)
        return jnp.concatenate([body, jnp.sum(table, axis=1)], axis=1)

    def whole_second(piece):
        gathered = lax.all_gather(piece, "batch", axis=0, tiled=False)
        return widen(gathered, second_sizes, times)

    second = [whole_second(piece) for piece in pair_second]
    natural = jnp.arange(second[0].shape[0], dtype=jnp.int32)
    placed = order if split else natural

    encoder_in = jnp.where(section == 0, pick(token_rows, section), token_other)
    first_e = whole_first(held_e)
    kept_e = attend(lengths_mine, placed, [encoder_in], first_e, per)
    held_d = jnp.concatenate([held_d] + [tie(b, kept_e[4]) for b in coming])
    coming = across(held_d, 1 << steps[-2])
    x2_e, hidden_e, slope_e, encoded = ffn_forward(
        placed, [encoder_in], tie(kept_e[3], held_d), first_e, second[0], per
    )
    denoiser_in = jnp.where(
        section == 0, tie(token_other, kept_e[4]), pick(token_rows, section)
    )
    held_d = joined(held_d, tie(coming, encoded))
    first_d = whole_first(joined(held_d, across(held_d, 1 << steps[-1])))
    inputs_d = [denoiser_in, encoded]
    kept_d = attend(lengths_mine, placed, inputs_d, first_d, per)
    encoder_cot, denoiser_cot = sorted_pair(pick(cot_rows, section), cot_other)
    decoded, dx2_d, *rest_d = ffn_back(
        placed, inputs_d, None, kept_d[3], denoiser_cot, first_d, second[1], per
    )

    def reduced(grads):
        return lax.psum_scatter(
            narrow(grads, second_sizes, times).reshape(-1, width),
            "batch",
            scatter_dimension=0,
            tiled=True,
        )

    def cores(grads):
        if split:
            return grads
        return halves(by_place(narrow(grads[0], first_sizes, times)))

    back = [1 << bit for bit in steps[::-1]]
    second_d = reduced(rest_d[5])
    all_pairs = (0, width // LANES)
    dx_d, dx_low_d, *grads_first_d = attend_back(
        lengths_mine, placed, inputs_d, first_d, kept_d, rest_d[:3], dx2_d, rest_d[3:5], per,
        all_pairs, (), split,
    )
    mine_d, other = cores(grads_first_d)
    coming_d = across(other, back[0])
    dx2_e, *rest_e = ffn_back(
        placed, [], (x2_e, hidden_e, slope_e, dx_d), kept_e[3], encoder_cot, first_e, second[0], per
    )
    second_e = reduced(rest_e[5])
    mine_d, other = halves(plus(mine_d, coming_d))
    coming_d = across(other, back[1])
    some = all_pairs[1] // 2
    earlier = attend_back(
        lengths_mine, placed, [], first_e, kept_e, [tie(rest_e[0], mine_d), *rest_e[1:3]], dx2_e, (),
        per, (0, some), None, split,
    )
    mine_d, other = halves(plus(mine_d, tie(coming_d, earlier[0])))
    coming_d = across(other, back[2])
    second_d, dx2_e, *earlier = lax.optimization_barrier((second_d, dx2_e, *earlier))
    dx_e, dx_low_e, *grads_first_e = attend_back(
        lengths_mine, placed, [encoder_in], first_e, kept_e, rest_e[:3], tie(dx2_e, mine_d),
        rest_e[3:5], per, (some, all_pairs[1]), tuple(earlier), split,
    )
    mine_e, other = cores(grads_first_e)
    coming_e = across(other, back[0])

    coming_d, bits_d = tie(coming_d, dx_low_e), back[3:]
    for bit in back[1:]:
        mine_e = plus(mine_e, coming_e)
        if coming_d is not None:
            mine_d = plus(mine_d, coming_d)
            coming_d = None
        if bits_d:
            mine_e, mine_d = lax.optimization_barrier((mine_e, mine_d))
            mine_d, other = halves(mine_d)
            coming_d = across(other, bits_d.pop(0))
        mine_e, other = halves(mine_e)
        coming_e = across(other, bit)
    if coming_d is not None:
        mine_d = plus(mine_d, coming_d)
    first_e, first_d = plus(mine_e, coming_e)[0], mine_d[0]

    def summed(of_first, of_second):
        is_first = section == 0
        mine = jnp.where(is_first, of_first.astype(full), of_second.astype(full))
        other = swap(jnp.where(is_first, of_second.astype(low), of_first.astype(low)))
        return mine + other.astype(full)

    total_first = summed(first_e, first_d)

    def both(encoder_part, denoiser_part, received):
        mine = jnp.where(section == 0, encoder_part, denoiser_part)
        received = received.astype(mine.dtype)
        return jnp.where(
            section == 0, jnp.stack([mine, received]), jnp.stack([received, mine])
        ).reshape(1, 2 * length, width)

    activations = both(
        encoded, decoded, tie(swap(jnp.where(section == 0, decoded, encoded)), dx_low_e)
    )
    input_grad = both(
        dx_e, dx_d, tie(swap(jnp.where(section == 0, dx_low_d, dx_low_e)), total_first)
    )
    total_second = summed(tie(second_e, total_first, input_grad, activations), second_d)

    qkv_grad = total_first[: 3 * own_rows].reshape(qkv_weight.shape)
    up_grad = total_second[: 4 * own_rows].reshape(PARTS, own_rows, width)
    up_grad = up_grad.transpose(1, 0, 2).reshape(up_weight.shape)
    down_grad = total_second[4 * own_rows : 8 * own_rows][None]
    out_grad = total_first[3 * own_rows : 4 * own_rows][None]
    norm_all = total_first[4 * own_rows : 4 * own_rows + 4]
    own_features = norm_params.shape[2]
    norm_grad = lax.dynamic_slice(
        norm_all, (0, here * own_features), (4, own_features)
    )[None]
    qkv_new = update(qkv_grad, qkv_weight, qkv_momentum, qkv_average, rate_qkv)
    out_new = update(out_grad, out_weight, out_momentum, out_average, rate_out)
    up_new = update(up_grad, up_weight, up_momentum, up_average, rate_up)
    down_new = update(down_grad, down_weight, down_momentum, down_average, rate_down)
    norm_new = update(norm_grad, norm_params, norm_momentum, norm_average, rate_norm)
    return (
        activations,
        input_grad,
        *qkv_new,
        *out_new,
        *up_new,
        *down_new,
        *norm_new,
        norm_grad[:, 3],
    )


def solution(mesh):
    rows = P("section", "batch", None)
    deep = P("section", None, "batch", None)
    features = P("section", None, "batch")
    return jax.shard_map(
        shards,
        mesh=mesh,
        in_specs=(rows, rows, P("batch", None))
        + (deep,) * 3
        + (rows,) * 9
        + (features,) * 3,
        out_specs=(rows, rows)
        + (deep,) * 4
        + (rows,) * 12
        + (features,) * 4
        + (P("section", "batch"),),
        check_vma=False,
    )
```

```python
import functools
import math

import jax
import jax.numpy as jnp
from jax import lax
from jax.experimental import pallas as pl
from jax.experimental.pallas import tpu as pltpu
from jax.sharding import PartitionSpec as P

HEADS = 8
HEAD_DIM = 64
STEP = 5

eps = 1e-05
momentum_decay = 0.9
rate_qkv = 0.0001
rate_out = 0.01
rate_up = 0.0002
rate_down = 4e-05
rate_norm = 0.0004
neg_large = -1e30

low = jnp.bfloat16
full = jnp.float32

NN = (((1,), (0,)), ((), ()))
NT = (((1,), (1,)), ((), ()))
TN = (((0,), (0,)), ((), ()))

POWER = math.log2(math.e) * HEAD_DIM ** (-0.5)
SCALE = HEAD_DIM ** (-0.5)
GELU_C = math.sqrt(2.0 / math.pi)
GELU_A = 0.044715
LANES = 128
TILE = 16
PARTS = 4
VMEM_LIMIT = 58 * 2**20


def dot(a, b, dims):
    return lax.dot_general(a, b, dims, preferred_element_type=full)


def norm_stats(values):
    centre = values - jnp.mean(values, axis=-1, keepdims=True)
    spread = jnp.mean(centre * centre, axis=-1, keepdims=True)
    scale = lax.rsqrt(spread + eps)
    return centre * scale, scale


def norm_back(hat, scale, gain, grad):
    inner = grad * gain
    back = scale * (
        inner
        - jnp.mean(inner, axis=-1, keepdims=True)
        - hat * jnp.mean(inner * hat, axis=-1, keepdims=True)
    )
    return (
        back,
        jnp.sum(grad * hat, axis=0, keepdims=True),
        jnp.sum(grad, axis=0, keepdims=True),
    )


def norm_rows(refs, rows=slice(None)):
    total = jnp.sum(refs[0][:, rows, :].astype(full), axis=0)
    for ref in refs[1:]:
        total = total + jnp.sum(ref[:, rows, :].astype(full), axis=0)
    return total


def gelu_both(u):
    square = u * u
    t = jnp.tanh(GELU_C * u * (1.0 + GELU_A * square))
    half = 0.5 + 0.5 * t
    slope = half + (0.5 * GELU_C) * u * (1.0 - t * t) * (1.0 + (3.0 * GELU_A) * square)
    return u * half, slope


def masks(lengths_ref, rows):
    place = lax.broadcasted_iota(jnp.int32, (rows, LANES), 0)
    lane = lax.broadcasted_iota(jnp.int32, (rows, LANES), 1)
    first = lengths_ref[0]
    second = first + lengths_ref[1]
    third = second + lengths_ref[2]
    item = (
        (place >= first).astype(jnp.int32)
        + (place >= second).astype(jnp.int32)
        + (place >= third).astype(jnp.int32)
    )
    own = item == lane
    query = jnp.where(own, neg_large, 0.0).astype(low)
    key = jnp.where(own | (lane > 3), 0.0, 1.0).astype(low)
    return query, key


def added(refs, rows=slice(None)):
    total = refs[0][rows].astype(full)
    for ref in refs[1:]:
        total = total + ref[rows].astype(full)
    return total


def put_in_order(order_ref, weight_refs, ordered, per, pieces):
    def put(b, j, rows):
        ordered[j, b * per : (b + 1) * per, :] = rows

    if len(weight_refs) == 1:
        for b in range(weight_refs[0].shape[0]):
            for j in range(pieces):
                put(b, j, weight_refs[0][order_ref[b], j * per : (j + 1) * per, :])
        return
    half = weight_refs[0].shape[0]
    for b in range(0, 2 * half, 2):
        places = order_ref[b], order_ref[b + 1]
        even = places[0] < half
        place = jnp.where(even, places[0], places[1])
        for j in range(pieces):
            own, other = (ref[place, j * per : (j + 1) * per, :] for ref in weight_refs)
            put(b, j, jnp.where(even, own, other))
            put(b + 1, j, jnp.where(even, other, own))


def put_blocks(order_ref, first, grad_refs, rows, values):
    if len(grad_refs) == 1:
        for b in range(values.shape[0]):
            grad_refs[0][order_ref[first + b], rows, :] = values[b]
        return
    half = grad_refs[0].shape[0]
    for b in range(0, values.shape[0], 2):
        places = order_ref[first + b], order_ref[first + b + 1]
        even = places[0] < half
        place = jnp.where(even, places[0], places[1])
        grad_refs[0][place, rows, :] = jnp.where(even, values[b], values[b + 1])
        grad_refs[1][place, rows, :] = jnp.where(even, values[b + 1], values[b])


def put_everywhere(grad_refs, rows, values):
    for ref in grad_refs:
        ref[:, rows, :] = jnp.broadcast_to(values[None], (ref.shape[0],) + values.shape)


def grad_shapes(devices, rows, width, split):
    if split:
        return [jax.ShapeDtypeStruct((devices // 2, rows, width), low)] * 2
    return [jax.ShapeDtypeStruct((devices, rows, width), low)]


def attend_kernel(count, parts, per, block, *refs):
    lengths_ref, order_ref, refs = refs[0], refs[1], refs[2:]
    inputs, refs = refs[:count], refs[count:]
    weight_refs, refs = refs[:parts], refs[parts:]
    q_ref, k_ref, v_ref, o_ref, log_ref, a_s, vt_s, qm_s, km_s, w_s = refs
    length, width = q_ref.shape
    norm_vals = norm_rows(weight_refs, slice(4 * per, 4 * per + TILE))
    put_in_order(order_ref, weight_refs, w_s, per, 3)

    def weight(j):
        return w_s[j]

    hat, _ = norm_stats(added(inputs))
    a_s[...] = (hat * norm_vals[0:1] + norm_vals[1:2]).astype(low)
    qm_s[...], km_s[...] = masks(lengths_ref, length)
    q_ref[...] = dot(a_s[...], weight(0), NN).astype(low)
    k_ref[...] = dot(a_s[...], weight(1), NN).astype(low)
    v_ref[...] = dot(a_s[...], weight(2), NN).astype(low)
    vt_s[...] = v_ref[...].T
    lanes = lax.broadcasted_iota(jnp.int32, (1, LANES), 1)
    zero = jnp.zeros((), low)

    jobs = [
        (p, h, b)
        for p in range(width // LANES)
        for h in range(2)
        for b in range(length // block)
    ]

    def scores(job):
        p, h, b = job
        cols = slice(p * LANES, (p + 1) * LANES)
        rows = slice(b * block, (b + 1) * block)
        queries = jnp.where(lanes // HEAD_DIM == h, q_ref[rows, cols], zero)
        return dot(
            jnp.concatenate([k_ref[:, cols], km_s[...]], axis=1),
            jnp.concatenate([queries, qm_s[rows, :]], axis=1),
            NT,
        )

    ahead = scores(jobs[0])
    for i, (p, h, b) in enumerate(jobs):
        s = ahead
        if i + 1 < len(jobs):
            ahead = scores(jobs[i + 1])
        head = 2 * p + h
        rows = slice(head * HEAD_DIM, (head + 1) * HEAD_DIM)
        cols = slice(b * block, (b + 1) * block)
        top = jnp.max(s, axis=0, keepdims=True) * POWER
        raised = jnp.exp2(s * POWER - top)
        total = jnp.sum(raised, axis=0, keepdims=True)
        mixed = dot(vt_s[rows, :], raised.astype(low), NN)
        o_ref[rows, cols] = (mixed * (1.0 / total)).astype(low)
        log_ref[head : head + 1, cols] = top + jnp.log2(total)


def attend(lengths, order, inputs, weights, per):
    length, width = inputs[0].shape
    shape = jax.ShapeDtypeStruct
    flops = 2 * length * width * width * 3 + 8 * length * length * width
    return pl.pallas_call(
        functools.partial(attend_kernel, len(inputs), len(weights), per, min(512, length)),
        out_shape=(
            shape((length, width), low),
            shape((length, width), low),
            shape((length, width), low),
            shape((width, length), low),
            shape((HEADS, length), full),
        ),
        in_specs=[pl.BlockSpec(memory_space=pltpu.SMEM)] * 2
        + [pl.BlockSpec(memory_space=pltpu.VMEM)] * (len(inputs) + len(weights)),
        out_specs=[pl.BlockSpec(memory_space=pltpu.VMEM)] * 5,
        scratch_shapes=[
            pltpu.VMEM((length, width), low),
            pltpu.VMEM((width, length), low),
            pltpu.VMEM((length, LANES), low),
            pltpu.VMEM((length, LANES), low),
            pltpu.VMEM((3, width, width), low),
        ],
        compiler_params=pltpu.CompilerParams(vmem_limit_bytes=VMEM_LIMIT),
        cost_estimate=pl.CostEstimate(
            flops=2 * flops, bytes_accessed=8 * 2**20, transcendentals=HEADS * length * length
        ),
        name="attend",
    )(lengths, order, *inputs, *weights)


def heads_back(refs, scratch, pairs, block):
    q_ref, k_ref, v_ref, do_ref, dot_ref, log_ref, sum_ref, dqt_ref, dkt_ref, dvt_ref = refs
    qt_s, kt_s, dk_s, dv_s, qm_s, km_s = scratch
    length = q_ref.shape[0]
    blocks = length // block
    qt_s[...] = q_ref[...].T
    kt_s[...] = k_ref[...].T
    lanes = lax.broadcasted_iota(jnp.int32, (1, LANES), 1)
    zero = jnp.zeros((), low)

    def pair(p, carry):
        off = pl.multiple_of(p * LANES, LANES)
        wide = pl.ds(off, LANES)
        keys = jnp.concatenate([k_ref[:, wide], km_s[...]], axis=1)
        jobs = [(h, b) for h in range(2) for b in range(blocks)]

        def scores(job):
            h, b = job
            rows = slice(b * block, (b + 1) * block)
            keep = lanes // HEAD_DIM == h
            queries = jnp.where(keep, q_ref[rows, wide], zero)
            outer = jnp.where(keep, do_ref[rows, wide], zero)
            return (
                dot(keys, jnp.concatenate([queries, qm_s[rows, :]], axis=1), NT),
                dot(v_ref[:, wide], outer, NT),
            )

        ahead = scores(jobs[0])
        for i, (h, b) in enumerate(jobs):
            s, dp = ahead
            if i + 1 < len(jobs):
                ahead = scores(jobs[i + 1])
            rows = pl.ds(pl.multiple_of(off + h * HEAD_DIM, HEAD_DIM), HEAD_DIM)
            cols = slice(b * block, (b + 1) * block)
            head = pl.ds(2 * (pairs[0] + p) + h, 1)
            prob = jnp.exp2(s * POWER - log_ref[head, cols])
            ds = (prob * (dp - sum_ref[head, cols])).astype(low)
            prob = prob.astype(low)
            dv = dot(dot_ref[rows, cols], prob, NT)
            dk = dot(qt_s[rows, cols], ds, NT)
            dqt_ref[rows, cols] = (dot(kt_s[rows, :], ds, NN) * SCALE).astype(low)
            if b > 0:
                dv = dv_s[...] + dv
                dk = dk_s[...] + dk
            if b < blocks - 1:
                dv_s[...] = dv
                dk_s[...] = dk
            else:
                dvt_ref[rows, :] = dv.astype(low)
                dkt_ref[rows, :] = (dk * SCALE).astype(low)
        return carry

    lax.fori_loop(0, pairs[1] - pairs[0], pair, 0)


def attend_back_kernel(count, parts, per, block, pairs, last, *refs):
    lengths_ref, refs = refs[0], refs[1:]
    heads, refs = refs[:7], refs[7:]
    if last:
        before = 3 if pairs[0] > 0 else 0
        order_ref, refs = refs[0], refs[1:]
        earlier, refs = refs[:before], refs[before:]
        inputs, refs = refs[:count], refs[count:]
        weight_refs, refs = refs[:parts], refs[parts:]
        dx2_ref, outg_ref, norms_ref, dx_ref, dxl_ref, *refs = refs
        grads_at = len(refs) - 10
        grad_refs, grads_s, scratch = refs[:grads_at], refs[grads_at : grads_at + 3], refs[grads_at + 3 :]
        *scratch, w_s = scratch
    else:
        grads_s, scratch = refs[:3], refs[3:]
    length = heads[0].shape[0]
    scratch[4][...], scratch[5][...] = masks(lengths_ref, length)
    heads_back(heads + tuple(grads_s), scratch, pairs, block)
    if not last:
        return
    width = w_s.shape[1]
    put_in_order(order_ref, weight_refs, w_s, per, 3)
    norm_vals = norm_rows(weight_refs, slice(4 * per, 4 * per + TILE))
    hat, scale = norm_stats(added(inputs))
    a = (hat * norm_vals[0:1] + norm_vals[1:2]).astype(low)
    da = jnp.zeros((length, width), full)
    for j in range(3):
        if before:
            grads = jnp.concatenate([earlier[j][...].T, grads_s[j][...].T], axis=1)
        else:
            grads = grads_s[j][...].T
        da = da + dot(grads, w_s[j], NT)
        put_blocks(
            order_ref,
            0,
            grad_refs,
            slice(j * per, (j + 1) * per),
            dot(a, grads, TN).astype(low).reshape(width // per, per, width),
        )
    back, gain, shift = norm_back(hat, scale, norm_vals[0:1], da)
    dx = dx2_ref[...] + back
    dx_ref[...] = dx
    dxl_ref[...] = dx.astype(low)
    put_blocks(
        order_ref,
        0,
        grad_refs,
        slice(3 * per, 4 * per),
        outg_ref[...].reshape(width // per, per, width),
    )
    tail = jnp.concatenate(
        [gain, shift, norms_ref[...], jnp.zeros((TILE - 4, width), full)], axis=0
    )
    put_everywhere(grad_refs, slice(4 * per, 4 * per + TILE), tail.astype(low))


def head_specs(length, pairs):
    wide = (pairs[1] - pairs[0]) * LANES
    at = pairs[0] * LANES // wide
    assert at * wide == pairs[0] * LANES
    columns = pl.BlockSpec((length, wide), lambda i: (0, at))
    return [columns] * 4 + [pl.BlockSpec((wide, length), lambda i: (at, 0))] + [
        pl.BlockSpec(memory_space=pltpu.VMEM)] * 2


def head_scratch(length, pairs):
    wide = (pairs[1] - pairs[0]) * LANES
    return (
        [pltpu.VMEM((wide, length), low)] * 2
        + [pltpu.VMEM((HEAD_DIM, length), full)] * 2
        + [pltpu.VMEM((length, LANES), low)] * 2
    )


def attend_back(
    lengths, order, inputs, weights, kept, outer, dx2, others, per, pairs, earlier, split
):
    q, k, v, _, logs = kept
    outer, outer_t, sums = outer
    length, width = q.shape
    shape = jax.ShapeDtypeStruct
    count = pairs[1] - pairs[0]
    wide = count * LANES
    devices = width // per
    last = earlier is not None
    flops = 20 * length * length * wide + (12 * length * width * width if last else 0)
    whole = pl.BlockSpec(memory_space=pltpu.VMEM)
    smem = pl.BlockSpec(memory_space=pltpu.SMEM)
    arrays = [lengths, q, k, v, outer, outer_t, logs, sums]
    specs = [smem] + head_specs(length, pairs)
    transposed = [shape((wide, length), low)] * 3
    scratch = head_scratch(length, pairs)
    if last:
        arrays += [order, *earlier, *inputs, *weights, dx2, *others]
        specs += [smem] + [whole] * (len(earlier) + len(inputs) + len(weights) + 3)
        outs = [shape((length, width), full), shape((length, width), low)]
        outs += grad_shapes(devices, 4 * per + TILE, width, split)
        scratch = [pltpu.VMEM((wide, length), low)] * 3 + scratch
        scratch += [pltpu.VMEM((3, width, width), low)]
    else:
        outs = transposed
    return pl.pallas_call(
        functools.partial(
            attend_back_kernel, len(inputs), len(weights), per, min(256, length), pairs, last
        ),
        grid=(1,),
        out_shape=tuple(outs),
        in_specs=specs,
        out_specs=[whole] * len(outs),
        scratch_shapes=scratch,
        compiler_params=pltpu.CompilerParams(vmem_limit_bytes=VMEM_LIMIT),
        cost_estimate=pl.CostEstimate(
            flops=2 * flops,
            bytes_accessed=16 * 2**20,
            transcendentals=2 * count * length * length,
        ),
        name="attend_back" if last else "attend_back_part",
    )(*arrays)


def middle_start(inputs, o_ref, out, norm_refs):
    norm_vals = norm_rows(norm_refs)
    x2 = added(inputs) + dot(o_ref[...], out, TN)
    hat, _ = norm_stats(x2)
    return x2, (hat * norm_vals[2:3] + norm_vals[3:4]).astype(low)


def ffn_forward_kernel(count, parts, block, *refs):
    order_ref, refs = refs[0], refs[1:]
    inputs, refs = refs[:count], refs[count:]
    norm_refs, out_refs, refs = refs[:parts], refs[parts : 2 * parts], refs[2 * parts :]
    (
        o_ref, up_ref, down_ref,
        x2_ref, h_ref, slope_ref, y_ref,
        c_s, acc_s, out_s,
    ) = refs
    length, width = x2_ref.shape
    j = pl.program_id(0)

    @pl.when(j == 0)
    def _():
        put_in_order(order_ref, out_refs, out_s, out_refs[0].shape[1], 1)
        x2, c = middle_start(inputs, o_ref, out_s[0], norm_refs)
        x2_ref[...] = x2
        acc_s[...] = x2
        c_s[...] = c

    up = up_ref[...].reshape(width, width)
    down = down_ref[...].reshape(width, width)
    spans = [slice(i, i + block) for i in range(0, length, block)]
    ahead = dot(c_s[spans[0], :], up, NN)
    for i, rows in enumerate(spans):
        u = ahead
        if i + 1 < len(spans):
            ahead = dot(c_s[spans[i + 1], :], up, NN)
        h, slope = gelu_both(u)
        h = h.astype(low)
        h_ref[rows, :] = h
        slope_ref[rows, :] = slope.astype(low)
        acc_s[rows, :] += dot(h, down, NN)

    @pl.when(j == pl.num_programs(0) - 1)
    def _():
        y_ref[...] = acc_s[...].astype(low)


def piece_specs(devices, per, width):
    return [
        pl.BlockSpec((devices, per, width), lambda j: (0, j, 0)),
        pl.BlockSpec((devices // PARTS, 4 * per, width), lambda j: (j, 1, 0)),
    ]


def first_specs(first, per):
    shapes = [array.shape for array in first]
    return [
        pl.BlockSpec((count, TILE, width), lambda j: (0, 4 * per // TILE, 0))
        for count, _, width in shapes
    ] + [
        pl.BlockSpec((count, per, width), lambda j: (0, 3, 0)) for count, _, width in shapes
    ]


def constant(*dims):
    return pl.BlockSpec(dims, lambda j: (0,) * len(dims))


def ffn_forward(order, inputs, mixed, first, second, per):
    length, width = inputs[0].shape
    devices = width // per
    shape = jax.ShapeDtypeStruct
    hidden = PARTS * width
    return pl.pallas_call(
        functools.partial(ffn_forward_kernel, len(inputs), len(first), min(256, length)),
        grid=(PARTS,),
        out_shape=(
            shape((length, width), full),
            shape((length, hidden), low),
            shape((length, hidden), low),
            shape((length, width), low),
        ),
        in_specs=[pl.BlockSpec(memory_space=pltpu.SMEM)]
        + [constant(length, width)] * len(inputs)
        + first_specs(first, per)
        + [constant(width, length)]
        + piece_specs(devices, per, width),
        out_specs=[
            constant(length, width),
            pl.BlockSpec((length, width), lambda j: (0, j)),
            pl.BlockSpec((length, width), lambda j: (0, j)),
            constant(length, width),
        ],
        scratch_shapes=[
            pltpu.VMEM((length, width), low),
            pltpu.VMEM((length, width), full),
            pltpu.VMEM((1, width, width), low),
        ],
        compiler_params=pltpu.CompilerParams(vmem_limit_bytes=VMEM_LIMIT),
        cost_estimate=pl.CostEstimate(
            flops=2 * length * width * width * 9,
            bytes_accessed=16 * 2**20,
            transcendentals=length * hidden,
        ),
        name="ffn_forward",
    )(order, *inputs, *first, *first, mixed, second, second)


def ffn_back_kernel(count, parts, per, fused, block, *refs):
    order_ref, refs = refs[0], refs[1:]
    norm_refs, out_refs, refs = refs[:parts], refs[parts : 2 * parts], refs[2 * parts :]
    if fused:
        inputs, refs = refs[:count], refs[count:]
        (
            o_ref, cot_ref, up_ref, down_ref,
            y_ref, dx2_ref, do_ref, dot_ref, sum_ref, outg_ref, norms_ref, grad_ref,
            out_s, c_s, dc_s, h_s, du_s, x2_ref, acc_s,
        ) = refs
        dyb_ref = cot_ref
    else:
        (
            x2_ref, h_ref, slope_ref, later_ref,
            o_ref, cot_ref, up_ref, down_ref,
            dx2_ref, do_ref, dot_ref, sum_ref, outg_ref, norms_ref, grad_ref,
            out_s, c_s, dc_s, h_s, du_s, dyb_ref,
        ) = refs
        h_s = h_ref
    length, width = dx2_ref.shape
    devices = width // per
    j = pl.program_id(0)

    def cot(rows):
        dy = cot_ref[rows, :].astype(full)
        if not fused:
            dy = dy + later_ref[rows, :].astype(full)
        return dy

    everything = slice(0, length)

    @pl.when(j == 0)
    def _():
        put_in_order(order_ref, out_refs, out_s, per, 1)
        if fused:
            x2, c = middle_start(inputs, o_ref, out_s[0], norm_refs)
            x2_ref[...] = x2
            acc_s[...] = x2
        else:
            norm_vals = norm_rows(norm_refs)
            hat, _ = norm_stats(x2_ref[...])
            c = (hat * norm_vals[2:3] + norm_vals[3:4]).astype(low)
            dyb_ref[...] = cot(everything).astype(low)
        c_s[...] = c
        dc_s[...] = jnp.zeros((length, width), full)

    up = up_ref[...].reshape(width, width)
    down = down_ref[...].reshape(width, width)
    spans = [slice(i, i + block) for i in range(0, length, block)]

    def products(rows):
        dh = dot(dyb_ref[rows, :], down, NT)
        return (dot(c_s[rows, :], up, NN) if fused else None), dh

    ahead = products(spans[0])
    for i, rows in enumerate(spans):
        u, dh = ahead
        if i + 1 < len(spans):
            ahead = products(spans[i + 1])
        if fused:
            h, slope = gelu_both(u)
            h = h.astype(low)
            h_s[rows, :] = h
            acc_s[rows, :] += dot(h, down, NN)
        else:
            slope = slope_ref[rows, :].astype(full)
        du = (slope * dh).astype(low)
        du_s[rows, :] = du
        dc_s[rows, :] += dot(du, up, NT)
    grad_ref[pl.ds(j * (devices // PARTS), devices // PARTS), 4 * per : 8 * per, :] = (
        dot(h_s[...], dyb_ref[...], TN).astype(low).reshape(devices // PARTS, 4 * per, width)
    )
    grad_ref[:, pl.ds(pl.multiple_of(j * per, TILE), per), :] = (
        dot(c_s[...], du_s[...], TN).astype(low).reshape(devices, per, width)
    )

    @pl.when(j == pl.num_programs(0) - 1)
    def _():
        if fused:
            y_ref[...] = acc_s[...].astype(low)
        norm_vals = norm_rows(norm_refs)
        hat, scale = norm_stats(x2_ref[...])
        back, gain, shift = norm_back(hat, scale, norm_vals[2:3], dc_s[...])
        dx2 = cot(everything) + back
        dx2_ref[...] = dx2
        dab = dx2.astype(low)
        out = out_s[0]
        outg_ref[...] = dot(o_ref[...], dab, NN).astype(low)
        do_ref[...] = dot(dab, out, NT).astype(low)
        outer = dot(out, dab, NT).astype(low)
        dot_ref[...] = outer
        product = outer.astype(full) * o_ref[...].astype(full)
        sum_ref[...] = jnp.sum(product.reshape(HEADS, HEAD_DIM, length), axis=1)
        norms_ref[0:1, :] = gain
        norms_ref[1:2, :] = shift


def ffn_back(order, inputs, kept, mixed, cot, first, second, per):
    fused = kept is None
    length, width = cot.shape
    devices = width // per
    shape = jax.ShapeDtypeStruct
    hidden = PARTS * width
    column = pl.BlockSpec((length, width), lambda j: (0, j))
    ahead = [constant(length, width)] * len(inputs) if fused else [
        constant(length, width), column, column, constant(length, width)]
    outs = [
        (shape((length, width), full), constant(length, width)),
        (shape((length, width), low), constant(length, width)),
        (shape((width, length), low), constant(width, length)),
        (shape((HEADS, length), full), constant(HEADS, length)),
        (shape((width, width), low), constant(width, width)),
        (shape((2, width), full), constant(2, width)),
        (shape(second.shape, low), constant(*second.shape)),
    ]
    scratch = [
        pltpu.VMEM((1, width, width), low),
        pltpu.VMEM((length, width), low),
        pltpu.VMEM((length, width), full),
        pltpu.VMEM((length, width) if fused else (TILE, LANES), low),
        pltpu.VMEM((length, width), low),
    ]
    if fused:
        outs = [(shape((length, width), low), constant(length, width))] + outs
        scratch += [pltpu.VMEM((length, width), full)] * 2
    else:
        scratch += [pltpu.VMEM((length, width), low)]
    return pl.pallas_call(
        functools.partial(
            ffn_back_kernel, len(inputs), len(first), per, fused, min(256, length)
        ),
        grid=(PARTS,),
        out_shape=tuple(o[0] for o in outs),
        in_specs=[pl.BlockSpec(memory_space=pltpu.SMEM)]
        + first_specs(first, per)
        + ahead
        + [constant(width, length), constant(length, width)]
        + piece_specs(devices, per, width),
        out_specs=tuple(o[1] for o in outs),
        scratch_shapes=scratch,
        compiler_params=pltpu.CompilerParams(vmem_limit_bytes=VMEM_LIMIT),
        cost_estimate=pl.CostEstimate(
            flops=2 * length * width * width * (28 if fused else 19),
            bytes_accessed=24 * 2**20,
            transcendentals=length * hidden if fused else 0,
        ),
        name="ffn_both" if fused else "ffn_back",
    )(order, *first, *first, *(inputs if fused else kept), mixed, cot, second, second)


def across(block, bit):
    devices = lax.axis_size("batch")
    return lax.ppermute(block, "batch", [(i, i ^ bit) for i in range(devices)])


def pick(blocks, index, axis=0):
    return lax.dynamic_index_in_dim(blocks, index, axis, keepdims=False)


def stages():
    return list(range(lax.axis_size("batch").bit_length() - 1))[::-1]


def places(device):
    flips = device ^ lax.axis_index("batch")
    place, weight = jnp.zeros_like(device), 1
    for bit in stages():
        place = place + ((flips >> bit) & 1) * weight
        weight *= 2
    return place


def flipped(blocks, axis, bit):
    halves = [lax.index_in_dim(blocks, i, axis) for i in range(2)]
    is_set = (lax.axis_index("batch") >> bit) & 1 == 1
    return jnp.where(is_set, jnp.concatenate(halves[::-1], axis), blocks)


def by_device(blocks):
    filled = stages()
    bits = len(filled)
    rest = tuple(range(bits, bits + blocks.ndim - 1))
    shape = blocks.shape
    blocks = blocks.reshape((2,) * bits + shape[1:])
    blocks = blocks.transpose(
        tuple(bits - 1 - filled.index(b) for b in range(bits - 1, -1, -1)) + rest
    )
    for b in range(bits):
        blocks = flipped(blocks, bits - 1 - b, b)
    return blocks.reshape(shape)


def by_place(blocks):
    filled = stages()
    bits = len(filled)
    rest = tuple(range(bits, bits + blocks.ndim - 1))
    shape = blocks.shape
    blocks = blocks.reshape((2,) * bits + shape[1:])
    for b in range(bits):
        blocks = flipped(blocks, bits - 1 - b, b)
    blocks = blocks.transpose(tuple(bits - 1 - b for b in filled[::-1]) + rest)
    return blocks.reshape(shape)


def tie(value, *after):
    return lax.optimization_barrier((value,) + after)[0]


def joined(held, received):
    return jnp.concatenate([held, received], axis=0)


def halves(blocks):
    count = blocks.shape[0] // 2
    return blocks[:count], blocks[count:]


def plus(mine, received):
    return (mine.astype(full) + received.astype(full)).astype(low)


def widen(gathered, sizes, times):
    if times == 1:
        return gathered
    devices, _, width = gathered.shape
    grouped = gathered.reshape(devices // times, times, -1, width)
    parts, at = [], 0
    for size in sizes:
        parts.append(
            grouped[:, :, at : at + size].reshape(devices // times, times * size, width)
        )
        at += size
    return jnp.concatenate(parts, axis=1)


def narrow(grads, sizes, times):
    if times == 1:
        return grads
    groups, _, width = grads.shape
    parts, at = [], 0
    for size in sizes:
        parts.append(
            grads[:, at : at + times * size].reshape(groups * times, size, width)
        )
        at += times * size
    rest = grads[:, at:]
    parts.append(jnp.repeat(rest, times, axis=0))
    return jnp.concatenate(parts, axis=1)


def update(gradient, weight, momentum, average, step_rate):
    new_momentum = momentum_decay * momentum + gradient
    new_weight = weight - step_rate * (gradient + momentum_decay * new_momentum)
    new_average = average + (new_weight - average) / (STEP + 1.0)
    return (gradient, new_momentum, new_weight, new_average)


def shards(
    tokens,
    cotangent,
    lengths,
    qkv_weight,
    qkv_momentum,
    qkv_average,
    out_weight,
    out_momentum,
    out_average,
    up_weight,
    up_momentum,
    up_average,
    down_weight,
    down_momentum,
    down_average,
    norm_params,
    norm_momentum,
    norm_average,
):
    section = lax.axis_index("section")
    here = lax.axis_index("batch")
    width = tokens.shape[2]
    length = tokens.shape[1] // lengths.shape[0]
    assert lengths.shape[0] == lax.axis_size("section") == 2
    own_rows = out_weight.shape[1]
    times = max(1, TILE // own_rows)
    per = own_rows * times
    first_sizes = (own_rows,) * 4
    second_sizes = (own_rows,) * PARTS + (PARTS * own_rows,)

    def swap(block):
        return lax.ppermute(block, "section", [(0, 1), (1, 0)])

    def sorted_pair(mine, other):
        is_first = section == 0
        return jnp.where(is_first, mine, other), jnp.where(is_first, other, mine)

    lengths_mine = pick(lengths, section)
    norm_table = lax.dynamic_update_slice(
        jnp.zeros((TILE, width), low),
        norm_params[0].astype(low),
        (0, here * norm_params.shape[2]),
    )
    pack_first = jnp.concatenate(
        [
            qkv_weight[0].astype(low).reshape(-1, width),
            out_weight[0].astype(low),
            norm_table,
        ],
        axis=0,
    )
    up_low = up_weight[0].astype(low).reshape(own_rows, PARTS, width)
    pack_second = jnp.concatenate(
        [
            up_low.transpose(1, 0, 2).reshape(-1, width),
            down_weight[0].astype(low),
        ],
        axis=0,
    )
    order = places(jnp.arange(lax.axis_size("batch"), dtype=jnp.int32))
    steps = stages()
    split = times == 1

    pair_second = sorted_pair(pack_second, swap(pack_second))
    received = swap(pack_first)
    piece_e, piece_d = sorted_pair(pack_first, received)
    token_rows = tokens[0].reshape(2, length, width)
    cot_rows = cotangent[0].reshape(2, length, width)
    token_other = swap(tie(pick(token_rows, 1 - section), received))
    cot_other = swap(tie(pick(cot_rows, 1 - section), token_other))

    def gathered(held, bits):
        flips = [sum(((d >> i) & 1) << b for i, b in enumerate(bits)) for d in range(1, 1 << len(bits))]
        return [across(held, flip) for flip in flips]

    high = steps[:-2]
    wide = [high[i : i + 2] for i in range(0, len(high), 2)]
    held_e = piece_e[None]
    for bits in wide:
        held_e = jnp.concatenate([held_e] + gathered(held_e, bits))
    held_d = tie(piece_d[None], held_e)
    for bits in wide:
        held_d = jnp.concatenate([held_d] + gathered(held_d, bits))
    held_e = joined(tie(held_e, token_other), across(held_e, 1 << steps[-2]))
    other_e = across(held_e, 1 << steps[-1])
    coming = across(held_d, 1 << steps[-2])

    def whole_first(held, other):
        if times == 1:
            return (held, other)
        held = by_device(joined(held, other))
        body = widen(held[:, : 4 * own_rows], first_sizes, times)
        table = held[:, 4 * own_rows :].reshape(-1, times, TILE, width)
        return (jnp.concatenate([body, jnp.sum(table, axis=1)], axis=1),)

    def whole_second(piece):
        gathered = lax.all_gather(piece, "batch", axis=0, tiled=False)
        return widen(gathered, second_sizes, times)

    second = [whole_second(piece) for piece in pair_second]
    natural = jnp.arange(second[0].shape[0], dtype=jnp.int32)
    placed = order if split else natural

    encoder_in = jnp.where(section == 0, pick(token_rows, section), token_other)
    denoiser_in = jnp.where(section == 0, token_other, pick(token_rows, section))
    encoder_cot, denoiser_cot = sorted_pair(pick(cot_rows, section), cot_other)
    encoder_in, denoiser_in, encoder_cot, denoiser_cot = lax.optimization_barrier(
        (encoder_in, denoiser_in, encoder_cot, denoiser_cot)
    )
    first_e = whole_first(held_e, other_e)
    kept_e = attend(lengths_mine, placed, [encoder_in], first_e, per)
    held_d = joined(held_d, tie(coming, kept_e[4]))
    other_d = across(held_d, 1 << steps[-1])
    x2_e, hidden_e, slope_e, encoded = ffn_forward(
        placed, [encoder_in], tie(kept_e[3], held_d), first_e, second[0], per
    )
    first_d = whole_first(held_d, tie(other_d, encoded))
    inputs_d = [denoiser_in, encoded]
    kept_d = attend(lengths_mine, placed, inputs_d, first_d, per)
    decoded, dx2_d, *rest_d = ffn_back(
        placed, inputs_d, None, kept_d[3], denoiser_cot, first_d, second[1], per
    )

    def reduced(grads):
        return lax.psum_scatter(
            narrow(grads, second_sizes, times).reshape(-1, width),
            "batch",
            scatter_dimension=0,
            tiled=True,
        )

    def cores(grads):
        if split:
            return grads
        return halves(by_place(narrow(grads[0], first_sizes, times)))

    back = [1 << bit for bit in steps[::-1]]
    second_d = reduced(rest_d[5])
    all_pairs = (0, width // LANES)
    dx_d, dx_low_d, *grads_first_d = attend_back(
        lengths_mine, placed, inputs_d, first_d, kept_d, rest_d[:3], dx2_d, rest_d[3:5], per,
        all_pairs, (), split,
    )
    mine_d, other = cores(grads_first_d)
    coming_d = across(other, back[0])
    dx2_e, *rest_e = ffn_back(
        placed, [], (x2_e, hidden_e, slope_e, dx_low_d), kept_e[3], encoder_cot, first_e, second[0], per
    )
    second_e = reduced(rest_e[5])
    mine_d, other = halves(plus(mine_d, coming_d))
    coming_d = across(other, back[1])
    some = all_pairs[1] // 2
    earlier = attend_back(
        lengths_mine, placed, [], first_e, kept_e, [tie(rest_e[0], mine_d), *rest_e[1:3]], dx2_e, (),
        per, (0, some), None, split,
    )
    mine_d, other = halves(plus(mine_d, tie(coming_d, earlier[0])))
    coming_d = across(other, back[2])
    second_d, dx2_e, *earlier = lax.optimization_barrier((second_d, dx2_e, *earlier))
    dx_e, dx_low_e, *grads_first_e = attend_back(
        lengths_mine, placed, [encoder_in], first_e, kept_e, rest_e[:3], tie(dx2_e, mine_d),
        rest_e[3:5], per, (some, all_pairs[1]), tuple(earlier), split,
    )
    mine_e, other = cores(grads_first_e)
    coming_e = across(other, back[0])

    coming_d, bits_d = tie(coming_d, dx_low_e), back[3:]
    for bit in back[1:]:
        mine_e = plus(mine_e, coming_e)
        if coming_d is not None:
            mine_d = plus(mine_d, coming_d)
            coming_d = None
        if bits_d:
            mine_e, mine_d = lax.optimization_barrier((mine_e, mine_d))
            mine_d, other = halves(mine_d)
            coming_d = across(other, bits_d.pop(0))
        mine_e, other = halves(mine_e)
        coming_e = across(other, bit)
    if coming_d is not None:
        mine_d = plus(mine_d, coming_d)
    first_e, first_d = plus(mine_e, coming_e)[0], mine_d[0]

    def summed(of_first, of_second):
        is_first = section == 0
        mine = jnp.where(is_first, of_first.astype(full), of_second.astype(full))
        other = swap(jnp.where(is_first, of_second.astype(low), of_first.astype(low)))
        return mine + other.astype(full)

    total_first = summed(first_e, first_d)

    def both(encoder_part, denoiser_part, received):
        mine = jnp.where(section == 0, encoder_part, denoiser_part)
        received = received.astype(mine.dtype)
        return jnp.where(
            section == 0, jnp.stack([mine, received]), jnp.stack([received, mine])
        ).reshape(1, 2 * length, width)

    activations = both(
        encoded, decoded, tie(swap(jnp.where(section == 0, decoded, encoded)), dx_low_e)
    )
    input_grad = both(
        dx_e, dx_d, tie(swap(jnp.where(section == 0, dx_low_d, dx_low_e)), total_first)
    )
    total_second = summed(tie(second_e, total_first, input_grad, activations), second_d)

    qkv_grad = total_first[: 3 * own_rows].reshape(qkv_weight.shape)
    up_grad = total_second[: 4 * own_rows].reshape(PARTS, own_rows, width)
    up_grad = up_grad.transpose(1, 0, 2).reshape(up_weight.shape)
    down_grad = total_second[4 * own_rows : 8 * own_rows][None]
    out_grad = total_first[3 * own_rows : 4 * own_rows][None]
    norm_all = total_first[4 * own_rows : 4 * own_rows + 4]
    own_features = norm_params.shape[2]
    norm_grad = lax.dynamic_slice(
        norm_all, (0, here * own_features), (4, own_features)
    )[None]
    qkv_new = update(qkv_grad, qkv_weight, qkv_momentum, qkv_average, rate_qkv)
    out_new = update(out_grad, out_weight, out_momentum, out_average, rate_out)
    up_new = update(up_grad, up_weight, up_momentum, up_average, rate_up)
    down_new = update(down_grad, down_weight, down_momentum, down_average, rate_down)
    norm_new = update(norm_grad, norm_params, norm_momentum, norm_average, rate_norm)
    return (
        activations,
        input_grad,
        *qkv_new,
        *out_new,
        *up_new,
        *down_new,
        *norm_new,
        norm_grad[:, 3],
    )


def solution(mesh):
    rows = P("section", "batch", None)
    deep = P("section", None, "batch", None)
    features = P("section", None, "batch")
    return jax.shard_map(
        shards,
        mesh=mesh,
        in_specs=(rows, rows, P("batch", None))
        + (deep,) * 3
        + (rows,) * 9
        + (features,) * 3,
        out_specs=(rows, rows)
        + (deep,) * 4
        + (rows,) * 12
        + (features,) * 4
        + (P("section", "batch"),),
        check_vma=False,
    )
```

```python
import functools
import math

import jax
import jax.numpy as jnp
from jax import lax
from jax.experimental import pallas as pl
from jax.experimental.pallas import tpu as pltpu
from jax.sharding import PartitionSpec as P

HEADS = 8
HEAD_DIM = 64
STEP = 5

eps = 1e-05
momentum_decay = 0.9
rate_qkv = 0.0001
rate_out = 0.01
rate_up = 0.0002
rate_down = 4e-05
rate_norm = 0.0004
neg_large = -1e30

low = jnp.bfloat16
full = jnp.float32

NN = (((1,), (0,)), ((), ()))
NT = (((1,), (1,)), ((), ()))
TN = (((0,), (0,)), ((), ()))

POWER = math.log2(math.e) * HEAD_DIM ** (-0.5)
SCALE = HEAD_DIM ** (-0.5)
GELU_C = math.sqrt(2.0 / math.pi)
GELU_A = 0.044715
LANES = 128
TILE = 16
PARTS = 4
VMEM_LIMIT = 58 * 2**20


def dot(a, b, dims):
    return lax.dot_general(a, b, dims, preferred_element_type=full)


def norm_stats(values):
    centre = values - jnp.mean(values, axis=-1, keepdims=True)
    spread = jnp.mean(centre * centre, axis=-1, keepdims=True)
    scale = lax.rsqrt(spread + eps)
    return centre * scale, scale


def norm_back(hat, scale, gain, grad):
    inner = grad * gain
    back = scale * (
        inner
        - jnp.mean(inner, axis=-1, keepdims=True)
        - hat * jnp.mean(inner * hat, axis=-1, keepdims=True)
    )
    return (
        back,
        jnp.sum(grad * hat, axis=0, keepdims=True),
        jnp.sum(grad, axis=0, keepdims=True),
    )


def norm_rows(refs, rows=slice(None)):
    total = jnp.sum(refs[0][:, rows, :].astype(full), axis=0)
    for ref in refs[1:]:
        total = total + jnp.sum(ref[:, rows, :].astype(full), axis=0)
    return total


def gelu_both(u):
    square = u * u
    t = jnp.tanh(GELU_C * u * (1.0 + GELU_A * square))
    half = 0.5 + 0.5 * t
    slope = half + (0.5 * GELU_C) * u * (1.0 - t * t) * (1.0 + (3.0 * GELU_A) * square)
    return u * half, slope


def masks(lengths_ref, rows):
    place = lax.broadcasted_iota(jnp.int32, (rows, LANES), 0)
    lane = lax.broadcasted_iota(jnp.int32, (rows, LANES), 1)
    first = lengths_ref[0]
    second = first + lengths_ref[1]
    third = second + lengths_ref[2]
    item = (
        (place >= first).astype(jnp.int32)
        + (place >= second).astype(jnp.int32)
        + (place >= third).astype(jnp.int32)
    )
    own = item == lane
    query = jnp.where(own, neg_large, 0.0).astype(low)
    key = jnp.where(own | (lane > 3), 0.0, 1.0).astype(low)
    return query, key


def added(refs, rows=slice(None)):
    total = refs[0][rows].astype(full)
    for ref in refs[1:]:
        total = total + ref[rows].astype(full)
    return total


def put_in_order(order_ref, weight_refs, ordered, per, pieces):
    def put(b, j, rows):
        ordered[j, b * per : (b + 1) * per, :] = rows

    if len(weight_refs) == 1:
        for b in range(weight_refs[0].shape[0]):
            for j in range(pieces):
                put(b, j, weight_refs[0][order_ref[b], j * per : (j + 1) * per, :])
        return
    half = weight_refs[0].shape[0]
    for b in range(0, 2 * half, 2):
        places = order_ref[b], order_ref[b + 1]
        even = places[0] < half
        place = jnp.where(even, places[0], places[1])
        for j in range(pieces):
            own, other = (ref[place, j * per : (j + 1) * per, :] for ref in weight_refs)
            put(b, j, jnp.where(even, own, other))
            put(b + 1, j, jnp.where(even, other, own))


def put_blocks(order_ref, first, grad_refs, rows, values):
    if len(grad_refs) == 1:
        for b in range(values.shape[0]):
            grad_refs[0][order_ref[first + b], rows, :] = values[b]
        return
    half = grad_refs[0].shape[0]
    for b in range(0, values.shape[0], 2):
        places = order_ref[first + b], order_ref[first + b + 1]
        even = places[0] < half
        place = jnp.where(even, places[0], places[1])
        grad_refs[0][place, rows, :] = jnp.where(even, values[b], values[b + 1])
        grad_refs[1][place, rows, :] = jnp.where(even, values[b + 1], values[b])


def put_everywhere(grad_refs, rows, values):
    for ref in grad_refs:
        ref[:, rows, :] = jnp.broadcast_to(values[None], (ref.shape[0],) + values.shape)


def grad_shapes(devices, rows, width, split):
    if split:
        return [jax.ShapeDtypeStruct((devices // 2, rows, width), low)] * 2
    return [jax.ShapeDtypeStruct((devices, rows, width), low)]


def attend_kernel(count, parts, per, block, *refs):
    lengths_ref, order_ref, refs = refs[0], refs[1], refs[2:]
    inputs, refs = refs[:count], refs[count:]
    weights_in, refs = refs[:parts], refs[parts:]
    q_out, k_out, v_out, o_ref, log_ref, *refs = refs
    weight_refs, refs = refs[:parts], refs[parts:]
    a_s, vt_s, qm_s, km_s, w_s, q_ref, k_ref, v_ref, in_sems, out_sems = refs
    length, width = q_ref.shape
    arriving = [
        pltpu.make_async_copy(source, target, in_sems.at[i])
        for i, (source, target) in enumerate(zip(weights_in, weight_refs))
    ]
    for copy in arriving:
        copy.start()
    hat, _ = norm_stats(added(inputs))
    qm_s[...], km_s[...] = masks(lengths_ref, length)
    for copy in arriving:
        copy.wait()
    norm_vals = norm_rows(weight_refs, slice(4 * per, 4 * per + TILE))
    put_in_order(order_ref, weight_refs, w_s, per, 3)

    def weight(j):
        return w_s[j]

    a_s[...] = (hat * norm_vals[0:1] + norm_vals[1:2]).astype(low)
    q_ref[...] = dot(a_s[...], weight(0), NN).astype(low)
    k_ref[...] = dot(a_s[...], weight(1), NN).astype(low)
    v_ref[...] = dot(a_s[...], weight(2), NN).astype(low)
    leaving = [
        pltpu.make_async_copy(source, target, out_sems.at[i])
        for i, (source, target) in enumerate(((q_ref, q_out), (k_ref, k_out), (v_ref, v_out)))
    ]
    for copy in leaving:
        copy.start()
    vt_s[...] = v_ref[...].T
    lanes = lax.broadcasted_iota(jnp.int32, (1, LANES), 1)
    zero = jnp.zeros((), low)

    jobs = [
        (p, h, b)
        for p in range(width // LANES)
        for h in range(2)
        for b in range(length // block)
    ]

    def scores(job):
        p, h, b = job
        cols = slice(p * LANES, (p + 1) * LANES)
        rows = slice(b * block, (b + 1) * block)
        queries = jnp.where(lanes // HEAD_DIM == h, q_ref[rows, cols], zero)
        return dot(
            jnp.concatenate([k_ref[:, cols], km_s[...]], axis=1),
            jnp.concatenate([queries, qm_s[rows, :]], axis=1),
            NT,
        )

    ahead = scores(jobs[0])
    for i, (p, h, b) in enumerate(jobs):
        s = ahead
        if i + 1 < len(jobs):
            ahead = scores(jobs[i + 1])
        head = 2 * p + h
        rows = slice(head * HEAD_DIM, (head + 1) * HEAD_DIM)
        cols = slice(b * block, (b + 1) * block)
        top = jnp.max(s, axis=0, keepdims=True) * POWER
        raised = jnp.exp2(s * POWER - top)
        total = jnp.sum(raised, axis=0, keepdims=True)
        mixed = dot(vt_s[rows, :], raised.astype(low), NN)
        o_ref[rows, cols] = (mixed * (1.0 / total)).astype(low)
        log_ref[head : head + 1, cols] = top + jnp.log2(total)
    for copy in leaving:
        copy.wait()


def attend(lengths, order, inputs, weights, per):
    length, width = inputs[0].shape
    shape = jax.ShapeDtypeStruct
    flops = 2 * length * width * width * 3 + 8 * length * length * width
    return pl.pallas_call(
        functools.partial(attend_kernel, len(inputs), len(weights), per, min(512, length)),
        out_shape=(
            shape((length, width), low),
            shape((length, width), low),
            shape((length, width), low),
            shape((width, length), low),
            shape((HEADS, length), full),
        ),
        in_specs=[pl.BlockSpec(memory_space=pltpu.SMEM)] * 2
        + [pl.BlockSpec(memory_space=pltpu.VMEM)] * len(inputs)
        + [pl.BlockSpec(memory_space=pl.ANY)] * len(weights),
        out_specs=[pl.BlockSpec(memory_space=pl.ANY)] * 3
        + [pl.BlockSpec(memory_space=pltpu.VMEM)] * 2,
        scratch_shapes=[pltpu.VMEM(array.shape, low) for array in weights]
        + [
            pltpu.VMEM((length, width), low),
            pltpu.VMEM((width, length), low),
            pltpu.VMEM((length, LANES), low),
            pltpu.VMEM((length, LANES), low),
            pltpu.VMEM((3, width, width), low),
        ]
        + [pltpu.VMEM((length, width), low)] * 3
        + [pltpu.SemaphoreType.DMA((len(weights),)), pltpu.SemaphoreType.DMA((3,))],
        compiler_params=pltpu.CompilerParams(vmem_limit_bytes=VMEM_LIMIT),
        cost_estimate=pl.CostEstimate(
            flops=2 * flops, bytes_accessed=8 * 2**20, transcendentals=HEADS * length * length
        ),
        name="attend",
    )(lengths, order, *inputs, *weights)


def heads_back(refs, scratch, pairs, block):
    q_ref, k_ref, v_ref, do_ref, dot_ref, log_ref, sum_ref, dqt_ref, dkt_ref, dvt_ref = refs
    qt_s, kt_s, dk_s, dv_s, qm_s, km_s = scratch
    length = q_ref.shape[0]
    blocks = length // block
    qt_s[...] = q_ref[...].T
    kt_s[...] = k_ref[...].T
    lanes = lax.broadcasted_iota(jnp.int32, (1, LANES), 1)
    zero = jnp.zeros((), low)

    def pair(p, carry):
        off = pl.multiple_of(p * LANES, LANES)
        wide = pl.ds(off, LANES)
        keys = jnp.concatenate([k_ref[:, wide], km_s[...]], axis=1)
        jobs = [(h, b) for h in range(2) for b in range(blocks)]

        def scores(job):
            h, b = job
            rows = slice(b * block, (b + 1) * block)
            keep = lanes // HEAD_DIM == h
            queries = jnp.where(keep, q_ref[rows, wide], zero)
            outer = jnp.where(keep, do_ref[rows, wide], zero)
            return (
                dot(keys, jnp.concatenate([queries, qm_s[rows, :]], axis=1), NT),
                dot(v_ref[:, wide], outer, NT),
            )

        ahead = scores(jobs[0])
        for i, (h, b) in enumerate(jobs):
            s, dp = ahead
            if i + 1 < len(jobs):
                ahead = scores(jobs[i + 1])
            rows = pl.ds(pl.multiple_of(off + h * HEAD_DIM, HEAD_DIM), HEAD_DIM)
            cols = slice(b * block, (b + 1) * block)
            head = pl.ds(2 * (pairs[0] + p) + h, 1)
            prob = jnp.exp2(s * POWER - log_ref[head, cols])
            ds = (prob * (dp - sum_ref[head, cols])).astype(low)
            prob = prob.astype(low)
            dv = dot(dot_ref[rows, cols], prob, NT)
            dk = dot(qt_s[rows, cols], ds, NT)
            dqt_ref[rows, cols] = (dot(kt_s[rows, :], ds, NN) * SCALE).astype(low)
            if b > 0:
                dv = dv_s[...] + dv
                dk = dk_s[...] + dk
            if b < blocks - 1:
                dv_s[...] = dv
                dk_s[...] = dk
            else:
                dvt_ref[rows, :] = dv.astype(low)
                dkt_ref[rows, :] = (dk * SCALE).astype(low)
        return carry

    lax.fori_loop(0, pairs[1] - pairs[0], pair, 0)


def attend_back_kernel(count, parts, per, block, pairs, last, *refs):
    lengths_ref, refs = refs[0], refs[1:]
    heads, refs = refs[:7], refs[7:]
    if last:
        before = 3 if pairs[0] > 0 else 0
        order_ref, refs = refs[0], refs[1:]
        earlier, refs = refs[:before], refs[before:]
        inputs, refs = refs[:count], refs[count:]
        weight_refs, refs = refs[:parts], refs[parts:]
        dx2_ref, outg_ref, norms_ref, dx_ref, dxl_ref, *refs = refs
        grads_at = len(refs) - 10
        grad_refs, grads_s, scratch = refs[:grads_at], refs[grads_at : grads_at + 3], refs[grads_at + 3 :]
        *scratch, w_s = scratch
    else:
        grads_s, scratch = refs[:3], refs[3:]
    length = heads[0].shape[0]
    scratch[4][...], scratch[5][...] = masks(lengths_ref, length)
    heads_back(heads + tuple(grads_s), scratch, pairs, block)
    if not last:
        return
    width = w_s.shape[1]
    put_in_order(order_ref, weight_refs, w_s, per, 3)
    norm_vals = norm_rows(weight_refs, slice(4 * per, 4 * per + TILE))
    hat, scale = norm_stats(added(inputs))
    a = (hat * norm_vals[0:1] + norm_vals[1:2]).astype(low)
    da = jnp.zeros((length, width), full)
    for j in range(3):
        if before:
            grads = jnp.concatenate([earlier[j][...].T, grads_s[j][...].T], axis=1)
        else:
            grads = grads_s[j][...].T
        da = da + dot(grads, w_s[j], NT)
        put_blocks(
            order_ref,
            0,
            grad_refs,
            slice(j * per, (j + 1) * per),
            dot(a, grads, TN).astype(low).reshape(width // per, per, width),
        )
    back, gain, shift = norm_back(hat, scale, norm_vals[0:1], da)
    dx = dx2_ref[...] + back
    dx_ref[...] = dx
    dxl_ref[...] = dx.astype(low)
    put_blocks(
        order_ref,
        0,
        grad_refs,
        slice(3 * per, 4 * per),
        outg_ref[...].reshape(width // per, per, width),
    )
    tail = jnp.concatenate(
        [gain, shift, norms_ref[...], jnp.zeros((TILE - 4, width), full)], axis=0
    )
    put_everywhere(grad_refs, slice(4 * per, 4 * per + TILE), tail.astype(low))


def head_specs(length, pairs):
    wide = (pairs[1] - pairs[0]) * LANES
    at = pairs[0] * LANES // wide
    assert at * wide == pairs[0] * LANES
    columns = pl.BlockSpec((length, wide), lambda i: (0, at))
    return [columns] * 4 + [pl.BlockSpec((wide, length), lambda i: (at, 0))] + [
        pl.BlockSpec(memory_space=pltpu.VMEM)] * 2


def head_scratch(length, pairs):
    wide = (pairs[1] - pairs[0]) * LANES
    return (
        [pltpu.VMEM((wide, length), low)] * 2
        + [pltpu.VMEM((HEAD_DIM, length), full)] * 2
        + [pltpu.VMEM((length, LANES), low)] * 2
    )


def attend_back(
    lengths, order, inputs, weights, kept, outer, dx2, others, per, pairs, earlier, split
):
    q, k, v, _, logs = kept
    outer, outer_t, sums = outer
    length, width = q.shape
    shape = jax.ShapeDtypeStruct
    count = pairs[1] - pairs[0]
    wide = count * LANES
    devices = width // per
    last = earlier is not None
    flops = 20 * length * length * wide + (12 * length * width * width if last else 0)
    whole = pl.BlockSpec(memory_space=pltpu.VMEM)
    smem = pl.BlockSpec(memory_space=pltpu.SMEM)
    arrays = [lengths, q, k, v, outer, outer_t, logs, sums]
    specs = [smem] + head_specs(length, pairs)
    transposed = [shape((wide, length), low)] * 3
    scratch = head_scratch(length, pairs)
    if last:
        arrays += [order, *earlier, *inputs, *weights, dx2, *others]
        specs += [smem] + [whole] * (len(earlier) + len(inputs) + len(weights) + 3)
        outs = [shape((length, width), full), shape((length, width), low)]
        outs += grad_shapes(devices, 4 * per + TILE, width, split)
        scratch = [pltpu.VMEM((wide, length), low)] * 3 + scratch
        scratch += [pltpu.VMEM((3, width, width), low)]
    else:
        outs = transposed
    return pl.pallas_call(
        functools.partial(
            attend_back_kernel, len(inputs), len(weights), per, min(256, length), pairs, last
        ),
        grid=(1,),
        out_shape=tuple(outs),
        in_specs=specs,
        out_specs=[whole] * len(outs),
        scratch_shapes=scratch,
        compiler_params=pltpu.CompilerParams(vmem_limit_bytes=VMEM_LIMIT),
        cost_estimate=pl.CostEstimate(
            flops=2 * flops,
            bytes_accessed=16 * 2**20,
            transcendentals=2 * count * length * length,
        ),
        name="attend_back" if last else "attend_back_part",
    )(*arrays)


def middle_start(inputs, o_ref, out, norm_refs):
    norm_vals = norm_rows(norm_refs)
    x2 = added(inputs) + dot(o_ref[...], out, TN)
    hat, _ = norm_stats(x2)
    return x2, (hat * norm_vals[2:3] + norm_vals[3:4]).astype(low)


def ffn_forward_kernel(count, parts, block, *refs):
    order_ref, refs = refs[0], refs[1:]
    inputs, refs = refs[:count], refs[count:]
    norm_refs, out_refs, refs = refs[:parts], refs[parts : 2 * parts], refs[2 * parts :]
    (
        o_ref, up_ref, down_ref,
        x2_ref, h_ref, slope_ref, y_ref,
        c_s, acc_s, out_s,
    ) = refs
    length, width = x2_ref.shape
    j = pl.program_id(0)

    @pl.when(j == 0)
    def _():
        put_in_order(order_ref, out_refs, out_s, out_refs[0].shape[1], 1)
        x2, c = middle_start(inputs, o_ref, out_s[0], norm_refs)
        x2_ref[...] = x2
        acc_s[...] = x2
        c_s[...] = c

    up = up_ref[...].reshape(width, width)
    down = down_ref[...].reshape(width, width)
    spans = [slice(i, i + block) for i in range(0, length, block)]
    ahead = dot(c_s[spans[0], :], up, NN)
    for i, rows in enumerate(spans):
        u = ahead
        if i + 1 < len(spans):
            ahead = dot(c_s[spans[i + 1], :], up, NN)
        h, slope = gelu_both(u)
        h = h.astype(low)
        h_ref[rows, :] = h
        slope_ref[rows, :] = slope.astype(low)
        acc_s[rows, :] += dot(h, down, NN)

    @pl.when(j == pl.num_programs(0) - 1)
    def _():
        y_ref[...] = acc_s[...].astype(low)


def piece_specs(devices, per, width):
    return [
        pl.BlockSpec((devices, per, width), lambda j: (0, j, 0)),
        pl.BlockSpec((devices // PARTS, 4 * per, width), lambda j: (j, 1, 0)),
    ]


def first_specs(first, per):
    shapes = [array.shape for array in first]
    return [
        pl.BlockSpec((count, TILE, width), lambda j: (0, 4 * per // TILE, 0))
        for count, _, width in shapes
    ] + [
        pl.BlockSpec((count, per, width), lambda j: (0, 3, 0)) for count, _, width in shapes
    ]


def constant(*dims):
    return pl.BlockSpec(dims, lambda j: (0,) * len(dims))


def ffn_forward(order, inputs, mixed, first, second, per):
    length, width = inputs[0].shape
    devices = width // per
    shape = jax.ShapeDtypeStruct
    hidden = PARTS * width
    return pl.pallas_call(
        functools.partial(ffn_forward_kernel, len(inputs), len(first), min(256, length)),
        grid=(PARTS,),
        out_shape=(
            shape((length, width), full),
            shape((length, hidden), low),
            shape((length, hidden), low),
            shape((length, width), low),
        ),
        in_specs=[pl.BlockSpec(memory_space=pltpu.SMEM)]
        + [constant(length, width)] * len(inputs)
        + first_specs(first, per)
        + [constant(width, length)]
        + piece_specs(devices, per, width),
        out_specs=[
            constant(length, width),
            pl.BlockSpec((length, width), lambda j: (0, j)),
            pl.BlockSpec((length, width), lambda j: (0, j)),
            constant(length, width),
        ],
        scratch_shapes=[
            pltpu.VMEM((length, width), low),
            pltpu.VMEM((length, width), full),
            pltpu.VMEM((1, width, width), low),
        ],
        compiler_params=pltpu.CompilerParams(vmem_limit_bytes=VMEM_LIMIT),
        cost_estimate=pl.CostEstimate(
            flops=2 * length * width * width * 9,
            bytes_accessed=16 * 2**20,
            transcendentals=length * hidden,
        ),
        name="ffn_forward",
    )(order, *inputs, *first, *first, mixed, second, second)


def ffn_back_kernel(count, parts, per, fused, block, *refs):
    order_ref, refs = refs[0], refs[1:]
    norm_refs, out_refs, refs = refs[:parts], refs[parts : 2 * parts], refs[2 * parts :]
    if fused:
        inputs, refs = refs[:count], refs[count:]
        (
            o_ref, cot_ref, up_ref, down_ref,
            y_ref, dx2_ref, do_ref, dot_ref, sum_ref, outg_ref, norms_ref, grad_ref,
            out_s, c_s, dc_s, h_s, du_s, x2_ref, acc_s, down_s, up_s, sems,
        ) = refs
        dyb_ref = cot_ref
    else:
        (
            x2_ref, h_ref, slope_ref, later_ref,
            o_ref, cot_ref, up_ref, down_ref,
            dx2_ref, do_ref, dot_ref, sum_ref, outg_ref, norms_ref, grad_ref,
            out_s, c_s, dc_s, h_s, du_s, dyb_ref, down_s, up_s, sems,
        ) = refs
        h_s = h_ref
    length, width = dx2_ref.shape
    devices = width // per
    j = pl.program_id(0)

    def cot(rows):
        dy = cot_ref[rows, :].astype(full)
        if not fused:
            dy = dy + later_ref[rows, :].astype(full)
        return dy

    everything = slice(0, length)

    @pl.when(j == 0)
    def _():
        put_in_order(order_ref, out_refs, out_s, per, 1)
        if fused:
            x2, c = middle_start(inputs, o_ref, out_s[0], norm_refs)
            x2_ref[...] = x2
            acc_s[...] = x2
        else:
            norm_vals = norm_rows(norm_refs)
            hat, _ = norm_stats(x2_ref[...])
            c = (hat * norm_vals[2:3] + norm_vals[3:4]).astype(low)
            dyb_ref[...] = cot(everything).astype(low)
        c_s[...] = c
        dc_s[...] = jnp.zeros((length, width), full)

    up = up_ref[...].reshape(width, width)
    down = down_ref[...].reshape(width, width)
    spans = [slice(i, i + block) for i in range(0, length, block)]

    def products(rows):
        dh = dot(dyb_ref[rows, :], down, NT)
        return (dot(c_s[rows, :], up, NN) if fused else None), dh

    ahead = products(spans[0])
    for i, rows in enumerate(spans):
        u, dh = ahead
        if i + 1 < len(spans):
            ahead = products(spans[i + 1])
        if fused:
            h, slope = gelu_both(u)
            h = h.astype(low)
            h_s[rows, :] = h
            acc_s[rows, :] += dot(h, down, NN)
        else:
            slope = slope_ref[rows, :].astype(full)
        du = (slope * dh).astype(low)
        du_s[rows, :] = du
        dc_s[rows, :] += dot(du, up, NT)
    some = devices // PARTS

    def leaving(step):
        down_rows = grad_ref.at[pl.ds(step * some, some), pl.ds(4 * per, 4 * per), :]
        up_rows = grad_ref.at[:, pl.ds(pl.multiple_of(step * per, TILE), per), :]
        return (
            pltpu.make_async_copy(down_s.at[step], down_rows, sems.at[0, step]),
            pltpu.make_async_copy(up_s.at[step], up_rows, sems.at[1, step]),
        )

    down_s[j] = dot(h_s[...], dyb_ref[...], TN).astype(low).reshape(some, 4 * per, width)
    leaving(j)[0].start()
    up_s[j] = dot(c_s[...], du_s[...], TN).astype(low).reshape(devices, per, width)
    leaving(j)[1].start()

    @pl.when(j == pl.num_programs(0) - 1)
    def _():
        if fused:
            y_ref[...] = acc_s[...].astype(low)
        norm_vals = norm_rows(norm_refs)
        hat, scale = norm_stats(x2_ref[...])
        back, gain, shift = norm_back(hat, scale, norm_vals[2:3], dc_s[...])
        dx2 = cot(everything) + back
        dx2_ref[...] = dx2
        dab = dx2.astype(low)
        out = out_s[0]
        outg_ref[...] = dot(o_ref[...], dab, NN).astype(low)
        do_ref[...] = dot(dab, out, NT).astype(low)
        outer = dot(out, dab, NT).astype(low)
        dot_ref[...] = outer
        product = outer.astype(full) * o_ref[...].astype(full)
        sum_ref[...] = jnp.sum(product.reshape(HEADS, HEAD_DIM, length), axis=1)
        norms_ref[0:1, :] = gain
        norms_ref[1:2, :] = shift
        for step in range(PARTS):
            for copy in leaving(step):
                copy.wait()


def ffn_back(order, inputs, kept, mixed, cot, first, second, per):
    fused = kept is None
    length, width = cot.shape
    devices = width // per
    shape = jax.ShapeDtypeStruct
    hidden = PARTS * width
    column = pl.BlockSpec((length, width), lambda j: (0, j))
    ahead = [constant(length, width)] * len(inputs) if fused else [
        constant(length, width), column, column, constant(length, width)]
    outs = [
        (shape((length, width), full), constant(length, width)),
        (shape((length, width), low), constant(length, width)),
        (shape((width, length), low), constant(width, length)),
        (shape((HEADS, length), full), constant(HEADS, length)),
        (shape((width, width), low), constant(width, width)),
        (shape((2, width), full), constant(2, width)),
        (shape(second.shape, low), pl.BlockSpec(memory_space=pl.ANY)),
    ]
    scratch = [
        pltpu.VMEM((1, width, width), low),
        pltpu.VMEM((length, width), low),
        pltpu.VMEM((length, width), full),
        pltpu.VMEM((length, width) if fused else (TILE, LANES), low),
        pltpu.VMEM((length, width), low),
    ]
    if fused:
        outs = [(shape((length, width), low), constant(length, width))] + outs
        scratch += [pltpu.VMEM((length, width), full)] * 2
    else:
        scratch += [pltpu.VMEM((length, width), low)]
    scratch += [
        pltpu.VMEM((PARTS, devices // PARTS, 4 * per, width), low),
        pltpu.VMEM((PARTS, devices, per, width), low),
        pltpu.SemaphoreType.DMA((2, PARTS)),
    ]
    return pl.pallas_call(
        functools.partial(
            ffn_back_kernel, len(inputs), len(first), per, fused, min(256, length)
        ),
        grid=(PARTS,),
        out_shape=tuple(o[0] for o in outs),
        in_specs=[pl.BlockSpec(memory_space=pltpu.SMEM)]
        + first_specs(first, per)
        + ahead
        + [constant(width, length), constant(length, width)]
        + piece_specs(devices, per, width),
        out_specs=tuple(o[1] for o in outs),
        scratch_shapes=scratch,
        compiler_params=pltpu.CompilerParams(vmem_limit_bytes=VMEM_LIMIT),
        cost_estimate=pl.CostEstimate(
            flops=2 * length * width * width * (28 if fused else 19),
            bytes_accessed=24 * 2**20,
            transcendentals=length * hidden if fused else 0,
        ),
        name="ffn_both" if fused else "ffn_back",
    )(order, *first, *first, *(inputs if fused else kept), mixed, cot, second, second)


def across(block, bit):
    devices = lax.axis_size("batch")
    return lax.ppermute(block, "batch", [(i, i ^ bit) for i in range(devices)])


def pick(blocks, index, axis=0):
    return lax.dynamic_index_in_dim(blocks, index, axis, keepdims=False)


def stages():
    return list(range(lax.axis_size("batch").bit_length() - 1))[::-1]


def places(device):
    flips = device ^ lax.axis_index("batch")
    place, weight = jnp.zeros_like(device), 1
    for bit in stages():
        place = place + ((flips >> bit) & 1) * weight
        weight *= 2
    return place


def flipped(blocks, axis, bit):
    halves = [lax.index_in_dim(blocks, i, axis) for i in range(2)]
    is_set = (lax.axis_index("batch") >> bit) & 1 == 1
    return jnp.where(is_set, jnp.concatenate(halves[::-1], axis), blocks)


def by_device(blocks):
    filled = stages()
    bits = len(filled)
    rest = tuple(range(bits, bits + blocks.ndim - 1))
    shape = blocks.shape
    blocks = blocks.reshape((2,) * bits + shape[1:])
    blocks = blocks.transpose(
        tuple(bits - 1 - filled.index(b) for b in range(bits - 1, -1, -1)) + rest
    )
    for b in range(bits):
        blocks = flipped(blocks, bits - 1 - b, b)
    return blocks.reshape(shape)


def by_place(blocks):
    filled = stages()
    bits = len(filled)
    rest = tuple(range(bits, bits + blocks.ndim - 1))
    shape = blocks.shape
    blocks = blocks.reshape((2,) * bits + shape[1:])
    for b in range(bits):
        blocks = flipped(blocks, bits - 1 - b, b)
    blocks = blocks.transpose(tuple(bits - 1 - b for b in filled[::-1]) + rest)
    return blocks.reshape(shape)


def tie(value, *after):
    return lax.optimization_barrier((value,) + after)[0]


def joined(held, received):
    return jnp.concatenate([held, received], axis=0)


def halves(blocks):
    count = blocks.shape[0] // 2
    return blocks[:count], blocks[count:]


def plus(mine, received):
    return (mine.astype(full) + received.astype(full)).astype(low)


def widen(gathered, sizes, times):
    if times == 1:
        return gathered
    devices, _, width = gathered.shape
    grouped = gathered.reshape(devices // times, times, -1, width)
    parts, at = [], 0
    for size in sizes:
        parts.append(
            grouped[:, :, at : at + size].reshape(devices // times, times * size, width)
        )
        at += size
    return jnp.concatenate(parts, axis=1)


def narrow(grads, sizes, times):
    if times == 1:
        return grads
    groups, _, width = grads.shape
    parts, at = [], 0
    for size in sizes:
        parts.append(
            grads[:, at : at + times * size].reshape(groups * times, size, width)
        )
        at += times * size
    rest = grads[:, at:]
    parts.append(jnp.repeat(rest, times, axis=0))
    return jnp.concatenate(parts, axis=1)


def update(gradient, weight, momentum, average, step_rate):
    new_momentum = momentum_decay * momentum + gradient
    new_weight = weight - step_rate * (gradient + momentum_decay * new_momentum)
    new_average = average + (new_weight - average) / (STEP + 1.0)
    return (gradient, new_momentum, new_weight, new_average)


def shards(
    tokens,
    cotangent,
    lengths,
    qkv_weight,
    qkv_momentum,
    qkv_average,
    out_weight,
    out_momentum,
    out_average,
    up_weight,
    up_momentum,
    up_average,
    down_weight,
    down_momentum,
    down_average,
    norm_params,
    norm_momentum,
    norm_average,
):
    section = lax.axis_index("section")
    here = lax.axis_index("batch")
    width = tokens.shape[2]
    length = tokens.shape[1] // lengths.shape[0]
    assert lengths.shape[0] == lax.axis_size("section") == 2
    own_rows = out_weight.shape[1]
    times = max(1, TILE // own_rows)
    per = own_rows * times
    first_sizes = (own_rows,) * 4
    second_sizes = (own_rows,) * PARTS + (PARTS * own_rows,)

    def swap(block):
        return lax.ppermute(block, "section", [(0, 1), (1, 0)])

    def sorted_pair(mine, other):
        is_first = section == 0
        return jnp.where(is_first, mine, other), jnp.where(is_first, other, mine)

    lengths_mine = pick(lengths, section)
    norm_table = lax.dynamic_update_slice(
        jnp.zeros((TILE, width), low),
        norm_params[0].astype(low),
        (0, here * norm_params.shape[2]),
    )
    pack_first = jnp.concatenate(
        [
            qkv_weight[0].astype(low).reshape(-1, width),
            out_weight[0].astype(low),
            norm_table,
        ],
        axis=0,
    )
    up_low = up_weight[0].astype(low).reshape(own_rows, PARTS, width)
    pack_second = jnp.concatenate(
        [
            up_low.transpose(1, 0, 2).reshape(-1, width),
            down_weight[0].astype(low),
        ],
        axis=0,
    )
    order = places(jnp.arange(lax.axis_size("batch"), dtype=jnp.int32))
    steps = stages()
    split = times == 1

    pair_second = sorted_pair(pack_second, swap(pack_second))
    received = swap(pack_first)
    piece_e, piece_d = sorted_pair(pack_first, received)
    token_rows = tokens[0].reshape(2, length, width)
    cot_rows = cotangent[0].reshape(2, length, width)
    token_other = swap(tie(pick(token_rows, 1 - section), received))
    cot_other = swap(tie(pick(cot_rows, 1 - section), token_other))

    def gathered(held, bits):
        flips = [sum(((d >> i) & 1) << b for i, b in enumerate(bits)) for d in range(1, 1 << len(bits))]
        return [across(held, flip) for flip in flips]

    high = steps[:-2]
    wide = [high[i : i + 2] for i in range(0, len(high), 2)]
    held_e = piece_e[None]
    for bits in wide:
        held_e = jnp.concatenate([held_e] + gathered(held_e, bits))
    held_d = tie(piece_d[None], held_e)
    for bits in wide:
        held_d = jnp.concatenate([held_d] + gathered(held_d, bits))
    held_e = joined(tie(held_e, token_other), across(held_e, 1 << steps[-2]))
    other_e = across(held_e, 1 << steps[-1])
    coming = across(held_d, 1 << steps[-2])

    def whole_first(held, other):
        if times == 1:
            return (held, other)
        held = by_device(joined(held, other))
        body = widen(held[:, : 4 * own_rows], first_sizes, times)
        table = held[:, 4 * own_rows :].reshape(-1, times, TILE, width)
        return (jnp.concatenate([body, jnp.sum(table, axis=1)], axis=1),)

    def whole_second(piece):
        gathered = lax.all_gather(piece, "batch", axis=0, tiled=False)
        return widen(gathered, second_sizes, times)

    second = [whole_second(piece) for piece in pair_second]
    natural = jnp.arange(second[0].shape[0], dtype=jnp.int32)
    placed = order if split else natural

    encoder_in = jnp.where(section == 0, pick(token_rows, section), token_other)
    denoiser_in = jnp.where(section == 0, token_other, pick(token_rows, section))
    encoder_cot, denoiser_cot = sorted_pair(pick(cot_rows, section), cot_other)
    encoder_in, denoiser_in, encoder_cot, denoiser_cot = lax.optimization_barrier(
        (encoder_in, denoiser_in, encoder_cot, denoiser_cot)
    )
    first_e = whole_first(held_e, other_e)
    kept_e = attend(lengths_mine, placed, [encoder_in], first_e, per)
    held_d = joined(held_d, tie(coming, kept_e[4]))
    other_d = across(held_d, 1 << steps[-1])
    x2_e, hidden_e, slope_e, encoded = ffn_forward(
        placed, [encoder_in], tie(kept_e[3], held_d), first_e, second[0], per
    )
    first_d = whole_first(held_d, tie(other_d, encoded))
    inputs_d = [denoiser_in, encoded]
    kept_d = attend(lengths_mine, placed, inputs_d, first_d, per)
    decoded, dx2_d, *rest_d = ffn_back(
        placed, inputs_d, None, kept_d[3], denoiser_cot, first_d, second[1], per
    )

    def reduced(grads):
        return lax.psum_scatter(
            narrow(grads, second_sizes, times).reshape(-1, width),
            "batch",
            scatter_dimension=0,
            tiled=True,
        )

    def cores(grads):
        if split:
            return grads
        return halves(by_place(narrow(grads[0], first_sizes, times)))

    back = [1 << bit for bit in steps[::-1]]
    second_d = reduced(rest_d[5])
    all_pairs = (0, width // LANES)
    dx_d, dx_low_d, *grads_first_d = attend_back(
        lengths_mine, placed, inputs_d, first_d, kept_d, rest_d[:3], dx2_d, rest_d[3:5], per,
        all_pairs, (), split,
    )
    mine_d, other = cores(grads_first_d)
    coming_d = across(other, back[0])
    dx2_e, *rest_e = ffn_back(
        placed, [], (x2_e, hidden_e, slope_e, dx_low_d), kept_e[3], encoder_cot, first_e, second[0], per
    )
    second_e = reduced(rest_e[5])
    mine_d, other = halves(plus(mine_d, coming_d))
    coming_d = across(other, back[1])
    some = all_pairs[1] // 2
    earlier = attend_back(
        lengths_mine, placed, [], first_e, kept_e, [tie(rest_e[0], mine_d), *rest_e[1:3]], dx2_e, (),
        per, (0, some), None, split,
    )
    mine_d, other = halves(plus(mine_d, tie(coming_d, earlier[0])))
    coming_d = across(other, back[2])
    second_d, dx2_e, *earlier = lax.optimization_barrier((second_d, dx2_e, *earlier))
    dx_e, dx_low_e, *grads_first_e = attend_back(
        lengths_mine, placed, [encoder_in], first_e, kept_e, rest_e[:3], tie(dx2_e, mine_d),
        rest_e[3:5], per, (some, all_pairs[1]), tuple(earlier), split,
    )
    mine_e, other = cores(grads_first_e)
    coming_e = across(other, back[0])

    coming_d, bits_d = tie(coming_d, dx_low_e), back[3:]
    for bit in back[1:]:
        mine_e = plus(mine_e, coming_e)
        if coming_d is not None:
            mine_d = plus(mine_d, coming_d)
            coming_d = None
        if bits_d:
            mine_e, mine_d = lax.optimization_barrier((mine_e, mine_d))
            mine_d, other = halves(mine_d)
            coming_d = across(other, bits_d.pop(0))
        mine_e, other = halves(mine_e)
        coming_e = across(other, bit)
    if coming_d is not None:
        mine_d = plus(mine_d, coming_d)
    first_e, first_d = plus(mine_e, coming_e)[0], mine_d[0]

    def summed(of_first, of_second):
        is_first = section == 0
        mine = jnp.where(is_first, of_first.astype(full), of_second.astype(full))
        other = swap(jnp.where(is_first, of_second.astype(low), of_first.astype(low)))
        return mine + other.astype(full)

    total_first = summed(first_e, first_d)

    def both(encoder_part, denoiser_part, received):
        mine = jnp.where(section == 0, encoder_part, denoiser_part)
        received = received.astype(mine.dtype)
        return jnp.where(
            section == 0, jnp.stack([mine, received]), jnp.stack([received, mine])
        ).reshape(1, 2 * length, width)

    activations = both(
        encoded, decoded, tie(swap(jnp.where(section == 0, decoded, encoded)), dx_low_e)
    )
    input_grad = both(
        dx_e, dx_d, tie(swap(jnp.where(section == 0, dx_low_d, dx_low_e)), total_first)
    )
    total_second = summed(tie(second_e, total_first, input_grad, activations), second_d)

    qkv_grad = total_first[: 3 * own_rows].reshape(qkv_weight.shape)
    up_grad = total_second[: 4 * own_rows].reshape(PARTS, own_rows, width)
    up_grad = up_grad.transpose(1, 0, 2).reshape(up_weight.shape)
    down_grad = total_second[4 * own_rows : 8 * own_rows][None]
    out_grad = total_first[3 * own_rows : 4 * own_rows][None]
    norm_all = total_first[4 * own_rows : 4 * own_rows + 4]
    own_features = norm_params.shape[2]
    norm_grad = lax.dynamic_slice(
        norm_all, (0, here * own_features), (4, own_features)
    )[None]
    qkv_new = update(qkv_grad, qkv_weight, qkv_momentum, qkv_average, rate_qkv)
    out_new = update(out_grad, out_weight, out_momentum, out_average, rate_out)
    up_new = update(up_grad, up_weight, up_momentum, up_average, rate_up)
    down_new = update(down_grad, down_weight, down_momentum, down_average, rate_down)
    norm_new = update(norm_grad, norm_params, norm_momentum, norm_average, rate_norm)
    return (
        activations,
        input_grad,
        *qkv_new,
        *out_new,
        *up_new,
        *down_new,
        *norm_new,
        norm_grad[:, 3],
    )


def solution(mesh):
    rows = P("section", "batch", None)
    deep = P("section", None, "batch", None)
    features = P("section", None, "batch")
    return jax.shard_map(
        shards,
        mesh=mesh,
        in_specs=(rows, rows, P("batch", None))
        + (deep,) * 3
        + (rows,) * 9
        + (features,) * 3,
        out_specs=(rows, rows)
        + (deep,) * 4
        + (rows,) * 12
        + (features,) * 4
        + (P("section", "batch"),),
        check_vma=False,
    )
```

```python
import functools
import math

import jax
import jax.numpy as jnp
from jax import lax
from jax.experimental import pallas as pl
from jax.experimental.pallas import tpu as pltpu
from jax.sharding import PartitionSpec as P

HEADS = 8
HEAD_DIM = 64
STEP = 5

eps = 1e-05
momentum_decay = 0.9
rate_qkv = 0.0001
rate_out = 0.01
rate_up = 0.0002
rate_down = 4e-05
rate_norm = 0.0004
neg_large = -1e30

low = jnp.bfloat16
full = jnp.float32

NN = (((1,), (0,)), ((), ()))
NT = (((1,), (1,)), ((), ()))
TN = (((0,), (0,)), ((), ()))

POWER = math.log2(math.e) * HEAD_DIM ** (-0.5)
SCALE = HEAD_DIM ** (-0.5)
GELU_C = math.sqrt(2.0 / math.pi)
GELU_A = 0.044715
LANES = 128
TILE = 16
PARTS = 4
VMEM_LIMIT = 58 * 2**20


def dot(a, b, dims):
    return lax.dot_general(a, b, dims, preferred_element_type=full)


def norm_stats(values):
    centre = values - jnp.mean(values, axis=-1, keepdims=True)
    spread = jnp.mean(centre * centre, axis=-1, keepdims=True)
    scale = lax.rsqrt(spread + eps)
    return centre * scale, scale


def norm_back(hat, scale, gain, grad):
    inner = grad * gain
    back = scale * (
        inner
        - jnp.mean(inner, axis=-1, keepdims=True)
        - hat * jnp.mean(inner * hat, axis=-1, keepdims=True)
    )
    return (
        back,
        jnp.sum(grad * hat, axis=0, keepdims=True),
        jnp.sum(grad, axis=0, keepdims=True),
    )


def norm_rows(refs, rows=slice(None)):
    total = jnp.sum(refs[0][:, rows, :].astype(full), axis=0)
    for ref in refs[1:]:
        total = total + jnp.sum(ref[:, rows, :].astype(full), axis=0)
    return total


def gelu_both(u):
    square = u * u
    t = jnp.tanh(GELU_C * u * (1.0 + GELU_A * square))
    half = 0.5 + 0.5 * t
    slope = half + (0.5 * GELU_C) * u * (1.0 - t * t) * (1.0 + (3.0 * GELU_A) * square)
    return u * half, slope


def masks(lengths_ref, rows):
    place = lax.broadcasted_iota(jnp.int32, (rows, LANES), 0)
    lane = lax.broadcasted_iota(jnp.int32, (rows, LANES), 1)
    first = lengths_ref[0]
    second = first + lengths_ref[1]
    third = second + lengths_ref[2]
    item = (
        (place >= first).astype(jnp.int32)
        + (place >= second).astype(jnp.int32)
        + (place >= third).astype(jnp.int32)
    )
    own = item == lane
    query = jnp.where(own, neg_large, 0.0).astype(low)
    key = jnp.where(own | (lane > 3), 0.0, 1.0).astype(low)
    return query, key


def added(refs, rows=slice(None)):
    total = refs[0][rows].astype(full)
    for ref in refs[1:]:
        total = total + ref[rows].astype(full)
    return total


def put_in_order(order_ref, weight_refs, ordered, per, pieces):
    def put(b, j, rows):
        ordered[j, b * per : (b + 1) * per, :] = rows

    if len(weight_refs) == 1:
        for b in range(weight_refs[0].shape[0]):
            for j in range(pieces):
                put(b, j, weight_refs[0][order_ref[b], j * per : (j + 1) * per, :])
        return
    half = weight_refs[0].shape[0]
    for b in range(0, 2 * half, 2):
        places = order_ref[b], order_ref[b + 1]
        even = places[0] < half
        place = jnp.where(even, places[0], places[1])
        for j in range(pieces):
            own, other = (ref[place, j * per : (j + 1) * per, :] for ref in weight_refs)
            put(b, j, jnp.where(even, own, other))
            put(b + 1, j, jnp.where(even, other, own))


def put_blocks(order_ref, first, grad_refs, rows, values):
    if len(grad_refs) == 1:
        for b in range(values.shape[0]):
            grad_refs[0][order_ref[first + b], rows, :] = values[b]
        return
    half = grad_refs[0].shape[0]
    for b in range(0, values.shape[0], 2):
        places = order_ref[first + b], order_ref[first + b + 1]
        even = places[0] < half
        place = jnp.where(even, places[0], places[1])
        grad_refs[0][place, rows, :] = jnp.where(even, values[b], values[b + 1])
        grad_refs[1][place, rows, :] = jnp.where(even, values[b + 1], values[b])


def put_everywhere(grad_refs, rows, values):
    for ref in grad_refs:
        ref[:, rows, :] = jnp.broadcast_to(values[None], (ref.shape[0],) + values.shape)


def grad_shapes(devices, rows, width, split):
    if split:
        return [jax.ShapeDtypeStruct((devices // 2, rows, width), low)] * 2
    return [jax.ShapeDtypeStruct((devices, rows, width), low)]


def attend_kernel(count, parts, per, block, *refs):
    lengths_ref, order_ref, refs = refs[0], refs[1], refs[2:]
    inputs, refs = refs[:count], refs[count:]
    weights_in, refs = refs[:parts], refs[parts:]
    q_out, k_out, v_out, o_ref, log_ref, *refs = refs
    weight_refs, refs = refs[:parts], refs[parts:]
    a_s, vt_s, qm_s, km_s, w_s, q_ref, k_ref, v_ref, in_sems, out_sems = refs
    length, width = q_ref.shape
    arriving = [
        pltpu.make_async_copy(source, target, in_sems.at[i])
        for i, (source, target) in enumerate(zip(weights_in, weight_refs))
    ]
    for copy in arriving:
        copy.start()
    hat, _ = norm_stats(added(inputs))
    qm_s[...], km_s[...] = masks(lengths_ref, length)
    for copy in arriving:
        copy.wait()
    norm_vals = norm_rows(weight_refs, slice(4 * per, 4 * per + TILE))
    put_in_order(order_ref, weight_refs, w_s, per, 3)

    def weight(j):
        return w_s[j]

    a_s[...] = (hat * norm_vals[0:1] + norm_vals[1:2]).astype(low)
    q_ref[...] = dot(a_s[...], weight(0), NN).astype(low)
    k_ref[...] = dot(a_s[...], weight(1), NN).astype(low)
    v_ref[...] = dot(a_s[...], weight(2), NN).astype(low)
    leaving = [
        pltpu.make_async_copy(source, target, out_sems.at[i])
        for i, (source, target) in enumerate(((q_ref, q_out), (k_ref, k_out), (v_ref, v_out)))
    ]
    for copy in leaving:
        copy.start()
    vt_s[...] = v_ref[...].T
    lanes = lax.broadcasted_iota(jnp.int32, (1, LANES), 1)
    zero = jnp.zeros((), low)

    jobs = [
        (p, h, b)
        for p in range(width // LANES)
        for h in range(2)
        for b in range(length // block)
    ]

    def scores(job):
        p, h, b = job
        cols = slice(p * LANES, (p + 1) * LANES)
        rows = slice(b * block, (b + 1) * block)
        queries = jnp.where(lanes // HEAD_DIM == h, q_ref[rows, cols], zero)
        return dot(
            jnp.concatenate([k_ref[:, cols], km_s[...]], axis=1),
            jnp.concatenate([queries, qm_s[rows, :]], axis=1),
            NT,
        )

    ahead = scores(jobs[0])
    for i, (p, h, b) in enumerate(jobs):
        s = ahead
        if i + 1 < len(jobs):
            ahead = scores(jobs[i + 1])
        head = 2 * p + h
        rows = slice(head * HEAD_DIM, (head + 1) * HEAD_DIM)
        cols = slice(b * block, (b + 1) * block)
        top = jnp.max(s, axis=0, keepdims=True) * POWER
        raised = jnp.exp2(s * POWER - top)
        total = jnp.sum(raised, axis=0, keepdims=True)
        mixed = dot(vt_s[rows, :], raised.astype(low), NN)
        o_ref[rows, cols] = (mixed * (1.0 / total)).astype(low)
        log_ref[head : head + 1, cols] = top + jnp.log2(total)
    for copy in leaving:
        copy.wait()


def attend(lengths, order, inputs, weights, per):
    length, width = inputs[0].shape
    shape = jax.ShapeDtypeStruct
    flops = 2 * length * width * width * 3 + 8 * length * length * width
    return pl.pallas_call(
        functools.partial(attend_kernel, len(inputs), len(weights), per, min(512, length)),
        out_shape=(
            shape((length, width), low),
            shape((length, width), low),
            shape((length, width), low),
            shape((width, length), low),
            shape((HEADS, length), full),
        ),
        in_specs=[pl.BlockSpec(memory_space=pltpu.SMEM)] * 2
        + [pl.BlockSpec(memory_space=pltpu.VMEM)] * len(inputs)
        + [pl.BlockSpec(memory_space=pl.ANY)] * len(weights),
        out_specs=[pl.BlockSpec(memory_space=pl.ANY)] * 3
        + [pl.BlockSpec(memory_space=pltpu.VMEM)] * 2,
        scratch_shapes=[pltpu.VMEM(array.shape, low) for array in weights]
        + [
            pltpu.VMEM((length, width), low),
            pltpu.VMEM((width, length), low),
            pltpu.VMEM((length, LANES), low),
            pltpu.VMEM((length, LANES), low),
            pltpu.VMEM((3, width, width), low),
        ]
        + [pltpu.VMEM((length, width), low)] * 3
        + [pltpu.SemaphoreType.DMA((len(weights),)), pltpu.SemaphoreType.DMA((3,))],
        compiler_params=pltpu.CompilerParams(vmem_limit_bytes=VMEM_LIMIT),
        cost_estimate=pl.CostEstimate(
            flops=2 * flops, bytes_accessed=8 * 2**20, transcendentals=HEADS * length * length
        ),
        name="attend",
    )(lengths, order, *inputs, *weights)


def heads_back(refs, scratch, pairs, block):
    q_ref, k_ref, v_ref, do_ref, dot_ref, log_ref, sum_ref, dqt_ref, dkt_ref, dvt_ref = refs
    qt_s, kt_s, dk_s, dv_s, qm_s, km_s = scratch
    length = q_ref.shape[0]
    blocks = length // block
    qt_s[...] = q_ref[...].T
    kt_s[...] = k_ref[...].T
    lanes = lax.broadcasted_iota(jnp.int32, (1, LANES), 1)
    zero = jnp.zeros((), low)

    def pair(p, carry):
        off = pl.multiple_of(p * LANES, LANES)
        wide = pl.ds(off, LANES)
        keys = jnp.concatenate([k_ref[:, wide], km_s[...]], axis=1)
        jobs = [(h, b) for h in range(2) for b in range(blocks)]

        def scores(job):
            h, b = job
            rows = slice(b * block, (b + 1) * block)
            keep = lanes // HEAD_DIM == h
            queries = jnp.where(keep, q_ref[rows, wide], zero)
            outer = jnp.where(keep, do_ref[rows, wide], zero)
            return (
                dot(keys, jnp.concatenate([queries, qm_s[rows, :]], axis=1), NT),
                dot(v_ref[:, wide], outer, NT),
            )

        ahead = scores(jobs[0])
        for i, (h, b) in enumerate(jobs):
            s, dp = ahead
            if i + 1 < len(jobs):
                ahead = scores(jobs[i + 1])
            rows = pl.ds(pl.multiple_of(off + h * HEAD_DIM, HEAD_DIM), HEAD_DIM)
            cols = slice(b * block, (b + 1) * block)
            head = pl.ds(2 * (pairs[0] + p) + h, 1)
            prob = jnp.exp2(s * POWER - log_ref[head, cols])
            ds = (prob * (dp - sum_ref[head, cols])).astype(low)
            prob = prob.astype(low)
            dv = dot(dot_ref[rows, cols], prob, NT)
            dk = dot(qt_s[rows, cols], ds, NT)
            dqt_ref[rows, cols] = (dot(kt_s[rows, :], ds, NN) * SCALE).astype(low)
            if b > 0:
                dv = dv_s[...] + dv
                dk = dk_s[...] + dk
            if b < blocks - 1:
                dv_s[...] = dv
                dk_s[...] = dk
            else:
                dvt_ref[rows, :] = dv.astype(low)
                dkt_ref[rows, :] = (dk * SCALE).astype(low)
        return carry

    lax.fori_loop(0, pairs[1] - pairs[0], pair, 0)


def attend_back_kernel(count, parts, per, block, pairs, last, *refs):
    lengths_ref, refs = refs[0], refs[1:]
    heads, refs = refs[:7], refs[7:]
    if last:
        before = 3 if pairs[0] > 0 else 0
        order_ref, refs = refs[0], refs[1:]
        earlier, refs = refs[:before], refs[before:]
        inputs, refs = refs[:count], refs[count:]
        weight_refs, refs = refs[:parts], refs[parts:]
        dx2_ref, outg_ref, norms_ref, dx_ref, dxl_ref, *refs = refs
        grads_at = len(refs) - 10
        grad_refs, grads_s, scratch = refs[:grads_at], refs[grads_at : grads_at + 3], refs[grads_at + 3 :]
        *scratch, w_s = scratch
    else:
        grads_s, scratch = refs[:3], refs[3:]
    length = heads[0].shape[0]
    scratch[4][...], scratch[5][...] = masks(lengths_ref, length)
    heads_back(heads + tuple(grads_s), scratch, pairs, block)
    if not last:
        return
    width = w_s.shape[1]
    put_in_order(order_ref, weight_refs, w_s, per, 3)
    norm_vals = norm_rows(weight_refs, slice(4 * per, 4 * per + TILE))
    hat, scale = norm_stats(added(inputs))
    a = (hat * norm_vals[0:1] + norm_vals[1:2]).astype(low)
    da = jnp.zeros((length, width), full)
    for j in range(3):
        if before:
            grads = jnp.concatenate([earlier[j][...].T, grads_s[j][...].T], axis=1)
        else:
            grads = grads_s[j][...].T
        da = da + dot(grads, w_s[j], NT)
        put_blocks(
            order_ref,
            0,
            grad_refs,
            slice(j * per, (j + 1) * per),
            dot(a, grads, TN).astype(low).reshape(width // per, per, width),
        )
    back, gain, shift = norm_back(hat, scale, norm_vals[0:1], da)
    dx = dx2_ref[...] + back
    dx_ref[...] = dx
    dxl_ref[...] = dx.astype(low)
    put_blocks(
        order_ref,
        0,
        grad_refs,
        slice(3 * per, 4 * per),
        outg_ref[...].reshape(width // per, per, width),
    )
    tail = jnp.concatenate(
        [gain, shift, norms_ref[...], jnp.zeros((TILE - 4, width), full)], axis=0
    )
    put_everywhere(grad_refs, slice(4 * per, 4 * per + TILE), tail.astype(low))


def head_specs(length, pairs):
    wide = (pairs[1] - pairs[0]) * LANES
    at = pairs[0] * LANES // wide
    assert at * wide == pairs[0] * LANES
    columns = pl.BlockSpec((length, wide), lambda i: (0, at))
    return [columns] * 4 + [pl.BlockSpec((wide, length), lambda i: (at, 0))] + [
        pl.BlockSpec(memory_space=pltpu.VMEM)] * 2


def head_scratch(length, pairs):
    wide = (pairs[1] - pairs[0]) * LANES
    return (
        [pltpu.VMEM((wide, length), low)] * 2
        + [pltpu.VMEM((HEAD_DIM, length), full)] * 2
        + [pltpu.VMEM((length, LANES), low)] * 2
    )


def attend_back(
    lengths, order, inputs, weights, kept, outer, dx2, others, per, pairs, earlier, split
):
    q, k, v, _, logs = kept
    outer, outer_t, sums = outer
    length, width = q.shape
    shape = jax.ShapeDtypeStruct
    count = pairs[1] - pairs[0]
    wide = count * LANES
    devices = width // per
    last = earlier is not None
    flops = 20 * length * length * wide + (12 * length * width * width if last else 0)
    whole = pl.BlockSpec(memory_space=pltpu.VMEM)
    smem = pl.BlockSpec(memory_space=pltpu.SMEM)
    arrays = [lengths, q, k, v, outer, outer_t, logs, sums]
    specs = [smem] + head_specs(length, pairs)
    transposed = [shape((wide, length), low)] * 3
    scratch = head_scratch(length, pairs)
    if last:
        arrays += [order, *earlier, *inputs, *weights, dx2, *others]
        specs += [smem] + [whole] * (len(earlier) + len(inputs) + len(weights) + 3)
        outs = [shape((length, width), full), shape((length, width), low)]
        outs += grad_shapes(devices, 4 * per + TILE, width, split)
        scratch = [pltpu.VMEM((wide, length), low)] * 3 + scratch
        scratch += [pltpu.VMEM((3, width, width), low)]
    else:
        outs = transposed
    return pl.pallas_call(
        functools.partial(
            attend_back_kernel, len(inputs), len(weights), per, min(256, length), pairs, last
        ),
        grid=(1,),
        out_shape=tuple(outs),
        in_specs=specs,
        out_specs=[whole] * len(outs),
        scratch_shapes=scratch,
        compiler_params=pltpu.CompilerParams(vmem_limit_bytes=VMEM_LIMIT),
        cost_estimate=pl.CostEstimate(
            flops=2 * flops,
            bytes_accessed=16 * 2**20,
            transcendentals=2 * count * length * length,
        ),
        name="attend_back" if last else "attend_back_part",
    )(*arrays)


def middle_start(inputs, o_ref, out, norm_refs):
    norm_vals = norm_rows(norm_refs)
    x2 = added(inputs) + dot(o_ref[...], out, TN)
    hat, _ = norm_stats(x2)
    return x2, (hat * norm_vals[2:3] + norm_vals[3:4]).astype(low)


def ffn_forward_kernel(count, parts, block, *refs):
    order_ref, refs = refs[0], refs[1:]
    inputs, refs = refs[:count], refs[count:]
    norm_refs, out_refs, refs = refs[:parts], refs[parts : 2 * parts], refs[2 * parts :]
    (
        o_ref, up_ref, down_ref,
        x2_ref, h_ref, slope_ref, y_ref,
        c_s, acc_s, out_s,
    ) = refs
    length, width = x2_ref.shape
    j = pl.program_id(0)

    @pl.when(j == 0)
    def _():
        put_in_order(order_ref, out_refs, out_s, out_refs[0].shape[1], 1)
        x2, c = middle_start(inputs, o_ref, out_s[0], norm_refs)
        x2_ref[...] = x2
        acc_s[...] = x2
        c_s[...] = c

    up = up_ref[...].reshape(width, width)
    down = down_ref[...].reshape(width, width)
    spans = [slice(i, i + block) for i in range(0, length, block)]
    ahead = dot(c_s[spans[0], :], up, NN)
    for i, rows in enumerate(spans):
        u = ahead
        if i + 1 < len(spans):
            ahead = dot(c_s[spans[i + 1], :], up, NN)
        h, slope = gelu_both(u)
        h = h.astype(low)
        h_ref[rows, :] = h
        slope_ref[rows, :] = slope.astype(low)
        acc_s[rows, :] += dot(h, down, NN)

    @pl.when(j == pl.num_programs(0) - 1)
    def _():
        y_ref[...] = acc_s[...].astype(low)


def piece_specs(devices, per, width):
    return [
        pl.BlockSpec((devices, per, width), lambda j: (0, j, 0)),
        pl.BlockSpec((devices // PARTS, 4 * per, width), lambda j: (j, 1, 0)),
    ]


def first_specs(first, per):
    shapes = [array.shape for array in first]
    return [
        pl.BlockSpec((count, TILE, width), lambda j: (0, 4 * per // TILE, 0))
        for count, _, width in shapes
    ] + [
        pl.BlockSpec((count, per, width), lambda j: (0, 3, 0)) for count, _, width in shapes
    ]


def constant(*dims):
    return pl.BlockSpec(dims, lambda j: (0,) * len(dims))


def ffn_forward(order, inputs, mixed, first, second, per):
    length, width = inputs[0].shape
    devices = width // per
    shape = jax.ShapeDtypeStruct
    hidden = PARTS * width
    return pl.pallas_call(
        functools.partial(ffn_forward_kernel, len(inputs), len(first), min(256, length)),
        grid=(PARTS,),
        out_shape=(
            shape((length, width), full),
            shape((length, hidden), low),
            shape((length, hidden), low),
            shape((length, width), low),
        ),
        in_specs=[pl.BlockSpec(memory_space=pltpu.SMEM)]
        + [constant(length, width)] * len(inputs)
        + first_specs(first, per)
        + [constant(width, length)]
        + piece_specs(devices, per, width),
        out_specs=[
            constant(length, width),
            pl.BlockSpec((length, width), lambda j: (0, j)),
            pl.BlockSpec((length, width), lambda j: (0, j)),
            constant(length, width),
        ],
        scratch_shapes=[
            pltpu.VMEM((length, width), low),
            pltpu.VMEM((length, width), full),
            pltpu.VMEM((1, width, width), low),
        ],
        compiler_params=pltpu.CompilerParams(vmem_limit_bytes=VMEM_LIMIT),
        cost_estimate=pl.CostEstimate(
            flops=2 * length * width * width * 9,
            bytes_accessed=16 * 2**20,
            transcendentals=length * hidden,
        ),
        name="ffn_forward",
    )(order, *inputs, *first, *first, mixed, second, second)


def ffn_back_kernel(count, parts, per, fused, block, *refs):
    order_ref, refs = refs[0], refs[1:]
    norm_refs, out_refs, refs = refs[:parts], refs[parts : 2 * parts], refs[2 * parts :]
    if fused:
        inputs, refs = refs[:count], refs[count:]
        (
            o_ref, cot_ref, up_ref, down_ref,
            y_ref, dx2_ref, do_ref, dot_ref, sum_ref, outg_ref, norms_ref, grad_ref,
            out_s, c_s, dc_s, h_s, du_s, x2_ref, acc_s, down_s, up_s, sems,
        ) = refs
        dyb_ref = cot_ref
    else:
        (
            x2_ref, h_ref, slope_ref, later_ref,
            o_ref, cot_ref, up_ref, down_ref,
            dx2_ref, do_ref, dot_ref, sum_ref, outg_ref, norms_ref, grad_ref,
            out_s, c_s, dc_s, h_s, du_s, dyb_ref, down_s, up_s, sems,
        ) = refs
        h_s = h_ref
    length, width = dx2_ref.shape
    devices = width // per
    j = pl.program_id(0)

    def cot(rows):
        dy = cot_ref[rows, :].astype(full)
        if not fused:
            dy = dy + later_ref[rows, :].astype(full)
        return dy

    everything = slice(0, length)

    @pl.when(j == 0)
    def _():
        put_in_order(order_ref, out_refs, out_s, per, 1)
        if fused:
            x2, c = middle_start(inputs, o_ref, out_s[0], norm_refs)
            x2_ref[...] = x2
            acc_s[...] = x2
        else:
            norm_vals = norm_rows(norm_refs)
            hat, _ = norm_stats(x2_ref[...])
            c = (hat * norm_vals[2:3] + norm_vals[3:4]).astype(low)
            dyb_ref[...] = cot(everything).astype(low)
        c_s[...] = c
        dc_s[...] = jnp.zeros((length, width), full)

    up = up_ref[...].reshape(width, width)
    down = down_ref[...].reshape(width, width)
    spans = [slice(i, i + block) for i in range(0, length, block)]

    def products(rows):
        dh = dot(dyb_ref[rows, :], down, NT)
        return (dot(c_s[rows, :], up, NN) if fused else None), dh

    ahead = products(spans[0])
    for i, rows in enumerate(spans):
        u, dh = ahead
        if i + 1 < len(spans):
            ahead = products(spans[i + 1])
        if fused:
            h, slope = gelu_both(u)
            h = h.astype(low)
            h_s[rows, :] = h
            acc_s[rows, :] += dot(h, down, NN)
        else:
            slope = slope_ref[rows, :].astype(full)
        du = (slope * dh).astype(low)
        du_s[rows, :] = du
        dc_s[rows, :] += dot(du, up, NT)
    some = devices // PARTS

    def leaving(step):
        down_rows = grad_ref.at[pl.ds(step * some, some), pl.ds(4 * per, 4 * per), :]
        up_rows = grad_ref.at[:, pl.ds(pl.multiple_of(step * per, TILE), per), :]
        return (
            pltpu.make_async_copy(down_s.at[step], down_rows, sems.at[0, step]),
            pltpu.make_async_copy(up_s.at[step], up_rows, sems.at[1, step]),
        )

    down_s[j] = dot(h_s[...], dyb_ref[...], TN).astype(low).reshape(some, 4 * per, width)
    leaving(j)[0].start()
    up_s[j] = dot(c_s[...], du_s[...], TN).astype(low).reshape(devices, per, width)
    leaving(j)[1].start()

    @pl.when(j == pl.num_programs(0) - 1)
    def _():
        if fused:
            y_ref[...] = acc_s[...].astype(low)
        norm_vals = norm_rows(norm_refs)
        hat, scale = norm_stats(x2_ref[...])
        back, gain, shift = norm_back(hat, scale, norm_vals[2:3], dc_s[...])
        dx2 = cot(everything) + back
        dx2_ref[...] = dx2
        dab = dx2.astype(low)
        out = out_s[0]
        outg_ref[...] = dot(o_ref[...], dab, NN).astype(low)
        do_ref[...] = dot(dab, out, NT).astype(low)
        outer = dot(out, dab, NT).astype(low)
        dot_ref[...] = outer
        product = outer.astype(full) * o_ref[...].astype(full)
        sum_ref[...] = jnp.sum(product.reshape(HEADS, HEAD_DIM, length), axis=1)
        norms_ref[0:1, :] = gain
        norms_ref[1:2, :] = shift
        for step in range(PARTS):
            for copy in leaving(step):
                copy.wait()


def ffn_back(order, inputs, kept, mixed, cot, first, second, per):
    fused = kept is None
    length, width = cot.shape
    devices = width // per
    shape = jax.ShapeDtypeStruct
    hidden = PARTS * width
    column = pl.BlockSpec((length, width), lambda j: (0, j))
    ahead = [constant(length, width)] * len(inputs) if fused else [
        constant(length, width), column, column, constant(length, width)]
    outs = [
        (shape((length, width), full), constant(length, width)),
        (shape((length, width), low), constant(length, width)),
        (shape((width, length), low), constant(width, length)),
        (shape((HEADS, length), full), constant(HEADS, length)),
        (shape((width, width), low), constant(width, width)),
        (shape((2, width), full), constant(2, width)),
        (shape(second.shape, low), pl.BlockSpec(memory_space=pl.ANY)),
    ]
    scratch = [
        pltpu.VMEM((1, width, width), low),
        pltpu.VMEM((length, width), low),
        pltpu.VMEM((length, width), full),
        pltpu.VMEM((length, width) if fused else (TILE, LANES), low),
        pltpu.VMEM((length, width), low),
    ]
    if fused:
        outs = [(shape((length, width), low), constant(length, width))] + outs
        scratch += [pltpu.VMEM((length, width), full)] * 2
    else:
        scratch += [pltpu.VMEM((length, width), low)]
    scratch += [
        pltpu.VMEM((PARTS, devices // PARTS, 4 * per, width), low),
        pltpu.VMEM((PARTS, devices, per, width), low),
        pltpu.SemaphoreType.DMA((2, PARTS)),
    ]
    return pl.pallas_call(
        functools.partial(
            ffn_back_kernel, len(inputs), len(first), per, fused, min(256, length)
        ),
        grid=(PARTS,),
        out_shape=tuple(o[0] for o in outs),
        in_specs=[pl.BlockSpec(memory_space=pltpu.SMEM)]
        + first_specs(first, per)
        + ahead
        + [constant(width, length), constant(length, width)]
        + piece_specs(devices, per, width),
        out_specs=tuple(o[1] for o in outs),
        scratch_shapes=scratch,
        compiler_params=pltpu.CompilerParams(vmem_limit_bytes=VMEM_LIMIT),
        cost_estimate=pl.CostEstimate(
            flops=2 * length * width * width * (28 if fused else 19),
            bytes_accessed=24 * 2**20,
            transcendentals=length * hidden if fused else 0,
        ),
        name="ffn_both" if fused else "ffn_back",
    )(order, *first, *first, *(inputs if fused else kept), mixed, cot, second, second)


def across(block, bit):
    devices = lax.axis_size("batch")
    return lax.ppermute(block, "batch", [(i, i ^ bit) for i in range(devices)])


def pick(blocks, index, axis=0):
    return lax.dynamic_index_in_dim(blocks, index, axis, keepdims=False)


def stages():
    return list(range(lax.axis_size("batch").bit_length() - 1))[::-1]


def places(device):
    flips = device ^ lax.axis_index("batch")
    place, weight = jnp.zeros_like(device), 1
    for bit in stages():
        place = place + ((flips >> bit) & 1) * weight
        weight *= 2
    return place


def flipped(blocks, axis, bit):
    halves = [lax.index_in_dim(blocks, i, axis) for i in range(2)]
    is_set = (lax.axis_index("batch") >> bit) & 1 == 1
    return jnp.where(is_set, jnp.concatenate(halves[::-1], axis), blocks)


def by_device(blocks):
    filled = stages()
    bits = len(filled)
    rest = tuple(range(bits, bits + blocks.ndim - 1))
    shape = blocks.shape
    blocks = blocks.reshape((2,) * bits + shape[1:])
    blocks = blocks.transpose(
        tuple(bits - 1 - filled.index(b) for b in range(bits - 1, -1, -1)) + rest
    )
    for b in range(bits):
        blocks = flipped(blocks, bits - 1 - b, b)
    return blocks.reshape(shape)


def by_place(blocks):
    filled = stages()
    bits = len(filled)
    rest = tuple(range(bits, bits + blocks.ndim - 1))
    shape = blocks.shape
    blocks = blocks.reshape((2,) * bits + shape[1:])
    for b in range(bits):
        blocks = flipped(blocks, bits - 1 - b, b)
    blocks = blocks.transpose(tuple(bits - 1 - b for b in filled[::-1]) + rest)
    return blocks.reshape(shape)


def tie(value, *after):
    return lax.optimization_barrier((value,) + after)[0]


def joined(held, received):
    return jnp.concatenate([held, received], axis=0)


def halves(blocks):
    count = blocks.shape[0] // 2
    return blocks[:count], blocks[count:]


def plus(mine, received):
    return (mine.astype(full) + received.astype(full)).astype(low)


def widen(gathered, sizes, times):
    if times == 1:
        return gathered
    devices, _, width = gathered.shape
    grouped = gathered.reshape(devices // times, times, -1, width)
    parts, at = [], 0
    for size in sizes:
        parts.append(
            grouped[:, :, at : at + size].reshape(devices // times, times * size, width)
        )
        at += size
    return jnp.concatenate(parts, axis=1)


def narrow(grads, sizes, times):
    if times == 1:
        return grads
    groups, _, width = grads.shape
    parts, at = [], 0
    for size in sizes:
        parts.append(
            grads[:, at : at + times * size].reshape(groups * times, size, width)
        )
        at += times * size
    rest = grads[:, at:]
    parts.append(jnp.repeat(rest, times, axis=0))
    return jnp.concatenate(parts, axis=1)


def update(gradient, weight, momentum, average, step_rate):
    new_momentum = momentum_decay * momentum + gradient
    new_weight = weight - step_rate * (gradient + momentum_decay * new_momentum)
    new_average = average + (new_weight - average) / (STEP + 1.0)
    return (gradient, new_momentum, new_weight, new_average)


def shards(
    tokens,
    cotangent,
    lengths,
    qkv_weight,
    qkv_momentum,
    qkv_average,
    out_weight,
    out_momentum,
    out_average,
    up_weight,
    up_momentum,
    up_average,
    down_weight,
    down_momentum,
    down_average,
    norm_params,
    norm_momentum,
    norm_average,
):
    section = lax.axis_index("section")
    here = lax.axis_index("batch")
    width = tokens.shape[2]
    length = tokens.shape[1] // lengths.shape[0]
    assert lengths.shape[0] == lax.axis_size("section") == 2
    own_rows = out_weight.shape[1]
    times = max(1, TILE // own_rows)
    per = own_rows * times
    first_sizes = (own_rows,) * 4
    second_sizes = (own_rows,) * PARTS + (PARTS * own_rows,)

    def swap(block):
        return lax.ppermute(block, "section", [(0, 1), (1, 0)])

    def sorted_pair(mine, other):
        is_first = section == 0
        return jnp.where(is_first, mine, other), jnp.where(is_first, other, mine)

    lengths_mine = pick(lengths, section)
    norm_table = lax.dynamic_update_slice(
        jnp.zeros((TILE, width), low),
        norm_params[0].astype(low),
        (0, here * norm_params.shape[2]),
    )
    pack_first = jnp.concatenate(
        [
            qkv_weight[0].astype(low).reshape(-1, width),
            out_weight[0].astype(low),
            norm_table,
        ],
        axis=0,
    )
    up_low = up_weight[0].astype(low).reshape(own_rows, PARTS, width)
    pack_second = jnp.concatenate(
        [
            up_low.transpose(1, 0, 2).reshape(-1, width),
            down_weight[0].astype(low),
        ],
        axis=0,
    )
    order = places(jnp.arange(lax.axis_size("batch"), dtype=jnp.int32))
    steps = stages()
    split = times == 1

    pair_second = sorted_pair(pack_second, swap(pack_second))
    received = swap(pack_first)
    piece_e, piece_d = sorted_pair(pack_first, received)
    token_rows = tokens[0].reshape(2, length, width)
    cot_rows = cotangent[0].reshape(2, length, width)
    token_other = swap(tie(pick(token_rows, 1 - section), received))
    cot_other = swap(tie(pick(cot_rows, 1 - section), token_other))

    def gathered(held, bits):
        flips = [sum(((d >> i) & 1) << b for i, b in enumerate(bits)) for d in range(1, 1 << len(bits))]
        return [across(held, flip) for flip in flips]

    high = steps[:-2]
    wide = [high[i : i + 2] for i in range(0, len(high), 2)]
    held_e = piece_e[None]
    for bits in wide:
        held_e = jnp.concatenate([held_e] + gathered(held_e, bits))
    held_d = tie(piece_d[None], held_e)
    for bits in wide:
        held_d = jnp.concatenate([held_d] + gathered(held_d, bits))
    held_e = joined(tie(held_e, token_other), across(held_e, 1 << steps[-2]))
    other_e = across(held_e, 1 << steps[-1])
    coming = across(held_d, 1 << steps[-2])

    def whole_first(held, other):
        if times == 1:
            return (held, other)
        held = by_device(joined(held, other))
        body = widen(held[:, : 4 * own_rows], first_sizes, times)
        table = held[:, 4 * own_rows :].reshape(-1, times, TILE, width)
        return (jnp.concatenate([body, jnp.sum(table, axis=1)], axis=1),)

    def whole_second(piece):
        gathered = lax.all_gather(piece, "batch", axis=0, tiled=False)
        return widen(gathered, second_sizes, times)

    second = [whole_second(piece) for piece in pair_second]
    natural = jnp.arange(second[0].shape[0], dtype=jnp.int32)
    placed = order if split else natural

    encoder_in = jnp.where(section == 0, pick(token_rows, section), token_other)
    denoiser_in = jnp.where(section == 0, token_other, pick(token_rows, section))
    encoder_cot, denoiser_cot = sorted_pair(pick(cot_rows, section), cot_other)
    encoder_in, denoiser_in, encoder_cot, denoiser_cot = lax.optimization_barrier(
        (encoder_in, denoiser_in, encoder_cot, denoiser_cot)
    )
    first_e = whole_first(held_e, other_e)
    kept_e = attend(lengths_mine, placed, [encoder_in], first_e, per)
    held_d = joined(held_d, tie(coming, kept_e[4]))
    other_d = across(held_d, 1 << steps[-1])
    x2_e, hidden_e, slope_e, encoded = ffn_forward(
        placed, [encoder_in], tie(kept_e[3], held_d), first_e, second[0], per
    )
    first_d = whole_first(held_d, tie(other_d, encoded))
    inputs_d = [denoiser_in, encoded]
    kept_d = attend(lengths_mine, placed, inputs_d, first_d, per)
    decoded, dx2_d, *rest_d = ffn_back(
        placed, inputs_d, None, kept_d[3], denoiser_cot, first_d, second[1], per
    )

    def reduced(grads):
        return lax.psum_scatter(
            narrow(grads, second_sizes, times).reshape(-1, width),
            "batch",
            scatter_dimension=0,
            tiled=True,
        )

    def cores(grads):
        if split:
            return grads
        return halves(by_place(narrow(grads[0], first_sizes, times)))

    back = [1 << bit for bit in steps[::-1]]
    second_d = reduced(rest_d[5])
    all_pairs = (0, width // LANES)
    dx_d, dx_low_d, *grads_first_d = attend_back(
        lengths_mine, placed, inputs_d, first_d, kept_d, rest_d[:3], dx2_d, rest_d[3:5], per,
        all_pairs, (), split,
    )
    mine_d, other = cores(grads_first_d)
    coming_d = across(other, back[0])
    dx2_e, *rest_e = ffn_back(
        placed, [], (x2_e, hidden_e, slope_e, dx_low_d), kept_e[3], encoder_cot, first_e, second[0], per
    )
    second_e = reduced(rest_e[5])
    mine_d, other = halves(plus(mine_d, coming_d))
    coming_d = across(other, back[1])
    some = all_pairs[1] // 2
    earlier = attend_back(
        lengths_mine, placed, [], first_e, kept_e, [tie(rest_e[0], mine_d), *rest_e[1:3]], dx2_e, (),
        per, (0, some), None, split,
    )
    mine_d, other = halves(plus(mine_d, tie(coming_d, earlier[0])))
    coming_d = across(other, back[2])
    second_d, dx2_e, *earlier = lax.optimization_barrier((second_d, dx2_e, *earlier))
    dx_e, dx_low_e, *grads_first_e = attend_back(
        lengths_mine, placed, [encoder_in], first_e, kept_e, rest_e[:3], tie(dx2_e, mine_d),
        rest_e[3:5], per, (some, all_pairs[1]), tuple(earlier), split,
    )
    mine_e, other = cores(grads_first_e)
    coming_e = across(other, back[0])

    coming_d, bits_d = tie(coming_d, dx_low_e), back[3:]
    for bit in back[1:-2]:
        mine_e = plus(mine_e, coming_e)
        if coming_d is not None:
            mine_d = plus(mine_d, coming_d)
            coming_d = None
        if bits_d:
            mine_e, mine_d = lax.optimization_barrier((mine_e, mine_d))
            mine_d, other = halves(mine_d)
            coming_d = across(other, bits_d.pop(0))
        mine_e, other = halves(mine_e)
        coming_e = across(other, bit)
    if coming_d is not None:
        mine_d = plus(mine_d, coming_d)
    mine_e = plus(mine_e, coming_e)
    flips = (back[-1], back[-2], back[-1] | back[-2])
    first_e, first_d = mine_e[0].astype(full), mine_d[0]
    for i, flip in enumerate(flips):
        first_e = first_e + across(mine_e[i + 1], flip).astype(full)

    def summed(of_first, of_second):
        is_first = section == 0
        mine = jnp.where(is_first, of_first.astype(full), of_second.astype(full))
        other = swap(jnp.where(is_first, of_second.astype(low), of_first.astype(low)))
        return mine + other.astype(full)

    total_first = summed(first_e, first_d)

    def both(encoder_part, denoiser_part, received):
        mine = jnp.where(section == 0, encoder_part, denoiser_part)
        received = received.astype(mine.dtype)
        return jnp.where(
            section == 0, jnp.stack([mine, received]), jnp.stack([received, mine])
        ).reshape(1, 2 * length, width)

    activations = both(
        encoded, decoded, tie(swap(jnp.where(section == 0, decoded, encoded)), dx_low_e)
    )
    input_grad = both(
        dx_e, dx_d, tie(swap(jnp.where(section == 0, dx_low_d, dx_low_e)), total_first)
    )
    total_second = summed(tie(second_e, total_first, input_grad, activations), second_d)

    qkv_grad = total_first[: 3 * own_rows].reshape(qkv_weight.shape)
    up_grad = total_second[: 4 * own_rows].reshape(PARTS, own_rows, width)
    up_grad = up_grad.transpose(1, 0, 2).reshape(up_weight.shape)
    down_grad = total_second[4 * own_rows : 8 * own_rows][None]
    out_grad = total_first[3 * own_rows : 4 * own_rows][None]
    norm_all = total_first[4 * own_rows : 4 * own_rows + 4]
    own_features = norm_params.shape[2]
    norm_grad = lax.dynamic_slice(
        norm_all, (0, here * own_features), (4, own_features)
    )[None]
    qkv_new = update(qkv_grad, qkv_weight, qkv_momentum, qkv_average, rate_qkv)
    out_new = update(out_grad, out_weight, out_momentum, out_average, rate_out)
    up_new = update(up_grad, up_weight, up_momentum, up_average, rate_up)
    down_new = update(down_grad, down_weight, down_momentum, down_average, rate_down)
    norm_new = update(norm_grad, norm_params, norm_momentum, norm_average, rate_norm)
    return (
        activations,
        input_grad,
        *qkv_new,
        *out_new,
        *up_new,
        *down_new,
        *norm_new,
        norm_grad[:, 3],
    )


def solution(mesh):
    rows = P("section", "batch", None)
    deep = P("section", None, "batch", None)
    features = P("section", None, "batch")
    return jax.shard_map(
        shards,
        mesh=mesh,
        in_specs=(rows, rows, P("batch", None))
        + (deep,) * 3
        + (rows,) * 9
        + (features,) * 3,
        out_specs=(rows, rows)
        + (deep,) * 4
        + (rows,) * 12
        + (features,) * 4
        + (P("section", "batch"),),
        check_vma=False,
    )
```
